128 devices in a mesh: au: 16 (over z_lo, y, core), aa: 8 (over x, z_hi).
Axes of the slice: x: 4, y: 4, z: 4 (z_hi: 2, z_lo: 2; z = z_hi * 2 + z_lo), core: 2. Of those that a mesh axis runs over, the one named last changes fastest.
Arguments:
- users: bfloat16 [32768, 256], P(('au', 'aa')), may hold values from -16 to 16
- ads: bfloat16 [32768, 256], P(('aa', 'au')), may hold values from -16 to 16
- counts: int32 [32768], P('aa'), may hold values from 1 to 999
- positives: int32 [32768], P('au'), may hold values from 0 to 32767
- weights: float32 [32768], P('au'), may hold values from 0.25 to 4
Outputs:
- grad_users: float32 [32768, 256], P(('au', 'aa'))
- grad_ads: float32 [32768, 256], P(('aa', 'au'))
- loss: float32 [], replicated
The draws below stay inside these ranges and needn't reach their ends.
All inputs are finite; a program needn't handle non-finite values.
Results may differ from the reference program's by a relative error of at most 0.015.
Values may be sent and summed in bfloat16 or wider, within the bound.
No kernel may reach another device: no remote copies, remote signals or barrier semaphores. Data moves between devices by JAX's collectives and lax.ppermute only.
A program may use at most 64 MiB of HBM per device.

```python
import math
import jax
import jax.numpy as jnp
from jax import lax

E = 256
UDEV = 2048
ADEV = 4096
USERS = 32768
ADS = 32768
N_AU = 16
N_AA = 8


def draw_users(key, part):
    key = jax.random.fold_in(key, 1)
    k_scale, k_base = jax.random.split(key, 2)
    scales = jnp.exp(jax.random.uniform(k_scale, (USERS, 1), jnp.float32, math.log(0.4), math.log(4.0)))
    value = jnp.clip(jax.random.normal(k_base, (USERS, E), jnp.float32), -4.0, 4.0) * scales
    return jnp.clip(value, -16.0, 16.0).astype(jnp.bfloat16)


def draw_ads(key, part):
    key = jax.random.fold_in(key, 2)
    k_scale, k_base = jax.random.split(key, 2)
    scales = jnp.exp(jax.random.uniform(k_scale, (ADS, 1), jnp.float32, math.log(0.4), math.log(4.0)))
    value = jnp.clip(jax.random.normal(k_base, (ADS, E), jnp.float32), -4.0, 4.0) * scales
    return jnp.clip(value, -16.0, 16.0).astype(jnp.bfloat16)


def draw_weights(key, part):
    key = jax.random.fold_in(key, 3)
    rising = 0.5 + 1.5 * jnp.arange(USERS, dtype=jnp.float32) / USERS
    factor = jnp.exp(jax.random.uniform(key, (USERS,), jnp.float32, math.log(0.5), math.log(2.0)))
    return rising * factor


def set_ends(drawn, rng, smallest, largest):
    extent = drawn.shape
    spot = [jax.random.randint(jax.random.fold_in(rng, axis), (), 0, extent[axis]) for axis in range(len(extent))]
    drawn = drawn.at[tuple(spot)].set(smallest)
    longest = extent.index(max(extent))
    spot[longest] = (spot[longest] + 1) % extent[longest]
    return drawn.at[tuple(spot)].set(largest)


def setup_inputs(seed: int = 0) -> dict:
    splits = jax.random.split(jax.random.key(seed), 6)
    return {
        "users": draw_users(jax.random.fold_in(splits[5], 71), 0),
        "ads": draw_ads(jax.random.fold_in(splits[5], 71), 0),
        "counts": set_ends(jax.random.randint(splits[2], (ADS,), 1, 1000), jax.random.fold_in(splits[2], 1), 1, 999).astype(jnp.int32),
        "positives": set_ends(jax.random.randint(splits[3], (USERS,), 0, ADS), jax.random.fold_in(splits[3], 1), 0, ADS - 1).astype(jnp.int32),
        "weights": draw_weights(jax.random.fold_in(splits[5], 71), 0),
    }


def rounded(value):
    return lax.optimization_barrier(value.astype(jnp.bfloat16)).astype(jnp.float32)


def reference(users, ads, counts, positives, weights):
    inv = E ** -0.5
    log_counts = jnp.log(counts.astype(jnp.float32))
    user_blocks = users.reshape(N_AU, UDEV, E)
    pos_blocks = positives.reshape(N_AU, UDEV)
    weight_blocks = weights.reshape(N_AU, UDEV)
    ad_blocks = ads.reshape(N_AA, ADEV, E)
    count_blocks = log_counts.reshape(N_AA, ADEV)
    starts = (jnp.arange(N_AA) * ADEV).astype(jnp.int32)

    def per_users(carry_ads, inputs):
        block_users, block_pos, block_weight = inputs

        def logits_of(block_ads, block_counts, start):
            scores = jnp.einsum("re,ce->rc", block_users, block_ads, preferred_element_type=jnp.float32)
            columns = start + jnp.arange(ADEV, dtype=jnp.int32)
            return inv * scores - block_counts[None, :], columns

        def stats(carry, pieces):
            top, total, positive = carry
            logits, columns = logits_of(*pieces)
            newtop = jnp.maximum(top, jnp.max(logits, axis=1))
            total = total * jnp.exp(top - newtop) + jnp.sum(jnp.exp(logits - newtop[:, None]), axis=1)
            hit = columns[None, :] == block_pos[:, None]
            positive = positive + jnp.sum(jnp.where(hit, logits, jnp.float32(0.0)), axis=1)
            return (newtop, total, positive), None

        start_carry = (jnp.full((UDEV,), -jnp.inf, jnp.float32), jnp.zeros((UDEV,), jnp.float32), jnp.zeros((UDEV,), jnp.float32))
        (top, total, positive), _ = lax.scan(stats, start_carry, (ad_blocks, count_blocks, starts))
        lse = top + jnp.log(total)

        def grads(grad_rows, pieces):
            block_ads = pieces[0]
            logits, columns = logits_of(*pieces)
            hit = (columns[None, :] == block_pos[:, None]).astype(jnp.float32)
            dlogits = (block_weight[:, None] * (jnp.exp(logits - lse[:, None]) - hit)).astype(jnp.bfloat16)
            user_part = inv * jnp.dot(dlogits, block_ads, preferred_element_type=jnp.float32)
            ad_part = inv * lax.dot_general(dlogits, block_users, (((0,), (0,)), ((), ())), preferred_element_type=jnp.float32)
            return grad_rows + rounded(user_part), rounded(ad_part)

        grad_rows, ad_parts = lax.scan(grads, jnp.zeros((UDEV, E), jnp.float32), (ad_blocks, count_blocks, starts))
        loss_part = jnp.sum(block_weight * (lse - positive))
        return carry_ads + ad_parts.reshape(ADS, E), (grad_rows, loss_part)

    grad_ads, (grad_rows, losses) = lax.scan(per_users, jnp.zeros((ADS, E), jnp.float32), (user_blocks, pos_blocks, weight_blocks))
    return grad_rows.reshape(USERS, E), grad_ads, jnp.sum(losses)
```

```python
import jax
import jax.numpy as jnp
from jax import lax
from jax.experimental import pallas as pl
from jax.experimental.pallas import tpu as pltpu
from jax.sharding import PartitionSpec as P

F32 = jnp.float32
BF16 = jnp.bfloat16
T = 256
LANES = 128
EXTRA = 16
NX, NZ, NY, NC = 4, 2, 4, 2
VMEM_LIMIT = 32 * 2**20


def params():
    return pltpu.CompilerParams(vmem_limit_bytes=VMEM_LIMIT)


def whole(shape):
    return pl.BlockSpec(shape, lambda *_: (0,) * len(shape))


def user_block(j, zr):
    me = lax.axis_index("aa")
    x, z = me // NZ, me % NZ
    return lax.rem(x + NX - j, NX) * NZ + (z + zr - 2 * z * zr)


def ads_block(t, cr):
    me = lax.axis_index("au")
    k, zr = t // NZ, t % NZ
    z, y, c = me // (NY * NC), (me // NC) % NY, me % NC
    return (z + zr - 2 * z * zr) * (NY * NC) + lax.rem(y + NY - k, NY) * NC + (c + cr - 2 * c * cr)


def stage_users(user_refs, staged, inv):
    for j in range(NX):
        for zr in range(NZ):
            spot = pl.multiple_of(user_block(j, zr) * T, T)
            block = user_refs[j][zr * T : (zr + 1) * T, :].astype(F32) * inv
            staged[pl.ds(spot, T), :] = block.astype(BF16)


def split(value):
    high = value.astype(BF16).astype(F32)
    mid = (value - high).astype(BF16).astype(F32)
    return high, mid, value - high - mid


def loss_rows(loss, width):
    high, mid, low = split(loss)
    lane = lax.broadcasted_iota(jnp.int32, (EXTRA, width), 1)
    return jnp.where(lane == 0, high, jnp.where(lane == 1, mid, jnp.where(lane == 2, low, 0.0))).astype(BF16)


def read_loss(rows):
    return jnp.sum(rows[:1, :LANES].astype(F32), axis=1, keepdims=True)


def logits_kernel(cr, steps, inv, *refs):
    n = NX * NZ
    chunks = 2 * steps
    user_refs = refs[:NX]
    ads_ref, logc_ref, pos_ref = refs[NX : NX + 3]
    rest = refs[NX + 3 :]
    if cr:
        m_in, t_in, hit_in = rest[:3]
        p_ref, m_ref, hit_ref, stats_ref, staged, s0, s1, total_ref = rest[3:]
    else:
        p_ref, m_ref, total_ref, hit_ref, staged, s0, s1 = rest
    step = pl.program_id(0)
    aa = lax.axis_index("aa")
    per_aa = NY * NZ * NC

    def product(chunk, dst, b):
        cols = slice(b * T, (b + 1) * T)
        ads = ads_ref[pl.ds(pl.multiple_of(chunk * T, T), T), :]
        logc = logc_ref[pl.ds(pl.multiple_of(ads_block(chunk, cr) * T, T), T), :]
        prod = lax.dot_general(
            ads, staged[cols, :], (((1,), (1,)), ((), ())), preferred_element_type=F32
        )
        dst[:, cols] = prod - jnp.concatenate([logc] * (T // LANES), axis=1)

    def tile(chunk, src, b, half):
        cols = slice(b * T, (b + 1) * T)
        logits = src[:, cols]
        rows = lax.broadcasted_iota(jnp.int32, (T, T), 0)
        base = (aa * per_aa + ads_block(chunk, cr)) * T
        hit = rows == pos_ref[:, cols] - base
        top = jnp.max(logits, axis=0, keepdims=True)
        hit_ref[:, cols] += jnp.sum(jnp.where(hit, logits, 0.0), axis=0, keepdims=True)
        e = jnp.exp(logits - top)
        total_ref[pl.ds(chunk, 1), cols] = jnp.sum(e, axis=0, keepdims=True)
        m_ref[pl.ds(chunk, 1), cols] = top
        p_ref[half * T : (half + 1) * T, cols] = e.astype(BF16)

    @pl.when(step == 0)
    def _():
        stage_users(user_refs, staged, inv)
        hit_ref[...] = hit_in[...] if cr else jnp.zeros_like(hit_ref)
        for b in range(n):
            product(0, s0, b)

    first = 2 * step
    for b in range(n):
        product(first + 1, s1, b)
        tile(first, s0, b, 0)
    after = jnp.minimum(first + 2, chunks - 1)
    for b in range(n):
        product(after, s0, b)
        tile(first + 1, s1, b, 1)

    if cr:

        @pl.when(step == steps - 1)
        def _():
            top = jnp.maximum(
                jnp.max(m_in[...], axis=0, keepdims=True), jnp.max(m_ref[...], axis=0, keepdims=True)
            )
            total = jnp.sum(t_in[...] * jnp.exp(m_in[...] - top), axis=0, keepdims=True)
            total += jnp.sum(total_ref[...] * jnp.exp(m_ref[...] - top), axis=0, keepdims=True)
            lse = top + jnp.log(total)
            width = n * T // LANES
            for r in range(width):
                cols = slice(r * LANES, (r + 1) * LANES)
                stats_ref[r : r + 1, :] = lse[:, cols]
                stats_ref[width + r : width + r + 1, :] = hit_ref[:, cols]


def run_logits(cr, users, ads, logc, positives, inv, before=()):
    width = ads.shape[1]
    count = ads.shape[0]
    chunks = count // T
    steps = chunks // 2
    total = NX * NZ * T
    rows = 2 * total // LANES
    p_spec = pl.BlockSpec((2 * T, total), lambda i: (i, 0))
    p_shape = jax.ShapeDtypeStruct((count, total), BF16)
    per_chunk = jax.ShapeDtypeStruct((chunks, total), F32)
    per_user = jax.ShapeDtypeStruct((1, total), F32)
    scratch = [pltpu.VMEM((total, width), BF16), pltpu.VMEM((T, total), F32), pltpu.VMEM((T, total), F32)]
    if cr:
        out_specs = [p_spec, whole((chunks, total)), whole((1, total)), whole((rows, LANES))]
        out_shape = [p_shape, per_chunk, per_user, jax.ShapeDtypeStruct((rows, LANES), F32)]
        scratch.append(pltpu.VMEM((chunks, total), F32))
    else:
        out_specs = [p_spec, whole((chunks, total)), whole((chunks, total)), whole((1, total))]
        out_shape = [p_shape, per_chunk, per_chunk, per_user]
    args = (*users, ads, logc, positives, *before)
    return pl.pallas_call(
        lambda *refs: logits_kernel(cr, steps, inv, *refs),
        grid=(steps,),
        in_specs=[whole(x.shape) for x in args],
        out_specs=out_specs,
        out_shape=out_shape,
        scratch_shapes=scratch,
        compiler_params=params(),
        name="logits_far" if cr else "logits_near",
    )(*args)


def grads_kernel(cr, steps, inv, *refs):
    n = NX * NZ
    user_refs = refs[:NX]
    ads_ref, p_ref, m_ref, hit_ref, pos_ref, weight_ref, stats_ref = refs[NX : NX + 7]
    rest = refs[NX + 7 :]
    if cr:
        da_ref, loss_ref, acc, staged, lse_row, coef_row = rest[:6]
        qs = rest[6:]
    else:
        acc_in, da_ref = rest[:2]
        du_refs = rest[2 : 2 + NX]
        acc, staged, lse_row, coef_row = rest[2 + NX : 6 + NX]
        qs = rest[6 + NX :]
    step = pl.program_id(0)
    aa = lax.axis_index("aa")
    per_aa = NY * NZ * NC
    width = n * T // LANES
    deep = 2 * T

    @pl.when(step == 0)
    def _():
        stage_users(user_refs, staged, inv)
        acc[...] = jnp.zeros_like(acc) if cr else acc_in[...]
        tops = stats_ref[:, :width, :]
        top = jnp.max(tops, axis=0)
        lse = top + jnp.log(jnp.sum(jnp.exp(tops - top[None]), axis=0))
        for r in range(width):
            lse_row[:, r * LANES : (r + 1) * LANES] = lse[r : r + 1, :]
        if cr:
            diff = lse - jnp.sum(stats_ref[:, width:, :], axis=0)
            loss = jnp.zeros((1, LANES), F32)
            for r in range(width):
                loss += weight_ref[:, r * LANES : (r + 1) * LANES] * diff[r : r + 1, :]
            loss_ref[...] = loss_rows(jnp.sum(loss, axis=1, keepdims=True), loss_ref.shape[1])
        coef_row[...] = weight_ref[...] * (jnp.exp(hit_ref[...] - lse_row[...]) - 1.0)

    ads = ads_ref[...]
    ads_t = ads.T
    rows = lax.broadcasted_iota(jnp.int32, (T, deep), 0)
    scales, bases = [], []
    for half in range(2):
        chunk = 2 * step + half
        scales.append(weight_ref[...] * jnp.exp(m_ref[pl.ds(chunk, 1), :] - lse_row[...]))
        bases.append((aa * per_aa + ads_block(chunk, cr)) * T)

    def build(b):
        cols = slice(b * deep, (b + 1) * deep)
        for half in range(2):
            part = slice(half * T, (half + 1) * T)
            hit = rows == pos_ref[:, cols] - bases[half]
            scaled = p_ref[part, cols].astype(F32) * scales[half][:, cols]
            qs[b][part, :] = jnp.where(hit, coef_row[:, cols], scaled).astype(BF16)

    def products(b, da):
        cols = slice(b * deep, (b + 1) * deep)
        q = qs[b][...]
        acc[:, cols] += jnp.dot(ads_t, q, preferred_element_type=F32)
        return da + jnp.dot(q, staged[cols, :], preferred_element_type=F32)

    tiles = n // 2
    da = jnp.zeros((deep, ads.shape[1]), F32)
    build(0)
    for b in range(tiles):
        if b + 1 < tiles:
            build(b + 1)
        da = products(b, da)
    da_ref[...] = da.astype(BF16)

    if not cr:

        @pl.when(step == steps - 1)
        def _():
            for j in range(NX):
                for zr in range(NZ):
                    spot = pl.multiple_of(user_block((NX - j) % NX, zr) * T, T)
                    du_refs[j][zr * T : (zr + 1) * T, :] = (acc[:, pl.ds(spot, T)] * inv).astype(BF16)


def run_grads(cr, users, ads, p, tops, hits, positives, weights, stats, inv, before=()):
    width = ads.shape[1]
    count = ads.shape[0]
    steps = count // (2 * T)
    total = NX * NZ * T
    args = (*users, ads, p, tops, hits, positives, weights, stats, *before)
    in_specs = [whole(x.shape) for x in args]
    in_specs[NX] = pl.BlockSpec((2 * T, width), lambda i: (i, 0))
    in_specs[NX + 1] = pl.BlockSpec((2 * T, total), lambda i: (i, 0))
    da_spec = pl.BlockSpec((2 * T, width), lambda i: (i, 0))
    acc_shape = jax.ShapeDtypeStruct((width, total), F32)
    da_shape = jax.ShapeDtypeStruct((count, width), BF16)
    scratch = [
        pltpu.VMEM((total, width), BF16),
        pltpu.VMEM((1, total), F32),
        pltpu.VMEM((1, total), F32),
    ] + [pltpu.VMEM((2 * T, 2 * T), BF16)] * (NX * NZ // 2)
    if cr:
        out_specs = [da_spec, whole((EXTRA, width)), whole((width, total))]
        out_shape = [da_shape, jax.ShapeDtypeStruct((EXTRA, width), BF16), acc_shape]
    else:
        out_specs = [da_spec] + [whole((NZ * width, T))] * NX
        out_shape = [da_shape] + [jax.ShapeDtypeStruct((NZ * width, T), BF16)] * NX
        scratch = [pltpu.VMEM((width, total), F32)] + scratch
    return pl.pallas_call(
        lambda *refs: grads_kernel(cr, steps, inv, *refs),
        grid=(steps,),
        in_specs=in_specs,
        out_specs=out_specs,
        out_shape=out_shape,
        scratch_shapes=scratch,
        compiler_params=params(),
        name="grads_far" if cr else "grads_near",
    )(*args)


def simple_call(kernel, name, out_shape, *args):
    return pl.pallas_call(
        kernel,
        in_specs=[whole(x.shape) for x in args],
        out_specs=[whole(x.shape) for x in out_shape],
        out_shape=out_shape,
        grid=(1,),
        compiler_params=params(),
        name=name,
    )(*args)


def add_cores(da, loss, da_far, loss_far):
    width = da.shape[1]
    rows = NZ * T

    def kernel(da_ref, loss_ref, far_ref, loss_far_ref, *outs):
        both = read_loss(loss_ref[...]) + read_loss(loss_far_ref[...])
        for k in range(NY):
            part = slice(k * rows, (k + 1) * rows)
            outs[k][:rows, :] = (da_ref[part, :].astype(F32) + far_ref[part, :].astype(F32)).astype(BF16)
            outs[k][rows:, :] = loss_rows(both, width)

    shape = jax.ShapeDtypeStruct((rows + EXTRA, width), BF16)
    return simple_call(kernel, "add_cores", [shape] * NY, da, loss, da_far, loss_far)


def add_rows(parts):
    width = parts[0].shape[1]

    def kernel(*refs):
        ins, (keep, kept_loss, send) = refs[:NY], refs[NY:]
        loss = sum(read_loss(r[NZ * T :, :]) for r in ins)
        keep[...] = sum(r[:T, :].astype(F32) for r in ins)
        kept_loss[...] = jnp.broadcast_to(loss, kept_loss.shape)
        send[:T, :] = sum(r[T : NZ * T, :].astype(F32) for r in ins).astype(BF16)
        send[T:, :] = loss_rows(loss, width)

    shapes = [
        jax.ShapeDtypeStruct((T, width), F32),
        jax.ShapeDtypeStruct((8, LANES), F32),
        jax.ShapeDtypeStruct((T + EXTRA, width), BF16),
    ]
    return simple_call(kernel, "add_rows", shapes, *parts)


def finish_ads(keep, kept_loss, received):
    def kernel(keep_ref, loss_ref, received_ref, grad, loss):
        grad[...] = keep_ref[...] + received_ref[:T, :].astype(F32)
        loss[...] = loss_ref[...] + read_loss(received_ref[T:, :])

    shapes = [jax.ShapeDtypeStruct(keep.shape, F32), jax.ShapeDtypeStruct(kept_loss.shape, F32)]
    return simple_call(kernel, "finish_ads", shapes, keep, kept_loss, received)


def add_users(parts):
    width = parts[0].shape[0] // NZ

    def kernel(*refs):
        ins, (keep, send) = refs[:NX], refs[NX:]
        keep[...] = sum(r[:width, :].astype(F32) for r in ins)
        send[...] = sum(r[width:, :].astype(F32) for r in ins).astype(BF16)

    shapes = [jax.ShapeDtypeStruct((width, T), F32), jax.ShapeDtypeStruct((width, T), BF16)]
    return simple_call(kernel, "add_users", shapes, *parts)


def finish_users(keep, received):
    def kernel(keep_ref, received_ref, grad):
        grad[...] = (keep_ref[...] + received_ref[...].astype(F32)).T

    shapes = [jax.ShapeDtypeStruct(keep.shape[::-1], F32)]
    return simple_call(kernel, "finish_users", shapes, keep, received)[0]


def move(x, axis, target):
    return lax.ppermute(x, axis, [(i, target(i)) for i in range(lax.axis_size(axis))])


def shift_x(x, j):
    return move(x, "aa", lambda i: (i + j * NZ) % (NX * NZ))


def swap_z_hi(x):
    return move(x, "aa", lambda i: i ^ 1)


def shift_y(x, k):
    return move(x, "au", lambda i: i // 8 * 8 + (i % 8 + k * NC) % 8)


def swap_core(x):
    return move(x, "au", lambda i: i ^ 1)


def swap_z_lo(x):
    return move(x, "au", lambda i: i ^ 8)


def local(users, ads, counts, positives, weights):
    inv = users.shape[1] ** (-0.5)
    ads_z, users_z = lax.optimization_barrier((swap_z_lo(ads), swap_z_hi(users)))
    ads_pair = jnp.concatenate([ads, ads_z], axis=0)
    user_pair = jnp.concatenate([users, users_z], axis=0)
    moved = [shift_y(ads_pair, k) for k in range(1, NY)] + [shift_x(user_pair, j) for j in range(1, NX)]
    moved = lax.optimization_barrier(tuple(moved))
    near = jnp.concatenate([ads_pair, *moved[: NY - 1]], axis=0)
    user_pairs = [user_pair, *moved[NY - 1 :]]
    far = swap_core(near)
    logc = jnp.broadcast_to(jnp.log(counts.astype(F32))[:, None], (counts.shape[0], LANES))
    pos_row = positives[None, :]
    weight_row = weights[None, :]

    p_near, m_near, t_near, h_near = run_logits(0, user_pairs, near, logc, pos_row, inv)
    p_far, m_far, hits, stats = run_logits(1, user_pairs, far, logc, pos_row, inv, (m_near, t_near, h_near))
    n_aa = lax.axis_size("aa")
    stats = lax.all_to_all(
        jnp.broadcast_to(stats[None], (n_aa,) + stats.shape), "aa", split_axis=0, concat_axis=0, tiled=True
    )
    da_far, loss, acc = run_grads(1, user_pairs, far, p_far, m_far, hits, pos_row, weight_row, stats, inv)
    da_back, loss_back = swap_core(da_far), swap_core(loss)
    da_near, *du = run_grads(0, user_pairs, near, p_near, m_near, hits, pos_row, weight_row, stats, inv, (acc,))

    da = add_cores(da_near, loss, da_back, loss_back)
    da = [da[0]] + [shift_y(da[k], -k) for k in range(1, NY)]
    du = [du[0]] + [shift_x(du[j], j) for j in range(1, NX)]
    keep, kept_loss, send = add_rows(da)
    keep_u, send_u = add_users(du)
    grad_ads, loss = finish_ads(keep, kept_loss, swap_z_lo(send))
    grad_users = finish_users(keep_u, swap_z_hi(send_u))
    return grad_users, grad_ads, loss[0, 0]


def solution(mesh):
    return jax.shard_map(
        local,
        mesh=mesh,
        in_specs=(P(("au", "aa"), None), P(("aa", "au"), None), P("aa"), P("au"), P("au")),
        out_specs=(P(("au", "aa"), None), P(("aa", "au"), None), P()),
        check_vma=False,
    )
```

```python
import jax
import jax.numpy as jnp
from jax import lax
from jax.experimental import pallas as pl
from jax.experimental.pallas import tpu as pltpu
from jax.sharding import PartitionSpec as P

F32 = jnp.float32
BF16 = jnp.bfloat16
T = 256
LANES = 128
EXTRA = 16
NX, NZ, NY, NC = 4, 2, 4, 2
VMEM_LIMIT = 32 * 2**20


def params():
    return pltpu.CompilerParams(vmem_limit_bytes=VMEM_LIMIT)


def whole(shape):
    return pl.BlockSpec(shape, lambda *_: (0,) * len(shape))


def user_block(j, zr):
    me = lax.axis_index("aa")
    x, z = me // NZ, me % NZ
    return lax.rem(x + NX - j, NX) * NZ + (z + zr - 2 * z * zr)


def ads_block(group, chunk):
    pair, zr = chunk // NZ, chunk % NZ
    k, cr = {"near": (pair + pair // 2, 0), "far": (pair + pair // 2, 1), "mid": (2, pair)}[group]
    me = lax.axis_index("au")
    z, y, c = me // (NY * NC), (me // NC) % NY, me % NC
    return (z + zr - 2 * z * zr) * (NY * NC) + lax.rem(y + NY - k, NY) * NC + (c + cr - 2 * c * cr)


USER_PARTS = 5


def stage_users(user_refs, staged, inv):
    places = [(0, 0, 0, 0), (0, 1, 0, 1), (1, 0, 1, 0), (1, 1, 1, 1), (3, 0, 2, 0), (3, 1, 2, 1), (2, 0, 3, 0), (2, 1, 4, 0)]
    for j, zr, part, half in places:
        spot = pl.multiple_of(user_block(j, zr) * T, T)
        block = user_refs[part][half * T : (half + 1) * T, :].astype(F32) * inv
        staged[pl.ds(spot, T), :] = block.astype(BF16)


def split(value):
    high = value.astype(BF16).astype(F32)
    mid = (value - high).astype(BF16).astype(F32)
    return high, mid, value - high - mid


def loss_rows(loss, width):
    high, mid, low = split(loss)
    lane = lax.broadcasted_iota(jnp.int32, (EXTRA, width), 1)
    return jnp.where(lane == 0, high, jnp.where(lane == 1, mid, jnp.where(lane == 2, low, 0.0))).astype(BF16)


def read_loss(rows):
    return jnp.sum(rows[:1, :LANES].astype(F32), axis=1, keepdims=True)


def logits_kernel(group, n_ads, first_call, last_call, steps, inv, *refs):
    n = NX * NZ
    chunks = 2 * steps
    user_refs, refs = refs[:USER_PARTS], refs[USER_PARTS:]
    ads_refs, refs = refs[:n_ads], refs[n_ads:]
    (count_ref, pos_ref), refs = refs[:2], refs[2:]
    hit_in = None
    olds = []
    if not first_call:
        hit_in, refs = refs[0], refs[1:]
    if last_call:
        olds, refs = refs[:4], refs[4:]
    p_ref, m_ref, total_ref, hit_ref = refs[:4]
    refs = refs[4:]
    if last_call:
        stats_ref, refs = refs[0], refs[1:]
    staged, ads_all, s0, s1 = refs
    step = pl.program_id(0)
    aa = lax.axis_index("aa")
    per_aa = NY * NZ * NC

    def product(chunk, dst, b):
        cols = slice(b * T, (b + 1) * T)
        ads = ads_all[pl.ds(pl.multiple_of(chunk * T, T), T), :]
        counts = count_ref[:, pl.ds(pl.multiple_of(ads_block(group, chunk) * T, T), T)]
        logc = jnp.broadcast_to(jnp.log(counts.astype(F32)), (LANES, T)).T
        prod = lax.dot_general(
            ads, staged[cols, :], (((1,), (1,)), ((), ())), preferred_element_type=F32
        )
        dst[:, cols] = prod - jnp.concatenate([logc] * (T // LANES), axis=1)

    def tile(chunk, src, b, half):
        cols = slice(b * T, (b + 1) * T)
        base = (aa * per_aa + ads_block(group, chunk)) * T
        ahead = pos_ref[:, cols] - base - lax.broadcasted_iota(jnp.int32, (8, T), 0)
        best = src[:8, cols]
        found = jnp.where(ahead == 0, best, 0.0)
        for r in range(8, T, 8):
            x = src[r : r + 8, cols]
            best = jnp.maximum(best, x)
            found = jnp.where(ahead == r, x, found)
        top = jnp.max(best, axis=0, keepdims=True)
        hit_ref[:, cols] += jnp.sum(found, axis=0, keepdims=True)
        total = jnp.zeros((8, T), F32)
        for r in range(0, T, 16):
            e = jnp.exp(src[r : r + 16, cols] - top)
            total += e[:8] + e[8:]
            p_ref[half * T + r : half * T + r + 16, cols] = e.astype(BF16)
        total_ref[pl.ds(chunk, 1), cols] = jnp.sum(total, axis=0, keepdims=True)
        m_ref[pl.ds(chunk, 1), cols] = top

    @pl.when(step == 0)
    def _():
        stage_users(user_refs, staged, inv)
        spot = 0
        for r in ads_refs:
            ads_all[spot : spot + r.shape[0], :] = r[...]
            spot += r.shape[0]
        hit_ref[...] = jnp.zeros_like(hit_ref) if first_call else hit_in[...]
        m_ref[...] = jnp.full(m_ref.shape, -jnp.inf, F32)
        total_ref[...] = jnp.zeros_like(total_ref)
        for b in range(n):
            product(0, s0, b)

    first = 2 * step
    for b in range(n):
        product(first + 1, s1, b)
        tile(first, s0, b, 0)
    after = jnp.minimum(first + 2, chunks - 1)
    for b in range(n):
        product(after, s0, b)
        tile(first + 1, s1, b, 1)

    if last_call:

        @pl.when(step == steps - 1)
        def _():
            ms = [olds[0][...], olds[2][...], m_ref[...]]
            ts = [olds[1][...], olds[3][...], total_ref[...]]
            top = jnp.max(jnp.maximum(jnp.maximum(ms[0], ms[1]), ms[2]), axis=0, keepdims=True)
            total = jnp.sum(sum(t * jnp.exp(m - top) for m, t in zip(ms, ts)), axis=0, keepdims=True)
            lse = top + jnp.log(total)
            width = n * T // LANES
            for r in range(width):
                cols = slice(r * LANES, (r + 1) * LANES)
                stats_ref[r : r + 1, :] = lse[:, cols]
                stats_ref[width + r : width + r + 1, :] = hit_ref[:, cols]


STATS = 8


def cost(rows, total, width, products):
    return pl.CostEstimate(
        flops=2 * products * rows * total * width, bytes_accessed=2 * rows * total, transcendentals=rows * total
    )


def run_logits(group, users, ads, counts, positives, inv, hits=(), olds=()):
    width = ads[0].shape[1]
    count = sum(x.shape[0] for x in ads)
    steps = count // (2 * T)
    total = NX * NZ * T
    rows = 2 * total // LANES
    out_specs = [
        pl.BlockSpec((2 * T, total), lambda i: (i, 0)),
        whole((STATS, total)),
        whole((STATS, total)),
        whole((1, total)),
    ]
    out_shape = [
        jax.ShapeDtypeStruct((count, total), BF16),
        jax.ShapeDtypeStruct((STATS, total), F32),
        jax.ShapeDtypeStruct((STATS, total), F32),
        jax.ShapeDtypeStruct((1, total), F32),
    ]
    if olds:
        out_specs.append(whole((rows, LANES)))
        out_shape.append(jax.ShapeDtypeStruct((rows, LANES), F32))
    args = (*users, *ads, counts, positives, *hits, *olds)
    return pl.pallas_call(
        lambda *refs: logits_kernel(group, len(ads), not hits, bool(olds), steps, inv, *refs),
        grid=(steps,),
        in_specs=[whole(x.shape) for x in args],
        out_specs=out_specs,
        out_shape=out_shape,
        scratch_shapes=[
            pltpu.VMEM((total, width), BF16),
            pltpu.VMEM((count, width), BF16),
            pltpu.VMEM((T, total), F32),
            pltpu.VMEM((T, total), F32),
        ],
        compiler_params=params(),
        cost_estimate=cost(count, total, width, 4),
        name="logits_" + group,
    )(*args)


def grads_kernel(group, n_ads, steps, inv, *refs):
    n = NX * NZ
    user_refs, refs = refs[:USER_PARTS], refs[USER_PARTS:]
    ads_refs, refs = refs[:n_ads], refs[n_ads:]
    (p_ref, m_ref, hit_ref, pos_ref, weight_ref, stats_ref), refs = refs[:6], refs[6:]
    if group == "mid":
        (near_ref, far_ref, loss_ref, acc), refs = refs[:4], refs[4:]
    elif group == "far":
        (acc_in, da_ref, acc), refs = refs[:3], refs[3:]
    else:
        (acc_in, da_ref), refs = refs[:2], refs[2:]
        du_refs, acc, refs = refs[:USER_PARTS], refs[USER_PARTS], refs[USER_PARTS + 1 :]
    staged, ads_all, lse_row, coef_row = refs[:4]
    qs = refs[4:]
    step = pl.program_id(0)
    aa = lax.axis_index("aa")
    per_aa = NY * NZ * NC
    width = n * T // LANES
    deep = 2 * T

    @pl.when(step == 0)
    def _():
        stage_users(user_refs, staged, inv)
        spot = 0
        for r in ads_refs:
            ads_all[spot : spot + r.shape[0], :] = r[...]
            spot += r.shape[0]
        acc[...] = jnp.zeros_like(acc) if group == "mid" else acc_in[...]
        tops = stats_ref[:, :width, :]
        top = jnp.max(tops, axis=0)
        lse = top + jnp.log(jnp.sum(jnp.exp(tops - top[None]), axis=0))
        for r in range(width):
            lse_row[:, r * LANES : (r + 1) * LANES] = lse[r : r + 1, :]
        if group == "mid":
            diff = lse - jnp.sum(stats_ref[:, width:, :], axis=0)
            loss = jnp.zeros((1, LANES), F32)
            for r in range(width):
                loss += weight_ref[:, r * LANES : (r + 1) * LANES] * diff[r : r + 1, :]
            rows = loss_rows(jnp.sum(loss, axis=1, keepdims=True), loss_ref.shape[1])
            loss_ref[...] = rows
            far_ref[deep:, :] = rows
        coef_row[...] = weight_ref[...] * (jnp.exp(hit_ref[...] - lse_row[...]) - 1.0)

    ads_t = ads_all[pl.ds(pl.multiple_of(step * deep, deep), deep), :].T
    rows = lax.broadcasted_iota(jnp.int32, (T, deep), 0)
    scales, bases = [], []
    for half in range(2):
        chunk = 2 * step + half
        scales.append(weight_ref[...] * jnp.exp(m_ref[pl.ds(chunk, 1), :] - lse_row[...]))
        bases.append((aa * per_aa + ads_block(group, chunk)) * T)

    def build(b):
        cols = slice(b * deep, (b + 1) * deep)
        for half in range(2):
            part = slice(half * T, (half + 1) * T)
            hit = rows == pos_ref[:, cols] - bases[half]
            scaled = p_ref[part, cols].astype(F32) * scales[half][:, cols]
            qs[b][part, :] = jnp.where(hit, coef_row[:, cols], scaled).astype(BF16)

    def products(b, da):
        cols = slice(b * deep, (b + 1) * deep)
        q = qs[b][...]
        acc[:, cols] += jnp.dot(ads_t, q, preferred_element_type=F32)
        return da + jnp.dot(q, staged[cols, :], preferred_element_type=F32)

    tiles = n // 2
    da = jnp.zeros((deep, ads_all.shape[1]), F32)
    build(0)
    for b in range(tiles):
        if b + 1 < tiles:
            build(b + 1)
        da = products(b, da)

    if group == "mid":

        @pl.when(step == 0)
        def _():
            near_ref[...] = da.astype(BF16)

        @pl.when(step == 1)
        def _():
            far_ref[:deep, :] = da.astype(BF16)

    else:
        da_ref[...] = da.astype(BF16)

    if group == "near":

        @pl.when(step == steps - 1)
        def _():
            def users_at(j, zr):
                spot = pl.multiple_of(user_block((NX - j) % NX, zr) * T, T)
                return (acc[:, pl.ds(spot, T)] * inv).astype(BF16)

            for part, j in enumerate((0, 1, 3)):
                for zr in range(NZ):
                    du_refs[part][zr * T : (zr + 1) * T, :] = users_at(j, zr)
            du_refs[3][...] = users_at(2, 0)
            du_refs[4][...] = users_at(2, 1)


def run_grads(group, users, ads, p, tops, hits, positives, weights, stats, inv, before=()):
    width = ads[0].shape[1]
    count = sum(x.shape[0] for x in ads)
    deep = 2 * T
    steps = count // deep
    total = NX * NZ * T
    args = (*users, *ads, p, tops, hits, positives, weights, stats, *before)
    in_specs = [whole(x.shape) for x in args]
    in_specs[len(users) + len(ads)] = pl.BlockSpec((deep, total), lambda i: (i, 0))
    da_spec = pl.BlockSpec((deep, width), lambda i: (i, 0))
    acc_shape = jax.ShapeDtypeStruct((width, total), F32)
    da_shape = jax.ShapeDtypeStruct((count, width), BF16)
    scratch = [
        pltpu.VMEM((total, width), BF16),
        pltpu.VMEM((count, width), BF16),
        pltpu.VMEM((1, total), F32),
        pltpu.VMEM((1, total), F32),
    ] + [pltpu.VMEM((deep, deep), BF16)] * (total // deep)
    if group == "mid":
        shapes = [(deep, width), (deep + EXTRA, width), (EXTRA, width)]
        out_shape = [jax.ShapeDtypeStruct(x, BF16) for x in shapes] + [acc_shape]
        out_specs = [whole(x.shape) for x in out_shape]
    elif group == "far":
        out_specs = [da_spec, whole((width, total))]
        out_shape = [da_shape, acc_shape]
    else:
        shapes = [(NZ * width, T)] * 3 + [(width, T)] * 2
        out_specs = [da_spec] + [whole(x) for x in shapes]
        out_shape = [da_shape] + [jax.ShapeDtypeStruct(x, BF16) for x in shapes]
        scratch = [pltpu.VMEM((width, total), F32)] + scratch
    return pl.pallas_call(
        lambda *refs: grads_kernel(group, len(ads), steps, inv, *refs),
        grid=(steps,),
        in_specs=in_specs,
        out_specs=out_specs,
        out_shape=out_shape,
        scratch_shapes=scratch,
        compiler_params=params(),
        cost_estimate=cost(count, total, width, 4),
        name="grads_" + group,
    )(*args)


def simple_call(kernel, name, out_shape, *args):
    return pl.pallas_call(
        kernel,
        in_specs=[whole(x.shape) for x in args],
        out_specs=[whole(x.shape) for x in out_shape],
        out_shape=out_shape,
        grid=(1,),
        compiler_params=params(),
        name=name,
    )(*args)


def add_mid(near, loss, back):
    width = near.shape[1]

    def kernel(near_ref, loss_ref, back_ref, first, second, both_ref):
        both = read_loss(loss_ref[...]) + read_loss(back_ref[NZ * T :, :])
        first[:T, :] = (near_ref[:T, :].astype(F32) + back_ref[:T, :].astype(F32)).astype(BF16)
        first[T:, :] = loss_rows(both, width)
        second[...] = (near_ref[T:, :].astype(F32) + back_ref[T : NZ * T, :].astype(F32)).astype(BF16)
        both_ref[...] = jnp.broadcast_to(both, both_ref.shape)

    shapes = [
        jax.ShapeDtypeStruct((T + EXTRA, width), BF16),
        jax.ShapeDtypeStruct((T, width), BF16),
        jax.ShapeDtypeStruct((8, LANES), F32),
    ]
    return simple_call(kernel, "add_mid", shapes, near, loss, back)


def add_near(near, back, both, first, second):
    width = near.shape[1]
    rows = NZ * T

    def kernel(near_ref, back_ref, both_ref, first_ref, second_ref, keep, one, three):
        both = both_ref[:1, :1]
        total = near_ref[...].astype(F32) + back_ref[...].astype(F32)
        keep[...] = total[:rows]
        one[:T, :] = (total[rows : rows + T] + first_ref[:T, :].astype(F32)).astype(BF16)
        one[T:rows, :] = total[rows + T : 2 * rows].astype(BF16)
        one[rows:, :] = loss_rows(both + read_loss(first_ref[T:, :]), width)
        three[:T, :] = total[2 * rows : 2 * rows + T].astype(BF16)
        three[T:rows, :] = (total[2 * rows + T :] + second_ref[...].astype(F32)).astype(BF16)
        three[rows:, :] = loss_rows(both, width)

    shape = jax.ShapeDtypeStruct((rows + EXTRA, width), BF16)
    return simple_call(
        kernel, "add_near", [jax.ShapeDtypeStruct((rows, width), F32), shape, shape], near, back, both, first, second
    )


def add_rows(kept, both, parts):
    width = kept.shape[1]

    def kernel(kept_ref, both_ref, r1, r3, keep, loss_ref, send):
        loss = both_ref[:1, :1] + read_loss(r1[NZ * T :, :]) + read_loss(r3[NZ * T :, :])
        keep[...] = kept_ref[:T, :] + r1[:T, :].astype(F32) + r3[:T, :].astype(F32)
        loss_ref[...] = jnp.broadcast_to(loss, loss_ref.shape)
        two = slice(T, NZ * T)
        send[:T, :] = (kept_ref[two, :] + r1[two, :].astype(F32) + r3[two, :].astype(F32)).astype(BF16)
        send[T:, :] = loss_rows(loss, width)

    shapes = [
        jax.ShapeDtypeStruct((T, width), F32),
        jax.ShapeDtypeStruct((8, LANES), F32),
        jax.ShapeDtypeStruct((T + EXTRA, width), BF16),
    ]
    return simple_call(kernel, "add_rows", shapes, kept, both, *parts)


def add_halves(one, three, first, second):
    half = one.shape[0] // NZ

    def kernel(one_ref, three_ref, first_ref, second_ref, out1, out3):
        out1[:half, :] = (one_ref[:half, :].astype(F32) + first_ref[...].astype(F32)).astype(BF16)
        out1[half:, :] = one_ref[half:, :]
        out3[:half, :] = three_ref[:half, :]
        out3[half:, :] = (three_ref[half:, :].astype(F32) + second_ref[...].astype(F32)).astype(BF16)

    shapes = [jax.ShapeDtypeStruct(one.shape, BF16)] * 2
    return simple_call(kernel, "add_halves", shapes, one, three, first, second)


def add_users(parts):
    width = parts[0].shape[0] // NZ

    def kernel(*refs):
        ins, (keep, send) = refs[:-2], refs[-2:]
        keep[...] = sum(r[:width, :].astype(F32) for r in ins)
        send[...] = sum(r[width:, :].astype(F32) for r in ins).astype(BF16)

    shapes = [jax.ShapeDtypeStruct((width, T), F32), jax.ShapeDtypeStruct((width, T), BF16)]
    return simple_call(kernel, "add_users", shapes, *parts)


def finish(keep_u, received_u, keep, kept_loss, received):
    def kernel(keep_u_ref, received_u_ref, keep_ref, loss_ref, received_ref, grad_u, grad, loss):
        grad_u[...] = (keep_u_ref[...] + received_u_ref[...].astype(F32)).T
        grad[...] = keep_ref[...] + received_ref[:T, :].astype(F32)
        loss[...] = loss_ref[:1, :1] + read_loss(received_ref[T:, :])

    shapes = [
        jax.ShapeDtypeStruct(keep_u.shape[::-1], F32),
        jax.ShapeDtypeStruct(keep.shape, F32),
        jax.ShapeDtypeStruct((1, 1), F32),
    ]
    return simple_call(kernel, "finish", shapes, keep_u, received_u, keep, kept_loss, received)


def move(x, axis, target):
    return lax.ppermute(x, axis, [(i, target(i)) for i in range(lax.axis_size(axis))])


def shift_x(x, j):
    return move(x, "aa", lambda i: (i + j * NZ) % (NX * NZ))


def swap_z_hi(x):
    return move(x, "aa", lambda i: i ^ 1)


def shift_y(x, k):
    return move(x, "au", lambda i: i // 8 * 8 + (i % 8 + k * NC) % 8)


def swap_core(x):
    return move(x, "au", lambda i: i ^ 1)


def swap_z_lo(x):
    return move(x, "au", lambda i: i ^ 8)


def local(users, ads, counts, positives, weights):
    inv = users.shape[1] ** (-0.5)
    count_row, pos_row, weight_row = counts[None, :], positives[None, :], weights[None, :]
    users_z, ads_z = lax.optimization_barrier((swap_z_hi(users), swap_z_lo(ads)))
    user_pair = jnp.concatenate([users, users_z], axis=0)
    ads_pair = jnp.concatenate([ads, ads_z], axis=0)
    user_1, user_3, ads_1, ads_3 = lax.optimization_barrier(
        (shift_x(user_pair, 1), shift_x(user_pair, -1), shift_y(ads_pair, 1), shift_y(ads_pair, -1))
    )
    user_2a, user_2b = shift_x(user_1[:T], 1), shift_x(user_3[T:], -1)
    ads_2a, ads_2b = shift_y(ads_1[:T], 1), shift_y(ads_3[T:], -1)
    near = jnp.concatenate([ads_pair, ads_1, ads_3], axis=0)
    far = swap_core(near)
    user_2a, user_2b, ads_2a, ads_2b = lax.optimization_barrier((user_2a, user_2b, ads_2a, ads_2b))
    near_2 = jnp.concatenate([ads_2a, ads_2b], axis=0)
    far_2 = swap_core(near_2)
    parts = (user_pair, user_1, user_3, user_2a, user_2b)

    p_near, m_near, t_near, hits = run_logits("near", parts, (near,), count_row, pos_row, inv)
    p_far, m_far, t_far, hits = run_logits("far", parts, (far,), count_row, pos_row, inv, (hits,))
    p_mid, m_mid, _, hits, stats = run_logits(
        "mid", parts, (near_2, far_2), count_row, pos_row, inv, (hits,), (m_near, t_near, m_far, t_far)
    )
    n_aa = lax.axis_size("aa")
    stats = lax.all_to_all(
        jnp.broadcast_to(stats[None], (n_aa,) + stats.shape), "aa", split_axis=0, concat_axis=0, tiled=True
    )
    tail = (hits, pos_row, weight_row, stats, inv)
    da_2, pay_2, loss, acc = run_grads("mid", parts, (near_2, far_2), p_mid, m_mid, *tail)
    back_2 = swap_core(pay_2)
    da_far, acc = run_grads("far", parts, (far,), p_far, m_far, *tail, (acc,))
    back = swap_core(da_far)
    first, second, both = add_mid(da_2, loss, back_2)
    first, second = shift_y(first, -1), shift_y(second, 1)
    da_near, du_0, du_1, du_3, du_2a, du_2b = run_grads("near", parts, (near,), p_near, m_near, *tail, (acc,))
    du_2a, du_2b = shift_x(du_2a, 1), shift_x(du_2b, -1)
    kept, one, three = add_near(da_near, back, both, first, second)
    one, three = shift_y(one, -1), shift_y(three, 1)
    du_1, du_3 = add_halves(du_1, du_3, du_2a, du_2b)
    du_1, du_3 = shift_x(du_1, 1), shift_x(du_3, -1)
    keep, kept_loss, send = add_rows(kept, both, (one, three))
    keep_u, send_u = add_users((du_0, du_1, du_3))
    grad_users, grad_ads, loss = finish(keep_u, swap_z_hi(send_u), keep, kept_loss, swap_z_lo(send))
    return grad_users, grad_ads, loss.reshape(())


def solution(mesh):
    return jax.shard_map(
        local,
        mesh=mesh,
        in_specs=(P(("au", "aa"), None), P(("aa", "au"), None), P("aa"), P("au"), P("au")),
        out_specs=(P(("au", "aa"), None), P(("aa", "au"), None), P()),
        check_vma=False,
    )
```

```python
import jax
import jax.numpy as jnp
from jax import lax
from jax.experimental import pallas as pl
from jax.experimental.pallas import tpu as pltpu
from jax.sharding import PartitionSpec as P

F32 = jnp.float32
BF16 = jnp.bfloat16
T = 256
LANES = 128
EXTRA = 16
NX, NZ, NY, NC = 4, 2, 4, 2
VMEM_LIMIT = 32 * 2**20


def params():
    return pltpu.CompilerParams(vmem_limit_bytes=VMEM_LIMIT)


def whole(shape):
    return pl.BlockSpec(shape, lambda *_: (0,) * len(shape))


def user_block(j, zr):
    me = lax.axis_index("aa")
    x, z = me // NZ, me % NZ
    return lax.rem(x + NX - j, NX) * NZ + (z + zr - 2 * z * zr)


def ads_block(group, chunk):
    pair, zr = chunk // NZ, chunk % NZ
    k, cr = {"near": (pair + pair // 2, 0), "far": (pair + pair // 2, 1), "mid": (2, pair)}[group]
    me = lax.axis_index("au")
    z, y, c = me // (NY * NC), (me // NC) % NY, me % NC
    return (z + zr - 2 * z * zr) * (NY * NC) + lax.rem(y + NY - k, NY) * NC + (c + cr - 2 * c * cr)


USER_PARTS = 5


def stage_users(user_refs, staged, inv):
    places = [(0, 0, 0, 0), (0, 1, 0, 1), (1, 0, 1, 0), (1, 1, 1, 1), (3, 0, 2, 0), (3, 1, 2, 1), (2, 0, 3, 0), (2, 1, 4, 0)]
    for j, zr, part, half in places:
        spot = pl.multiple_of(user_block(j, zr) * T, T)
        block = user_refs[part][half * T : (half + 1) * T, :].astype(F32) * inv
        staged[pl.ds(spot, T), :] = block.astype(BF16)


def first_row(group, chunk):
    return pl.multiple_of(ads_block(group, chunk) * T, T)


def split(value):
    high = value.astype(BF16).astype(F32)
    mid = (value - high).astype(BF16).astype(F32)
    return high, mid, value - high - mid


def loss_rows(loss, width):
    high, mid, low = split(loss)
    lane = lax.broadcasted_iota(jnp.int32, (EXTRA, width), 1) - 3 * lax.axis_index("au")
    return jnp.where(lane == 0, high, jnp.where(lane == 1, mid, jnp.where(lane == 2, low, 0.0))).astype(BF16)


def plus(*values):
    return sum(v.astype(F32) for v in values)


def logits_kernel(group, n_ads, rows, inv, *refs):
    n = NX * NZ
    steps = n // 2
    chunks = rows // T
    first_call = group == "near"
    last_call = group == "mid"
    if first_call:
        user_refs, refs = refs[:USER_PARTS], refs[USER_PARTS:]
    else:
        (users_t,), refs = refs[:1], refs[1:]
    ads_refs, refs = refs[:n_ads], refs[n_ads:]
    (logc_ref, pos_ref), refs = refs[:2], refs[2:]
    if not first_call:
        (acc_in, m_in, total_in, hit_in), refs = refs[:4], refs[4:]
    (p_ref, top_ref, ads_t, acc_ref, m_ref, total_ref, hit_ref), refs = refs[:7], refs[7:]
    if first_call:
        (staged, users_t), refs = refs[:2], refs[2:]
    if last_call:
        (stats_ref,), refs = refs[:1], refs[1:]
    ads_all, logc_all, s0, s1, late = refs
    step = pl.program_id(0)

    @pl.when(step == 0)
    def _():
        if first_call:
            stage_users(user_refs, staged, inv)
            for b in range(n):
                users_t[:, b * T : (b + 1) * T] = staged[b * T : (b + 1) * T, :].T
        spot = 0
        for r in ads_refs:
            ads_all[spot : spot + r.shape[0], :] = r[...]
            spot += r.shape[0]
        for c in range(chunks):
            part = slice(c * T, (c + 1) * T)
            ads_t[:, part] = ads_all[part, :].T
            logc = logc_ref[:, pl.ds(first_row(group, c), T)]
            logc_all[part, :] = jnp.broadcast_to(logc, (LANES, T)).T

    def product(tile, dst):
        cols = pl.ds(pl.multiple_of(tile * T, T), T)
        side = users_t[:, cols]
        pos = pos_ref[:, cols] - lax.broadcasted_iota(jnp.int32, (8, T), 0)
        best = jnp.full((8, T), -jnp.inf, F32)
        found = jnp.zeros((8, T), F32)
        for c in range(chunks):
            ahead = pos - first_row(group, c)
            prod = jnp.dot(ads_all[c * T : (c + 1) * T, :], side, preferred_element_type=F32)
            for r in range(0, T, 8):
                row = c * T + r
                logc = logc_all[row : row + 8, :]
                x = prod[r : r + 8, :] - jnp.concatenate([logc] * (T // LANES), axis=1)
                dst[row : row + 8, :] = x
                best = jnp.maximum(best, x)
                found = jnp.where(ahead == r, x, found)
        top_ref[:, cols] = jnp.max(best, axis=0, keepdims=True)
        hit = jnp.sum(found, axis=0, keepdims=True)
        hit_ref[:, cols] = hit if first_call else hit + hit_in[:, cols]

    def exps(tile, src, half, extra):
        cols = pl.ds(pl.multiple_of(tile * T, T), T)
        top = top_ref[:, cols]
        total = jnp.zeros((8, T), F32)
        for r in range(0, rows, 16):
            e = jnp.exp(src[r : r + 16, :] - top)
            total += e[:8] + e[8:]
            e = e.astype(BF16)
            p_ref[r : r + 16, half * T : (half + 1) * T] = e
            if extra is not None:
                extra[r : r + 16, :] = e
        total = jnp.sum(total, axis=0, keepdims=True)
        if first_call:
            m_ref[:, cols] = top
            total_ref[:, cols] = total
        else:
            m = jnp.maximum(m_in[:, cols], top)
            m_ref[:, cols] = m
            total_ref[:, cols] = total_in[:, cols] * jnp.exp(m_in[:, cols] - m) + total * jnp.exp(top - m)

    def gather(tile, e):
        cols = pl.ds(pl.multiple_of(tile * T, T), T)
        new = jnp.dot(ads_t[...], e, preferred_element_type=F32)
        if first_call:
            acc_ref[:, cols] = new
        else:
            m = m_ref[:, cols]
            acc_ref[:, cols] = acc_in[:, cols] * jnp.exp(m_in[:, cols] - m) + new * jnp.exp(top_ref[:, cols] - m)

    @pl.when(step == 0)
    def _():
        product(0, s0)
        late[...] = jnp.zeros_like(late)

    first = 2 * step
    gather(jnp.maximum(first - 1, 0), late[...])
    product(first + 1, s1)
    exps(first, s0, 0, None)
    gather(first, p_ref[:, :T])
    product(jnp.minimum(first + 2, n - 1), s0)
    exps(first + 1, s1, 1, late)

    @pl.when(step == steps - 1)
    def _():
        gather(n - 1, late[...])
        if last_call:
            lse = m_ref[...] + jnp.log(total_ref[...])
            width = n * T // LANES
            for r in range(width):
                cols = slice(r * LANES, (r + 1) * LANES)
                stats_ref[r : r + 1, :] = lse[:, cols]
                stats_ref[width + r : width + r + 1, :] = hit_ref[:, cols]


def cost(rows, total, width):
    return pl.CostEstimate(flops=rows * total * width // 8, bytes_accessed=rows * total // 8, transcendentals=0)


def run_logits(group, users, ads, logc, positives, inv, before=()):
    width = ads[0].shape[1]
    count = sum(x.shape[0] for x in ads)
    total = NX * NZ * T
    stats_rows = 2 * total // LANES
    row = jax.ShapeDtypeStruct((1, total), F32)
    out_shape = [
        jax.ShapeDtypeStruct((count, total), BF16),
        row,
        jax.ShapeDtypeStruct((width, count), BF16),
        jax.ShapeDtypeStruct((width, total), F32),
        row,
        row,
        row,
    ]
    if group == "near":
        out_shape.append(jax.ShapeDtypeStruct((total, width), BF16))
        out_shape.append(jax.ShapeDtypeStruct((width, total), BF16))
    if group == "mid":
        out_shape.append(jax.ShapeDtypeStruct((stats_rows, LANES), F32))
    out_specs = [whole(x.shape) for x in out_shape]
    out_specs[0] = pl.BlockSpec((count, 2 * T), lambda i: (0, i))
    args = (*users, *ads, logc, positives, *before)
    return pl.pallas_call(
        lambda *refs: logits_kernel(group, len(ads), count, inv, *refs),
        grid=(total // (2 * T),),
        in_specs=[whole(x.shape) for x in args],
        out_specs=out_specs,
        out_shape=out_shape,
        scratch_shapes=[
            pltpu.VMEM((count, width), BF16),
            pltpu.VMEM((count, LANES), F32),
            pltpu.VMEM((count, T), F32),
            pltpu.VMEM((count, T), F32),
            pltpu.VMEM((count, T), BF16),
        ],
        compiler_params=params(),
        cost_estimate=cost(count, total, width),
        name="logits_" + group,
    )(*args)


GROUPS = ("near", "far", "mid")


def rows_kernel(sizes, start, *refs):
    ads_refs, (pos_ref, out_ref, h0, h1) = refs[: len(sizes)], refs[len(sizes) :]
    step = pl.program_id(0)
    steps = out_ref.shape[1] // (2 * T)

    def build(tile, dst):
        cols = pl.ds(pl.multiple_of(start + tile * T, T), T)
        pos = pos_ref[:, cols] - lax.broadcasted_iota(jnp.int32, (16, T), 0)
        spot = 0
        for group, size in zip(GROUPS, sizes):
            for c in range(size // T):
                ahead = pos - first_row(group, c)
                for r in range(0, T, 16):
                    dst[spot + r : spot + r + 16, :] = jnp.where(ahead == r, 1.0, 0.0).astype(BF16)
                spot += T

    def product(tile, src):
        cols = pl.ds(pl.multiple_of(tile * T, T), T)
        out = jnp.zeros((out_ref.shape[0], T), F32)
        spot = 0
        for ads, size in zip(ads_refs, sizes):
            out += jnp.dot(ads[...], src[spot : spot + size, :], preferred_element_type=F32)
            spot += size
        out_ref[:, cols] = out.astype(BF16)

    @pl.when(step == 0)
    def _():
        h1[...] = jnp.zeros_like(h1)

    first = 2 * step
    product(jnp.maximum(first - 1, 0), h1)
    build(first, h0)
    product(first, h0)
    build(first + 1, h1)

    @pl.when(step == steps - 1)
    def _():
        product(first + 1, h1)


def run_rows(ads_t, positives, start, total):
    width = ads_t[0].shape[0]
    sizes = [x.shape[1] for x in ads_t]
    args = (*ads_t, positives)
    return pl.pallas_call(
        lambda *refs: rows_kernel(sizes, start, *refs),
        grid=(total // (2 * T),),
        in_specs=[whole(x.shape) for x in args],
        out_specs=whole((width, total)),
        out_shape=jax.ShapeDtypeStruct((width, total), BF16),
        scratch_shapes=[pltpu.VMEM((sum(sizes), T), BF16)] * 2,
        compiler_params=params(),
        cost_estimate=cost(sum(sizes), total, width),
        name="positive_rows",
    )(*args)


def users_kernel(inv, acc_ref, m_ref, rows_a, rows_b, hit_ref, weight_ref, *rest):
    stats_in, rest = rest[:NX], rest[NX:]
    du_refs, (lse_ref, coef_ref, loss_ref, stats_ref, rows_ref) = rest[:USER_PARTS], rest[USER_PARTS:]
    n = NX * NZ
    width = n * T // LANES
    for j in range(NX):
        stats_ref[pl.ds(lax.rem(lax.axis_index("aa") // NZ + NX - j, NX), 1)] = stats_in[j][...][None]
    rows_ref[:, : n * T // 2] = rows_a[...]
    rows_ref[:, n * T // 2 :] = rows_b[...]
    tops = stats_ref[:, :width, :]
    top = jnp.max(tops, axis=0)
    lse = top + jnp.log(jnp.sum(jnp.exp(tops - top[None]), axis=0))
    diff = lse - jnp.sum(stats_ref[:, width:, :], axis=0)
    loss = jnp.zeros((1, LANES), F32)
    for r in range(width):
        cols = slice(r * LANES, (r + 1) * LANES)
        lse_ref[:, cols] = lse[r : r + 1, :]
        loss += weight_ref[:, cols] * diff[r : r + 1, :]
    loss_ref[...] = loss_rows(jnp.sum(loss, axis=1, keepdims=True), loss_ref.shape[1])
    coef_ref[...] = weight_ref[...] * (jnp.exp(hit_ref[...] - lse_ref[...]) - 1.0)

    def users_at(j, zr):
        cols = pl.ds(pl.multiple_of(user_block((NX - j) % NX, zr) * T, T), T)
        weight = weight_ref[:, cols] * inv
        scale = weight * jnp.exp(m_ref[:, cols] - lse_ref[:, cols])
        return (acc_ref[:, cols] * scale - rows_ref[:, cols].astype(F32) * weight).astype(BF16)

    for part, j in enumerate((0, 1, 3)):
        for zr in range(NZ):
            du_refs[part][zr * T : (zr + 1) * T, :] = users_at(j, zr)
    du_refs[3][...] = users_at(2, 0)
    du_refs[4][...] = users_at(2, 1)


def run_users(acc, m, rows_a, rows_b, hits, weights, stats, inv):
    width, total = acc.shape
    row = jax.ShapeDtypeStruct((1, total), F32)
    shapes = [(NZ * width, T)] * 3 + [(width, T)] * 2
    out_shape = [jax.ShapeDtypeStruct(x, BF16) for x in shapes]
    out_shape += [row, row, jax.ShapeDtypeStruct((EXTRA, width), BF16)]
    args = (acc, m, rows_a, rows_b, hits, weights, *stats)
    return pl.pallas_call(
        lambda *refs: users_kernel(inv, *refs),
        grid=(1,),
        in_specs=[whole(x.shape) for x in args],
        out_specs=[whole(x.shape) for x in out_shape],
        out_shape=out_shape,
        scratch_shapes=[pltpu.VMEM((NX, *stats[0].shape), F32), pltpu.VMEM((width, total), BF16)],
        compiler_params=params(),
        name="grad_users",
    )(*args)


def grads_kernel(group, steps, users_ref, p_ref, top_ref, lse_ref, coef_ref, weight_ref, pos_ref, loss_in, *refs):
    if group == "mid":
        near_ref, far_ref, da_ref, q0, q1, scale_row = refs
    else:
        da_ref, q0, q1, scale_row = refs
    step = pl.program_id(0)
    deep = 2 * T
    total = p_ref.shape[1]

    @pl.when(step == 0)
    def _():
        scale_row[...] = weight_ref[...] * jnp.exp(top_ref[...] - lse_ref[...])
        q1[...] = jnp.zeros_like(q1)

    def build(half, dst):
        base = first_row(group, 2 * step + half)
        for b in range(total // T):
            cols = slice(b * T, (b + 1) * T)
            ahead = pos_ref[:, cols] - base - lax.broadcasted_iota(jnp.int32, (16, T), 0)
            scale, coef = scale_row[:, cols], coef_ref[:, cols]
            for r in range(0, T, 16):
                scaled = p_ref[half * T + r : half * T + r + 16, cols].astype(F32) * scale
                dst[r : r + 16, cols] = jnp.where(ahead == r, coef, scaled).astype(BF16)

    def product(chunk, src):
        da = jnp.dot(src[...], users_ref[...], preferred_element_type=F32)
        da_ref[pl.ds(pl.multiple_of(chunk * T, T), T), :] = da.astype(BF16)

    first = 2 * step
    product(jnp.maximum(first - 1, 0), q1)
    build(0, q0)
    product(first, q0)
    build(1, q1)

    @pl.when(step == steps - 1)
    def _():
        product(first + 1, q1)
        if group == "mid":
            near_ref[...] = da_ref[:deep, :]
            far_ref[:deep, :] = da_ref[deep:, :]
            far_ref[deep:, :] = loss_in[...]


def run_grads(group, users, p, top, lse, coefs, weights, positives, loss):
    count, total = p.shape
    width = users.shape[1]
    deep = 2 * T
    steps = count // deep
    args = (users, p, top, lse, coefs, weights, positives, loss)
    in_specs = [whole(x.shape) for x in args]
    in_specs[1] = pl.BlockSpec((deep, total), lambda i: (i, 0))
    da = pltpu.VMEM((count, width), BF16)
    scratch = [pltpu.VMEM((T, total), BF16)] * 2 + [pltpu.VMEM((1, total), F32)]
    shapes = [(deep, width), (deep + EXTRA, width)] if group == "mid" else [(count, width)]
    return pl.pallas_call(
        lambda *refs: grads_kernel(group, steps, *refs),
        grid=(steps,),
        in_specs=in_specs,
        out_specs=[whole(x) for x in shapes],
        out_shape=[jax.ShapeDtypeStruct(x, BF16) for x in shapes],
        scratch_shapes=([da] if group == "mid" else []) + scratch,
        compiler_params=params(),
        cost_estimate=cost(count, total, width),
        name="grads_" + group,
    )(*args)


def simple_call(kernel, name, out_shape, *args):
    return pl.pallas_call(
        kernel,
        in_specs=[whole(x.shape) for x in args],
        out_specs=[whole(x.shape) for x in out_shape],
        out_shape=out_shape,
        grid=(1,),
        compiler_params=params(),
        name=name,
    )(*args)


def add_mid(near, loss, back):
    width = near.shape[1]

    def kernel(near_ref, loss_ref, back_ref, first, second, both_ref):
        both = plus(loss_ref[...], back_ref[NZ * T :, :]).astype(BF16)
        first[:T, :] = plus(near_ref[:T, :], back_ref[:T, :]).astype(BF16)
        first[T:, :] = both
        second[...] = plus(near_ref[T:, :], back_ref[T : NZ * T, :]).astype(BF16)
        both_ref[...] = both

    shapes = [(T + EXTRA, width), (T, width), (EXTRA, width)]
    shapes = [jax.ShapeDtypeStruct(x, BF16) for x in shapes]
    return simple_call(kernel, "add_mid", shapes, near, loss, back)


def add_near(near, back, both, first, second):
    width = near.shape[1]
    rows = NZ * T

    def kernel(near_ref, back_ref, both_ref, first_ref, second_ref, keep, one, three):
        total = plus(near_ref[...], back_ref[...])
        keep[:rows, :] = total[:rows]
        keep[rows:, :] = both_ref[...].astype(F32)
        one[:T, :] = plus(total[rows : rows + T], first_ref[:T, :]).astype(BF16)
        one[T:rows, :] = total[rows + T : 2 * rows].astype(BF16)
        one[rows:, :] = plus(both_ref[...], first_ref[T:, :]).astype(BF16)
        three[:T, :] = total[2 * rows : 2 * rows + T].astype(BF16)
        three[T:rows, :] = plus(total[2 * rows + T :], second_ref[...]).astype(BF16)
        three[rows:, :] = both_ref[...]

    shape = jax.ShapeDtypeStruct((rows + EXTRA, width), BF16)
    shapes = [jax.ShapeDtypeStruct((rows + EXTRA, width), F32), shape, shape]
    return simple_call(kernel, "add_near", shapes, near, back, both, first, second)


def add_rows(*parts):
    width = parts[0].shape[1]

    def kernel(*refs):
        ins, (keep, send) = refs[:3], refs[3:]
        loss = plus(*(r[NZ * T :, :] for r in ins))
        keep[:T, :] = plus(*(r[:T, :] for r in ins))
        keep[T:, :] = loss
        send[:T, :] = plus(*(r[T : NZ * T, :] for r in ins)).astype(BF16)
        send[T:, :] = loss.astype(BF16)

    shapes = [jax.ShapeDtypeStruct((T + EXTRA, width), F32), jax.ShapeDtypeStruct((T + EXTRA, width), BF16)]
    return simple_call(kernel, "add_rows", shapes, *parts)


def add_halves(one, three, first, second):
    half = one.shape[0] // NZ

    def kernel(one_ref, three_ref, first_ref, second_ref, out1, out3):
        out1[:half, :] = (one_ref[:half, :].astype(F32) + first_ref[...].astype(F32)).astype(BF16)
        out1[half:, :] = one_ref[half:, :]
        out3[:half, :] = three_ref[:half, :]
        out3[half:, :] = (three_ref[half:, :].astype(F32) + second_ref[...].astype(F32)).astype(BF16)

    shapes = [jax.ShapeDtypeStruct(one.shape, BF16)] * 2
    return simple_call(kernel, "add_halves", shapes, one, three, first, second)


def add_users(parts):
    width = parts[0].shape[0] // NZ

    def kernel(*refs):
        ins, (keep, send) = refs[:-2], refs[-2:]
        keep[...] = sum(r[:width, :].astype(F32) for r in ins)
        send[...] = sum(r[width:, :].astype(F32) for r in ins).astype(BF16)

    shapes = [jax.ShapeDtypeStruct((width, T), F32), jax.ShapeDtypeStruct((width, T), BF16)]
    return simple_call(kernel, "add_users", shapes, *parts)


def finish(keep_u, received_u, keep, received):
    def kernel(keep_u_ref, received_u_ref, keep_ref, received_ref, grad_u, grad, loss):
        grad_u[...] = plus(keep_u_ref[...], received_u_ref[...]).T
        grad[...] = plus(keep_ref[:T, :], received_ref[:T, :])
        loss[...] = jnp.sum(plus(keep_ref[T : T + 1, :], received_ref[T : T + 1, :]), axis=1, keepdims=True)

    shapes = [(T, keep_u.shape[0]), (T, keep.shape[1]), (1, 1)]
    shapes = [jax.ShapeDtypeStruct(x, F32) for x in shapes]
    return simple_call(kernel, "finish", shapes, keep_u, received_u, keep, received)


def join_stats(own, other):
    half = own.shape[0] // 2

    def kernel(own_ref, other_ref, out_ref):
        a, b = own_ref[:half, :], other_ref[:half, :]
        top = jnp.maximum(a, b)
        out_ref[:half, :] = top + jnp.log(jnp.exp(a - top) + jnp.exp(b - top))
        out_ref[half:, :] = own_ref[half:, :] + other_ref[half:, :]

    return simple_call(kernel, "join_stats", [jax.ShapeDtypeStruct(own.shape, F32)], own, other)[0]


def move(x, axis, target):
    return lax.ppermute(x, axis, [(i, target(i)) for i in range(lax.axis_size(axis))])


def shift_x(x, j):
    return move(x, "aa", lambda i: (i + j * NZ) % (NX * NZ))


def swap_z_hi(x):
    return move(x, "aa", lambda i: i ^ 1)


def shift_y(x, k):
    return move(x, "au", lambda i: i // 8 * 8 + (i % 8 + k * NC) % 8)


def swap_core(x):
    return move(x, "au", lambda i: i ^ 1)


def swap_z_lo(x):
    return move(x, "au", lambda i: i ^ 8)


def local(users, ads, counts, positives, weights):
    inv = users.shape[1] ** (-0.5)
    pos_row = (positives - lax.axis_index("aa") * counts.shape[0])[None, :]
    logc = jnp.log(counts.astype(F32))[None, :]
    weight_row = weights[None, :]
    users_z, ads_z, pos_row, logc = lax.optimization_barrier((swap_z_hi(users), swap_z_lo(ads), pos_row, logc))
    user_pair = jnp.concatenate([users, users_z], axis=0)
    ads_pair = jnp.concatenate([ads, ads_z], axis=0)
    user_1, user_3, ads_1, ads_3 = lax.optimization_barrier(
        (shift_x(user_pair, 1), shift_x(user_pair, -1), shift_y(ads_pair, 1), shift_y(ads_pair, -1))
    )
    user_2a, user_2b = shift_x(user_1[:T], 1), shift_x(user_3[T:], -1)
    ads_2a, ads_2b = shift_y(ads_1[:T], 1), shift_y(ads_3[T:], -1)
    near = jnp.concatenate([ads_pair, ads_1, ads_3], axis=0)
    far = swap_core(near)
    parts = (user_pair, user_1, user_3, user_2a, user_2b)

    p_near, top_near, at_near, acc, m, total, hits, staged, users_t = run_logits(
        "near", parts, (near,), logc, pos_row, inv
    )
    ads_2a, ads_2b, hits = lax.optimization_barrier((ads_2a, ads_2b, hits))
    near_2 = jnp.concatenate([ads_2a, ads_2b], axis=0)
    far_2 = swap_core(near_2)
    p_far, top_far, at_far, acc, m, total, hits = run_logits(
        "far", (users_t,), (far,), logc, pos_row, inv, (acc, m, total, hits)
    )
    p_mid, top_mid, at_mid, acc, m, total, hits, stats = run_logits(
        "mid", (users_t,), (near_2, far_2), logc, pos_row, inv, (acc, m, total, hits)
    )
    half = stats.shape[0] * LANES // 4
    ads_t = (at_near, at_far, at_mid)
    stats_z, rows_a = lax.optimization_barrier((swap_z_hi(stats), run_rows(ads_t, pos_row, 0, half)))
    stats = join_stats(stats, stats_z)
    moved = tuple(shift_x(stats, j) for j in range(1, NX))
    moved, rows_b = lax.optimization_barrier((moved, run_rows(ads_t, pos_row, half, half)))
    du_0, du_1, du_3, du_2a, du_2b, lse, coefs, loss = run_users(
        acc, m, rows_a, rows_b, hits, weight_row, (stats, *moved), inv
    )
    tail = (lse, coefs, weight_row, pos_row, loss)
    du_2a, du_2b = shift_x(du_2a, 1), shift_x(du_2b, -1)
    da_2, pay_2 = run_grads("mid", staged, p_mid, top_mid, *tail)
    back_2 = swap_core(pay_2)
    da_2, staged = lax.optimization_barrier((da_2, staged))
    (da_far,) = run_grads("far", staged, p_far, top_far, *tail)
    da_far, back_2, du_2a, du_2b = lax.optimization_barrier((da_far, back_2, du_2a, du_2b))
    du_1, du_3 = add_halves(du_1, du_3, du_2a, du_2b)
    back = swap_core(da_far)
    first, second, both = add_mid(da_2, loss, back_2)
    first, second, du_1, du_3, staged = lax.optimization_barrier((first, second, du_1, du_3, staged))
    first, second = shift_y(first, -1), shift_y(second, 1)
    du_1, du_3 = shift_x(du_1, 1), shift_x(du_3, -1)
    (da_near,) = run_grads("near", staged, p_near, top_near, *tail)
    da_near, first, second = lax.optimization_barrier((da_near, first, second))
    kept, one, three = add_near(da_near, back, both, first, second)
    one, three = shift_y(one, -1), shift_y(three, 1)
    keep_u, send_u = add_users((du_0, du_1, du_3))
    one, three, received_u = lax.optimization_barrier((one, three, swap_z_hi(send_u)))
    keep, send = add_rows(kept, one, three)
    grad_users, grad_ads, loss = finish(keep_u, received_u, keep, swap_z_lo(send))
    return grad_users, grad_ads, loss.reshape(())


def solution(mesh):
    return jax.shard_map(
        local,
        mesh=mesh,
        in_specs=(P(("au", "aa"), None), P(("aa", "au"), None), P("aa"), P("au"), P("au")),
        out_specs=(P(("au", "aa"), None), P(("aa", "au"), None), P()),
        check_vma=False,
    )
```

```python
import jax
import jax.numpy as jnp
from jax import lax
from jax.experimental import pallas as pl
from jax.experimental.pallas import tpu as pltpu
from jax.sharding import PartitionSpec as P

F32 = jnp.float32
BF16 = jnp.bfloat16
T = 256
LANES = 128
EXTRA = 16
NX, NZ, NY, NC = 4, 2, 4, 2
VMEM_LIMIT = 24 * 2**20


def params():
    return pltpu.CompilerParams(vmem_limit_bytes=VMEM_LIMIT)


def call(kernel, name, out_shape, scratch, args, estimate=None):
    vmem = pl.BlockSpec(memory_space=pltpu.VMEM)
    return pl.pallas_call(
        kernel,
        in_specs=[vmem] * len(args),
        out_specs=[vmem] * len(out_shape),
        out_shape=out_shape,
        scratch_shapes=scratch,
        compiler_params=params(),
        cost_estimate=estimate,
        name=name,
    )(*args)


def user_block(j, zr):
    me = lax.axis_index("aa")
    x, z = me // NZ, me % NZ
    return lax.rem(x + NX - j, NX) * NZ + (z + zr - 2 * z * zr)


def ads_block(group, chunk):
    pair, zr = chunk // NZ, chunk % NZ
    k, cr = {"near": (pair + pair // 2, 0), "far": (pair + pair // 2, 1), "mid": (2, pair)}[group]
    me = lax.axis_index("au")
    z, y, c = me // (NY * NC), (me // NC) % NY, me % NC
    return (z + zr - 2 * z * zr) * (NY * NC) + lax.rem(y + NY - k, NY) * NC + (c + cr - 2 * c * cr)


USER_PARTS = 5


def stage_users(user_refs, staged, inv):
    places = [(0, 0, 0, 0), (0, 1, 0, 1), (1, 0, 1, 0), (1, 1, 1, 1), (3, 0, 2, 0), (3, 1, 2, 1), (2, 0, 3, 0), (2, 1, 4, 0)]
    for j, zr, part, half in places:
        spot = pl.multiple_of(user_block(j, zr) * T, T)
        block = user_refs[part][half * T : (half + 1) * T, :].astype(F32) * inv
        staged[pl.ds(spot, T), :] = block.astype(BF16)


def first_row(group, chunk):
    return pl.multiple_of(ads_block(group, chunk) * T, T)


def split(value):
    high = value.astype(BF16).astype(F32)
    mid = (value - high).astype(BF16).astype(F32)
    return high, mid, value - high - mid


def loss_rows(loss, width):
    high, mid, low = split(loss)
    lane = lax.broadcasted_iota(jnp.int32, (EXTRA, width), 1) - 3 * lax.axis_index("au")
    return jnp.where(lane == 0, high, jnp.where(lane == 1, mid, jnp.where(lane == 2, low, 0.0))).astype(BF16)


def plus(*values):
    return sum(v.astype(F32) for v in values)


def logits_kernel(group, n_ads, rows, inv, *refs):
    n = NX * NZ
    steps = n // 2
    chunks = rows // T
    first_call = group == "near"
    last_call = group == "mid"
    if first_call:
        user_refs, refs = refs[:USER_PARTS], refs[USER_PARTS:]
    else:
        (users_t,), refs = refs[:1], refs[1:]
    ads_refs, refs = refs[:n_ads], refs[n_ads:]
    (logc_ref, pos_ref), refs = refs[:2], refs[2:]
    if not first_call:
        (acc_in, m_in, total_in, hit_in), refs = refs[:4], refs[4:]
    (p_ref, top_ref, ads_t, acc_ref, m_ref, total_ref, hit_ref), refs = refs[:7], refs[7:]
    if first_call:
        (staged, users_t), refs = refs[:2], refs[2:]
    if last_call:
        (stats_ref,), refs = refs[:1], refs[1:]
    ads_all, logc_all, s0, s1, *late = refs

    if first_call:
        stage_users(user_refs, staged, inv)
        for b in range(n):
            users_t[:, b * T : (b + 1) * T] = staged[b * T : (b + 1) * T, :].T
    spot = 0
    for r in ads_refs:
        ads_all[spot : spot + r.shape[0], :] = r[...]
        spot += r.shape[0]
    for c in range(chunks):
        part = slice(c * T, (c + 1) * T)
        ads_t[:, part] = ads_all[part, :].T
        logc = logc_ref[:, pl.ds(first_row(group, c), T)]
        logc_all[part, :] = jnp.broadcast_to(logc, (LANES, T)).T

    def columns(tile):
        return pl.ds(pl.multiple_of(tile * T, T), T)

    class Product:
        def __init__(self, tile, dst):
            self.cols, self.dst = columns(tile), dst
            self.side = users_t[:, self.cols]
            self.pos = pos_ref[:, self.cols] - lax.broadcasted_iota(jnp.int32, (8, T), 0)
            self.best = jnp.full((8, T), -jnp.inf, F32)
            self.found = jnp.zeros((8, T), F32)

        def chunk(self, c):
            ahead = self.pos - first_row(group, c)
            prod = jnp.dot(ads_all[c * T : (c + 1) * T, :], self.side, preferred_element_type=F32)
            for r in range(0, T, 8):
                row = c * T + r
                logc = logc_all[row : row + 8, :]
                x = prod[r : r + 8, :] - jnp.concatenate([logc] * (T // LANES), axis=1)
                self.dst[row : row + 8, :] = x
                self.best = jnp.maximum(self.best, x)
                self.found = jnp.where(ahead == r, x, self.found)

        def end(self):
            top_ref[:, self.cols] = jnp.max(self.best, axis=0, keepdims=True)
            hit = jnp.sum(self.found, axis=0, keepdims=True)
            hit_ref[:, self.cols] = hit if first_call else hit + hit_in[:, self.cols]

    class Exps:
        def __init__(self, tile, src, extra):
            self.cols, self.src, self.extra = columns(tile), src, extra
            self.top = top_ref[:, self.cols]
            self.total = jnp.zeros((8, T), F32)

        def chunk(self, c):
            for r in range(c * T, (c + 1) * T, 16):
                e = jnp.exp(self.src[r : r + 16, :] - self.top)
                self.total += e[:8] + e[8:]
                e = e.astype(BF16)
                p_ref[r : r + 16, self.cols] = e
                self.extra[r : r + 16, :] = e

        def end(self):
            cols, top = self.cols, self.top
            total = jnp.sum(self.total, axis=0, keepdims=True)
            if first_call:
                m_ref[:, cols] = top
                total_ref[:, cols] = total
            else:
                m = jnp.maximum(m_in[:, cols], top)
                m_ref[:, cols] = m
                total_ref[:, cols] = total_in[:, cols] * jnp.exp(m_in[:, cols] - m) + total * jnp.exp(top - m)

    def gather(tile, e):
        cols = columns(tile)
        new = jnp.dot(ads_t[...], e[...], preferred_element_type=F32)
        if first_call:
            acc_ref[:, cols] = new
        else:
            m = m_ref[:, cols]
            acc_ref[:, cols] = acc_in[:, cols] * jnp.exp(m_in[:, cols] - m) + new * jnp.exp(top_ref[:, cols] - m)

    def turn(tile, src, dst, e_now, e_before):
        gather(jnp.maximum(tile - 1, 0), e_before)
        product, exps = Product(jnp.minimum(tile + 1, n - 1), dst), Exps(tile, src, e_now)
        for c in range(chunks):
            product.chunk(c)
            exps.chunk(c)
        product.end()
        exps.end()

    opening = Product(0, s0)
    for c in range(chunks):
        opening.chunk(c)
    opening.end()
    e0, e1 = late
    e1[...] = jnp.zeros_like(e1)
    m_ref[...] = jnp.zeros_like(m_ref) if first_call else m_in[...]

    @pl.loop(0, steps)
    def _(step):
        turn(2 * step, s0, s1, e0, e1)
        turn(2 * step + 1, s1, s0, e1, e0)

    gather(n - 1, e1)
    if last_call:
        lse = m_ref[...] + jnp.log(total_ref[...])
        width = n * T // LANES
        for r in range(width):
            cols = slice(r * LANES, (r + 1) * LANES)
            stats_ref[r : r + 1, :] = lse[:, cols]
            stats_ref[width + r : width + r + 1, :] = hit_ref[:, cols]


def cost(rows, total, width):
    return pl.CostEstimate(flops=rows * total * width // 8, bytes_accessed=rows * total // 8, transcendentals=0)


def run_logits(group, users, ads, logc, positives, inv, before=()):
    width = ads[0].shape[1]
    count = sum(x.shape[0] for x in ads)
    total = NX * NZ * T
    stats_rows = 2 * total // LANES
    row = jax.ShapeDtypeStruct((1, total), F32)
    out_shape = [
        jax.ShapeDtypeStruct((count, total), BF16),
        row,
        jax.ShapeDtypeStruct((width, count), BF16),
        jax.ShapeDtypeStruct((width, total), F32),
        row,
        row,
        row,
    ]
    if group == "near":
        out_shape.append(jax.ShapeDtypeStruct((total, width), BF16))
        out_shape.append(jax.ShapeDtypeStruct((width, total), BF16))
    if group == "mid":
        out_shape.append(jax.ShapeDtypeStruct((stats_rows, LANES), F32))
    scratch = [
        pltpu.VMEM((count, width), BF16),
        pltpu.VMEM((count, LANES), F32),
        pltpu.VMEM((count, T), F32),
        pltpu.VMEM((count, T), F32),
        pltpu.VMEM((count, T), BF16),
        pltpu.VMEM((count, T), BF16),
    ]
    return call(
        lambda *refs: logits_kernel(group, len(ads), count, inv, *refs),
        "logits_" + group,
        out_shape,
        scratch,
        (*users, *ads, logc, positives, *before),
        cost(count, total, width),
    )


GROUPS = ("near", "far", "mid")


def rows_kernel(sizes, start, *refs):
    ads_refs, (pos_ref, out_ref, h0, h1) = refs[: len(sizes)], refs[len(sizes) :]
    tiles = out_ref.shape[1] // T

    def build(tile, dst):
        cols = pl.ds(pl.multiple_of(start + tile * T, T), T)
        pos = pos_ref[:, cols] - lax.broadcasted_iota(jnp.int32, (16, T), 0)
        spot = 0
        for group, size in zip(GROUPS, sizes):
            for c in range(size // T):
                ahead = pos - first_row(group, c)
                for r in range(0, T, 16):
                    dst[spot + r : spot + r + 16, :] = jnp.where(ahead == r, 1.0, 0.0).astype(BF16)
                spot += T

    def product(tile, src):
        cols = pl.ds(pl.multiple_of(tile * T, T), T)
        out = jnp.zeros((out_ref.shape[0], T), F32)
        spot = 0
        for ads, size in zip(ads_refs, sizes):
            out += jnp.dot(ads[...], src[spot : spot + size, :], preferred_element_type=F32)
            spot += size
        out_ref[:, cols] = out.astype(BF16)

    build(0, h0)

    @pl.loop(0, tiles // 2)
    def _(step):
        product(2 * step, h0)
        build(2 * step + 1, h1)
        product(2 * step + 1, h1)
        build(jnp.minimum(2 * step + 2, tiles - 1), h0)


def run_rows(ads_t, positives, start, total):
    width = ads_t[0].shape[0]
    sizes = [x.shape[1] for x in ads_t]
    return call(
        lambda *refs: rows_kernel(sizes, start, *refs),
        "positive_rows",
        [jax.ShapeDtypeStruct((width, total), BF16)],
        [pltpu.VMEM((sum(sizes), T), BF16)] * 2,
        (*ads_t, positives),
        cost(sum(sizes), total, width),
    )[0]


def users_kernel(inv, acc_ref, m_ref, rows_a, rows_b, hit_ref, weight_ref, *rest):
    stats_in, rest = rest[:NX], rest[NX:]
    du_refs, (lse_ref, coef_ref, loss_ref, stats_ref, rows_ref) = rest[:USER_PARTS], rest[USER_PARTS:]
    n = NX * NZ
    width = n * T // LANES
    for j in range(NX):
        stats_ref[pl.ds(lax.rem(lax.axis_index("aa") // NZ + NX - j, NX), 1)] = stats_in[j][...][None]
    rows_ref[:, : n * T // 2] = rows_a[...]
    rows_ref[:, n * T // 2 :] = rows_b[...]
    tops = stats_ref[:, :width, :]
    top = jnp.max(tops, axis=0)
    lse = top + jnp.log(jnp.sum(jnp.exp(tops - top[None]), axis=0))
    diff = lse - jnp.sum(stats_ref[:, width:, :], axis=0)
    loss = jnp.zeros((1, LANES), F32)
    for r in range(width):
        cols = slice(r * LANES, (r + 1) * LANES)
        lse_ref[:, cols] = lse[r : r + 1, :]
        loss += weight_ref[:, cols] * diff[r : r + 1, :]
    loss_ref[...] = loss_rows(jnp.sum(loss, axis=1, keepdims=True), loss_ref.shape[1])
    coef_ref[...] = weight_ref[...] * (jnp.exp(hit_ref[...] - lse_ref[...]) - 1.0)

    def users_at(j, zr):
        cols = pl.ds(pl.multiple_of(user_block((NX - j) % NX, zr) * T, T), T)
        weight = weight_ref[:, cols] * inv
        scale = weight * jnp.exp(m_ref[:, cols] - lse_ref[:, cols])
        return (acc_ref[:, cols] * scale - rows_ref[:, cols].astype(F32) * weight).astype(BF16)

    for part, j in enumerate((0, 1, 3)):
        for zr in range(NZ):
            du_refs[part][zr * T : (zr + 1) * T, :] = users_at(j, zr)
    du_refs[3][...] = users_at(2, 0)
    du_refs[4][...] = users_at(2, 1)


def run_users(acc, m, rows_a, rows_b, hits, weights, stats, inv):
    width, total = acc.shape
    row = jax.ShapeDtypeStruct((1, total), F32)
    shapes = [(NZ * width, T)] * 3 + [(width, T)] * 2
    out_shape = [jax.ShapeDtypeStruct(x, BF16) for x in shapes]
    out_shape += [row, row, jax.ShapeDtypeStruct((EXTRA, width), BF16)]
    return call(
        lambda *refs: users_kernel(inv, *refs),
        "grad_users",
        out_shape,
        [pltpu.VMEM((NX, *stats[0].shape), F32), pltpu.VMEM((width, total), BF16)],
        (acc, m, rows_a, rows_b, hits, weights, *stats),
    )


def grads_kernel(group, users_ref, p_ref, top_ref, lse_ref, coef_ref, weight_ref, pos_ref, loss_in, *refs):
    outs, qs = refs[:-2], refs[-2:]
    deep = 2 * T
    count, total = p_ref.shape

    def build(unit, dst):
        for b in range(total // T):
            cols = slice(b * T, (b + 1) * T)
            scale = weight_ref[:, cols] * jnp.exp(top_ref[:, cols] - lse_ref[:, cols])
            coef = coef_ref[:, cols]
            pos = pos_ref[:, cols] - lax.broadcasted_iota(jnp.int32, (16, T), 0)
            for half in range(2):
                ahead = pos - first_row(group, 2 * unit + half)
                for r in range(0, T, 16):
                    row = half * T + r
                    scaled = p_ref[unit * deep + row : unit * deep + row + 16, cols].astype(F32) * scale
                    dst[row : row + 16, cols] = jnp.where(ahead == r, coef, scaled).astype(BF16)

    def product(unit, src):
        da = jnp.dot(src[...], users_ref[...], preferred_element_type=F32).astype(BF16)
        if group == "mid":
            outs[unit][:deep, :] = da
        else:
            outs[0][unit * deep : (unit + 1) * deep, :] = da

    units = count // deep
    build(0, qs[0])
    for unit in range(units):
        product(unit, qs[unit % 2])
        if unit + 1 < units:
            build(unit + 1, qs[(unit + 1) % 2])
    if group == "mid":
        outs[1][deep:, :] = loss_in[...]


def run_grads(group, users, p, top, lse, coefs, weights, positives, loss):
    count, total = p.shape
    width = users.shape[1]
    deep = 2 * T
    shapes = [(deep, width), (deep + EXTRA, width)] if group == "mid" else [(count, width)]
    return call(
        lambda *refs: grads_kernel(group, *refs),
        "grads_" + group,
        [jax.ShapeDtypeStruct(x, BF16) for x in shapes],
        [pltpu.VMEM((deep, total), BF16)] * 2,
        (users, p, top, lse, coefs, weights, positives, loss),
        cost(count, total, width),
    )


def simple_call(kernel, name, out_shape, *args):
    return call(kernel, name, out_shape, [], args)


def add_mid(near, loss, back):
    width = near.shape[1]

    def kernel(near_ref, loss_ref, back_ref, first, second, both_ref):
        both = plus(loss_ref[...], back_ref[NZ * T :, :]).astype(BF16)
        first[:T, :] = plus(near_ref[:T, :], back_ref[:T, :]).astype(BF16)
        first[T:, :] = both
        second[...] = plus(near_ref[T:, :], back_ref[T : NZ * T, :]).astype(BF16)
        both_ref[...] = both

    shapes = [(T + EXTRA, width), (T, width), (EXTRA, width)]
    shapes = [jax.ShapeDtypeStruct(x, BF16) for x in shapes]
    return simple_call(kernel, "add_mid", shapes, near, loss, back)


def add_near(near, back, both, first, second):
    width = near.shape[1]
    rows = NZ * T

    def kernel(near_ref, back_ref, both_ref, first_ref, second_ref, keep, one, three):
        total = plus(near_ref[...], back_ref[...])
        keep[:rows, :] = total[:rows]
        keep[rows:, :] = both_ref[...].astype(F32)
        one[:T, :] = plus(total[rows : rows + T], first_ref[:T, :]).astype(BF16)
        one[T:rows, :] = total[rows + T : 2 * rows].astype(BF16)
        one[rows:, :] = plus(both_ref[...], first_ref[T:, :]).astype(BF16)
        three[:T, :] = total[2 * rows : 2 * rows + T].astype(BF16)
        three[T:rows, :] = plus(total[2 * rows + T :], second_ref[...]).astype(BF16)
        three[rows:, :] = both_ref[...]

    shape = jax.ShapeDtypeStruct((rows + EXTRA, width), BF16)
    shapes = [jax.ShapeDtypeStruct((rows + EXTRA, width), F32), shape, shape]
    return simple_call(kernel, "add_near", shapes, near, back, both, first, second)


def add_rows(*parts):
    width = parts[0].shape[1]

    def kernel(*refs):
        ins, (keep, send) = refs[:3], refs[3:]
        loss = plus(*(r[NZ * T :, :] for r in ins))
        keep[:T, :] = plus(*(r[:T, :] for r in ins))
        keep[T:, :] = loss
        send[:T, :] = plus(*(r[T : NZ * T, :] for r in ins)).astype(BF16)
        send[T:, :] = loss.astype(BF16)

    shapes = [jax.ShapeDtypeStruct((T + EXTRA, width), F32), jax.ShapeDtypeStruct((T + EXTRA, width), BF16)]
    return simple_call(kernel, "add_rows", shapes, *parts)


def add_halves(one, three, first, second):
    half = one.shape[0] // NZ

    def kernel(one_ref, three_ref, first_ref, second_ref, out1, out3):
        out1[:half, :] = (one_ref[:half, :].astype(F32) + first_ref[...].astype(F32)).astype(BF16)
        out1[half:, :] = one_ref[half:, :]
        out3[:half, :] = three_ref[:half, :]
        out3[half:, :] = (three_ref[half:, :].astype(F32) + second_ref[...].astype(F32)).astype(BF16)

    shapes = [jax.ShapeDtypeStruct(one.shape, BF16)] * 2
    return simple_call(kernel, "add_halves", shapes, one, three, first, second)


def add_users(parts):
    width = parts[0].shape[0] // NZ

    def kernel(*refs):
        ins, (keep, send) = refs[:-2], refs[-2:]
        keep[...] = sum(r[:width, :].astype(F32) for r in ins)
        send[...] = sum(r[width:, :].astype(F32) for r in ins).astype(BF16)

    shapes = [jax.ShapeDtypeStruct((width, T), F32), jax.ShapeDtypeStruct((width, T), BF16)]
    return simple_call(kernel, "add_users", shapes, *parts)


def finish(keep_u, received_u, keep, received):
    def kernel(keep_u_ref, received_u_ref, keep_ref, received_ref, grad_u, grad, loss):
        grad_u[...] = plus(keep_u_ref[...], received_u_ref[...]).T
        grad[...] = plus(keep_ref[:T, :], received_ref[:T, :])
        loss[...] = jnp.sum(plus(keep_ref[T : T + 1, :], received_ref[T : T + 1, :]), axis=1, keepdims=True)

    shapes = [(T, keep_u.shape[0]), (T, keep.shape[1]), (1, 1)]
    shapes = [jax.ShapeDtypeStruct(x, F32) for x in shapes]
    return simple_call(kernel, "finish", shapes, keep_u, received_u, keep, received)


def join_stats(own, other):
    half = own.shape[0] // 2

    def kernel(own_ref, other_ref, out_ref):
        a, b = own_ref[:half, :], other_ref[:half, :]
        top = jnp.maximum(a, b)
        out_ref[:half, :] = top + jnp.log(jnp.exp(a - top) + jnp.exp(b - top))
        out_ref[half:, :] = own_ref[half:, :] + other_ref[half:, :]

    return simple_call(kernel, "join_stats", [jax.ShapeDtypeStruct(own.shape, F32)], own, other)[0]


def move(x, axis, target):
    return lax.ppermute(x, axis, [(i, target(i)) for i in range(lax.axis_size(axis))])


def shift_x(x, j):
    return move(x, "aa", lambda i: (i + j * NZ) % (NX * NZ))


def swap_z_hi(x):
    return move(x, "aa", lambda i: i ^ 1)


def shift_y(x, k):
    return move(x, "au", lambda i: i // 8 * 8 + (i % 8 + k * NC) % 8)


def swap_core(x):
    return move(x, "au", lambda i: i ^ 1)


def swap_z_lo(x):
    return move(x, "au", lambda i: i ^ 8)


def local(users, ads, counts, positives, weights):
    inv = users.shape[1] ** (-0.5)
    pos_row = (positives - lax.axis_index("aa") * counts.shape[0])[None, :]
    logc = jnp.log(counts.astype(F32))[None, :]
    weight_row = weights[None, :]
    users_z, ads_z, pos_row, logc = lax.optimization_barrier((swap_z_hi(users), swap_z_lo(ads), pos_row, logc))
    user_pair = jnp.concatenate([users, users_z], axis=0)
    ads_pair = jnp.concatenate([ads, ads_z], axis=0)
    user_1, user_3, ads_1, ads_3 = lax.optimization_barrier(
        (shift_x(user_pair, 1), shift_x(user_pair, -1), shift_y(ads_pair, 1), shift_y(ads_pair, -1))
    )
    user_2a, user_2b = shift_x(user_1[:T], 1), shift_x(user_3[T:], -1)
    ads_2a, ads_2b = shift_y(ads_1[:T], 1), shift_y(ads_3[T:], -1)
    near = jnp.concatenate([ads_pair, ads_1, ads_3], axis=0)
    far = swap_core(near)
    parts = (user_pair, user_1, user_3, user_2a, user_2b)

    p_near, top_near, at_near, acc, m, total, hits, staged, users_t = run_logits(
        "near", parts, (near,), logc, pos_row, inv
    )
    ads_2a, ads_2b, hits = lax.optimization_barrier((ads_2a, ads_2b, hits))
    near_2 = jnp.concatenate([ads_2a, ads_2b], axis=0)
    far_2 = swap_core(near_2)
    p_far, top_far, at_far, acc, m, total, hits = run_logits(
        "far", (users_t,), (far,), logc, pos_row, inv, (acc, m, total, hits)
    )
    p_mid, top_mid, at_mid, acc, m, total, hits, stats = run_logits(
        "mid", (users_t,), (near_2, far_2), logc, pos_row, inv, (acc, m, total, hits)
    )
    half = stats.shape[0] * LANES // 4
    ads_t = (at_near, at_far, at_mid)
    stats_z, rows_a = lax.optimization_barrier((swap_z_hi(stats), run_rows(ads_t, pos_row, 0, half)))
    stats = join_stats(stats, stats_z)
    moved = tuple(shift_x(stats, j) for j in range(1, NX))
    moved, rows_b = lax.optimization_barrier((moved, run_rows(ads_t, pos_row, half, half)))
    du_0, du_1, du_3, du_2a, du_2b, lse, coefs, loss = run_users(
        acc, m, rows_a, rows_b, hits, weight_row, (stats, *moved), inv
    )
    tail = (lse, coefs, weight_row, pos_row, loss)
    du_2a, du_2b = shift_x(du_2a, 1), shift_x(du_2b, -1)
    da_2, pay_2 = run_grads("mid", staged, p_mid, top_mid, *tail)
    back_2 = swap_core(pay_2)
    da_2, staged = lax.optimization_barrier((da_2, staged))
    (da_far,) = run_grads("far", staged, p_far, top_far, *tail)
    da_far, back_2, du_2a, du_2b = lax.optimization_barrier((da_far, back_2, du_2a, du_2b))
    du_1, du_3 = add_halves(du_1, du_3, du_2a, du_2b)
    back = swap_core(da_far)
    first, second, both = add_mid(da_2, loss, back_2)
    first, second, du_1, du_3, staged = lax.optimization_barrier((first, second, du_1, du_3, staged))
    first, second = shift_y(first, -1), shift_y(second, 1)
    du_1, du_3 = shift_x(du_1, 1), shift_x(du_3, -1)
    (da_near,) = run_grads("near", staged, p_near, top_near, *tail)
    da_near, first, second, du_1, du_3 = lax.optimization_barrier((da_near, first, second, du_1, du_3))
    kept, one, three = add_near(da_near, back, both, first, second)
    one, three = shift_y(one, -1), shift_y(three, 1)
    keep_u, send_u = add_users((du_0, du_1, du_3))
    one, three, received_u = lax.optimization_barrier((one, three, swap_z_hi(send_u)))
    keep, send = add_rows(kept, one, three)
    grad_users, grad_ads, loss = finish(keep_u, received_u, keep, swap_z_lo(send))
    return grad_users, grad_ads, loss.reshape(())


def solution(mesh):
    return jax.shard_map(
        local,
        mesh=mesh,
        in_specs=(P(("au", "aa"), None), P(("aa", "au"), None), P("aa"), P("au"), P("au")),
        out_specs=(P(("au", "aa"), None), P(("aa", "au"), None), P()),
        check_vma=False,
    )
```

```python
import jax
import jax.numpy as jnp
from jax import lax
from jax.experimental import pallas as pl
from jax.experimental.pallas import tpu as pltpu
from jax.sharding import PartitionSpec as P

F32 = jnp.float32
BF16 = jnp.bfloat16
T = 256
LANES = 128
EXTRA = 16
NX, NZ, NY, NC = 4, 2, 4, 2
VMEM_LIMIT = 24 * 2**20


def params():
    return pltpu.CompilerParams(vmem_limit_bytes=VMEM_LIMIT)


def call(kernel, name, out_shape, scratch, args, estimate=None):
    vmem = pl.BlockSpec(memory_space=pltpu.VMEM)
    return pl.pallas_call(
        kernel,
        in_specs=[vmem] * len(args),
        out_specs=[vmem] * len(out_shape),
        out_shape=out_shape,
        scratch_shapes=scratch,
        compiler_params=params(),
        cost_estimate=estimate,
        name=name,
    )(*args)


def user_block(j, zr):
    me = lax.axis_index("aa")
    x, z = me // NZ, me % NZ
    return lax.rem(x + NX - j, NX) * NZ + (z + zr - 2 * z * zr)


def ads_block(group, chunk):
    pair, zr = chunk // NZ, chunk % NZ
    k, cr = {"near": (pair + pair // 2, 0), "far": (pair + pair // 2, 1), "mid": (2, pair)}[group]
    me = lax.axis_index("au")
    z, y, c = me // (NY * NC), (me // NC) % NY, me % NC
    return (z + zr - 2 * z * zr) * (NY * NC) + lax.rem(y + NY - k, NY) * NC + (c + cr - 2 * c * cr)


USER_PARTS = 5


def stage_users(user_refs, staged, inv):
    places = [(0, 0, 0, 0), (0, 1, 0, 1), (1, 0, 1, 0), (1, 1, 1, 1), (3, 0, 2, 0), (3, 1, 2, 1), (2, 0, 3, 0), (2, 1, 4, 0)]
    for j, zr, part, half in places:
        spot = pl.multiple_of(user_block(j, zr) * T, T)
        block = user_refs[part][half * T : (half + 1) * T, :].astype(F32) * inv
        staged[pl.ds(spot, T), :] = block.astype(BF16)


def first_row(group, chunk):
    return pl.multiple_of(ads_block(group, chunk) * T, T)


def split(value):
    high = value.astype(BF16).astype(F32)
    mid = (value - high).astype(BF16).astype(F32)
    return high, mid, value - high - mid


def loss_rows(loss, width):
    high, mid, low = split(loss)
    lane = lax.broadcasted_iota(jnp.int32, (EXTRA, width), 1) - 3 * lax.axis_index("au")
    return jnp.where(lane == 0, high, jnp.where(lane == 1, mid, jnp.where(lane == 2, low, 0.0))).astype(BF16)


def plus(*values):
    return sum(v.astype(F32) for v in values)


def logits_kernel(group, n_ads, rows, inv, *refs):
    n = NX * NZ
    steps = n // 2
    chunks = rows // T
    deep = 2 * T
    first_call = group == "near"
    last_call = group == "mid"
    if first_call:
        user_refs, refs = refs[:USER_PARTS], refs[USER_PARTS:]
    else:
        (users_t,), refs = refs[:1], refs[1:]
    ads_refs, refs = refs[:n_ads], refs[n_ads:]
    (logc_ref, pos_ref), refs = refs[:2], refs[2:]
    if first_call:
        (ads_t,), refs = refs[:1], refs[1:]
    if not first_call:
        (acc_in, m_in, total_in, hit_in), refs = refs[:4], refs[4:]
    (p_ref, top_ref, acc_ref, m_ref, total_ref, hit_ref), refs = refs[:6], refs[6:]
    if first_call:
        (staged, users_t), refs = refs[:2], refs[2:]
    else:
        (ads_t,), refs = refs[:1], refs[1:]
    if last_call:
        (stats_ref,), refs = refs[:1], refs[1:]
    ads_all, logc_all, s0, s1, *late = refs

    if first_call:
        stage_users(user_refs, staged, inv)
        for b in range(n):
            users_t[:, b * T : (b + 1) * T] = staged[b * T : (b + 1) * T, :].T
    spot = 0
    for r in ads_refs:
        ads_all[spot : spot + r.shape[0], :] = r[...]
        spot += r.shape[0]
    for c in range(chunks):
        part = slice(c * T, (c + 1) * T)
        if not first_call:
            ads_t[:, part] = ads_all[part, :].T
        logc = logc_ref[:, pl.ds(first_row(group, c), T)]
        logc_all[part, :] = jnp.broadcast_to(logc, (LANES, T)).T

    def columns(tile):
        return pl.ds(pl.multiple_of(tile * T, T), T)

    class Product:
        def __init__(self, tile, dst):
            self.cols, self.dst = columns(tile), dst
            self.side = users_t[:, self.cols]
            self.pos = pos_ref[:, self.cols] - lax.broadcasted_iota(jnp.int32, (16, T), 0)
            self.best = jnp.full((16, T), -jnp.inf, F32)
            self.found = jnp.zeros((16, T), F32)

        def chunk(self, c):
            prod = jnp.dot(ads_all[c * deep : (c + 1) * deep, :], self.side, preferred_element_type=F32)
            for half in range(2):
                ahead = self.pos - first_row(group, 2 * c + half)
                for r in range(0, T, 16):
                    row = half * T + r
                    at = slice(c * deep + row, c * deep + row + 16)
                    x = prod[row : row + 16, :] - jnp.concatenate([logc_all[at, :]] * (T // LANES), axis=1)
                    self.dst[at, :] = x
                    self.best = jnp.maximum(self.best, x)
                    self.found = jnp.where(ahead == r, x, self.found)

        def end(self):
            top_ref[:, self.cols] = jnp.max(self.best, axis=0, keepdims=True)
            hit = jnp.sum(self.found, axis=0, keepdims=True)
            hit_ref[:, self.cols] = hit if first_call else hit + hit_in[:, self.cols]

    class Exps:
        def __init__(self, tile, src, extra):
            self.cols, self.src, self.extra = columns(tile), src, extra
            self.top = top_ref[:, self.cols]
            self.total = jnp.zeros((16, T), F32)

        def chunk(self, c):
            for r in range(c * deep, (c + 1) * deep, 16):
                e = jnp.exp(self.src[r : r + 16, :] - self.top)
                self.total += e
                e = e.astype(BF16)
                p_ref[r : r + 16, self.cols] = e
                self.extra[r : r + 16, :] = e

        def end(self):
            cols, top = self.cols, self.top
            total = jnp.sum(self.total, axis=0, keepdims=True)
            if first_call:
                m_ref[:, cols] = top
                total_ref[:, cols] = total
            else:
                m = jnp.maximum(m_in[:, cols], top)
                m_ref[:, cols] = m
                total_ref[:, cols] = total_in[:, cols] * jnp.exp(m_in[:, cols] - m) + total * jnp.exp(top - m)

    def gather(tile, e):
        cols = columns(tile)
        new = jnp.dot(ads_t[...], e[...], preferred_element_type=F32)
        if first_call:
            acc_ref[:, cols] = new
        else:
            m = m_ref[:, cols]
            acc_ref[:, cols] = acc_in[:, cols] * jnp.exp(m_in[:, cols] - m) + new * jnp.exp(top_ref[:, cols] - m)

    def turn(tile, src, dst, e_now, e_before):
        gather(jnp.maximum(tile - 1, 0), e_before)
        product, exps = Product(jnp.minimum(tile + 1, n - 1), dst), Exps(tile, src, e_now)
        for c in range(chunks // 2):
            product.chunk(c)
            exps.chunk(c)
        product.end()
        exps.end()

    opening = Product(0, s0)
    for c in range(chunks // 2):
        opening.chunk(c)
    opening.end()
    e0, e1 = late
    e1[...] = jnp.zeros_like(e1)
    m_ref[...] = jnp.zeros_like(m_ref) if first_call else m_in[...]

    @pl.loop(0, steps)
    def _(step):
        turn(2 * step, s0, s1, e0, e1)
        turn(2 * step + 1, s1, s0, e1, e0)

    gather(n - 1, e1)
    if last_call:
        lse = m_ref[...] + jnp.log(total_ref[...])
        width = n * T // LANES
        for r in range(width):
            cols = slice(r * LANES, (r + 1) * LANES)
            stats_ref[r : r + 1, :] = lse[:, cols]
            stats_ref[width + r : width + r + 1, :] = hit_ref[:, cols]


def cost(rows, total, width):
    return pl.CostEstimate(flops=rows * total * width // 8, bytes_accessed=rows * total // 8, transcendentals=0)


def run_logits(group, users, ads, logc, positives, inv, before=()):
    width = ads[0].shape[1]
    count = sum(x.shape[0] for x in ads)
    total = NX * NZ * T
    stats_rows = 2 * total // LANES
    row = jax.ShapeDtypeStruct((1, total), F32)
    out_shape = [
        jax.ShapeDtypeStruct((count, total), BF16),
        row,
        jax.ShapeDtypeStruct((width, total), F32),
        row,
        row,
        row,
    ]
    if group == "near":
        out_shape.append(jax.ShapeDtypeStruct((total, width), BF16))
        out_shape.append(jax.ShapeDtypeStruct((width, total), BF16))
    else:
        out_shape.append(jax.ShapeDtypeStruct((width, count), BF16))
    if group == "mid":
        out_shape.append(jax.ShapeDtypeStruct((stats_rows, LANES), F32))
    scratch = [
        pltpu.VMEM((count, width), BF16),
        pltpu.VMEM((count, LANES), F32),
        pltpu.VMEM((count, T), F32),
        pltpu.VMEM((count, T), F32),
        pltpu.VMEM((count, T), BF16),
        pltpu.VMEM((count, T), BF16),
    ]
    return call(
        lambda *refs: logits_kernel(group, len(ads), count, inv, *refs),
        "logits_" + group,
        out_shape,
        scratch,
        (*users, *ads, logc, positives, *before),
        cost(count, total, width),
    )


def rows_kernel(groups, sizes, start, *refs):
    ads_refs, refs = refs[: len(sizes)], refs[len(sizes) :]
    (pos_ref, out_ref), refs = refs[:2], refs[2:]
    if groups == ("near",):
        (ads_t, h0, h1) = refs
        for spot in range(0, sizes[0], T):
            ads_t[:, spot : spot + T] = ads_refs[0][spot : spot + T, :].T
        ads_refs = (ads_t,)
    else:
        h0, h1 = refs
    tiles = out_ref.shape[1] // T

    def build(tile, dst):
        cols = pl.ds(pl.multiple_of(start + tile * T, T), T)
        pos = pos_ref[:, cols] - lax.broadcasted_iota(jnp.int32, (16, T), 0)
        spot = 0
        for group, size in zip(groups, sizes):
            for c in range(size // T):
                ahead = pos - first_row(group, c)
                for r in range(0, T, 16):
                    dst[spot + r : spot + r + 16, :] = jnp.where(ahead == r, 1.0, 0.0).astype(BF16)
                spot += T

    def product(tile, src):
        cols = pl.ds(pl.multiple_of(tile * T, T), T)
        out = jnp.zeros((out_ref.shape[0], T), F32)
        spot = 0
        for ads, size in zip(ads_refs, sizes):
            out += jnp.dot(ads[...], src[spot : spot + size, :], preferred_element_type=F32)
            spot += size
        out_ref[:, cols] = out.astype(BF16)

    build(0, h0)

    @pl.loop(0, tiles // 2)
    def _(step):
        product(2 * step, h0)
        build(2 * step + 1, h1)
        product(2 * step + 1, h1)
        build(jnp.minimum(2 * step + 2, tiles - 1), h0)


def run_rows(groups, ads, positives, start, total):
    near = groups == ("near",)
    sizes = [x.shape[0] if near else x.shape[1] for x in ads]
    width = ads[0].shape[1] if near else ads[0].shape[0]
    out_shape = [jax.ShapeDtypeStruct((width, total), BF16)]
    if near:
        out_shape.append(jax.ShapeDtypeStruct((width, sizes[0]), BF16))
    return call(
        lambda *refs: rows_kernel(groups, sizes, start, *refs),
        "positive_rows_" + groups[0],
        out_shape,
        [pltpu.VMEM((sum(sizes), T), BF16)] * 2,
        (*ads, positives),
        cost(sum(sizes), total, width),
    )


def users_kernel(inv, acc_ref, m_ref, rows_n, rows_a, rows_b, hit_ref, weight_ref, *rest):
    stats_in, rest = rest[:NX], rest[NX:]
    du_refs, (lse_ref, coef_ref, loss_ref, stats_ref, rows_ref) = rest[:USER_PARTS], rest[USER_PARTS:]
    n = NX * NZ
    width = n * T // LANES
    for j in range(NX):
        stats_ref[pl.ds(lax.rem(lax.axis_index("aa") // NZ + NX - j, NX), 1)] = stats_in[j][...][None]
    rows_ref[:, : n * T // 2] = plus(rows_n[:, : n * T // 2], rows_a[...]).astype(BF16)
    rows_ref[:, n * T // 2 :] = plus(rows_n[:, n * T // 2 :], rows_b[...]).astype(BF16)
    tops = stats_ref[:, :width, :]
    top = jnp.max(tops, axis=0)
    lse = top + jnp.log(jnp.sum(jnp.exp(tops - top[None]), axis=0))
    diff = lse - jnp.sum(stats_ref[:, width:, :], axis=0)
    loss = jnp.zeros((1, LANES), F32)
    for r in range(width):
        cols = slice(r * LANES, (r + 1) * LANES)
        lse_ref[:, cols] = lse[r : r + 1, :]
        loss += weight_ref[:, cols] * diff[r : r + 1, :]
    loss_ref[...] = loss_rows(jnp.sum(loss, axis=1, keepdims=True), loss_ref.shape[1])
    coef_ref[...] = weight_ref[...] * (jnp.exp(hit_ref[...] - lse_ref[...]) - 1.0)

    def users_at(j, zr):
        cols = pl.ds(pl.multiple_of(user_block((NX - j) % NX, zr) * T, T), T)
        weight = weight_ref[:, cols] * inv
        scale = weight * jnp.exp(m_ref[:, cols] - lse_ref[:, cols])
        return (acc_ref[:, cols] * scale - rows_ref[:, cols].astype(F32) * weight).astype(BF16)

    for part, j in enumerate((0, 1, 3)):
        for zr in range(NZ):
            du_refs[part][zr * T : (zr + 1) * T, :] = users_at(j, zr)
    du_refs[3][...] = users_at(2, 0)
    du_refs[4][...] = users_at(2, 1)


def run_users(acc, m, rows_n, rows_a, rows_b, hits, weights, stats, inv):
    width, total = acc.shape
    row = jax.ShapeDtypeStruct((1, total), F32)
    shapes = [(NZ * width, T)] * 3 + [(width, T)] * 2
    out_shape = [jax.ShapeDtypeStruct(x, BF16) for x in shapes]
    out_shape += [row, row, jax.ShapeDtypeStruct((EXTRA, width), BF16)]
    return call(
        lambda *refs: users_kernel(inv, *refs),
        "grad_users",
        out_shape,
        [pltpu.VMEM((NX, *stats[0].shape), F32), pltpu.VMEM((width, total), BF16)],
        (acc, m, rows_n, rows_a, rows_b, hits, weights, *stats),
    )


def grads_kernel(
    group, users_ref, p_ref, p_mid, top_ref, top_mid, lse_ref, coef_ref, weight_ref, pos_ref, loss_in, da_ref, *qs
):
    deep = 2 * T
    total = p_ref.shape[1]
    mine = [(group, p_ref, top_ref, unit) for unit in range(p_ref.shape[0] // deep)]
    units = mine + [("mid", p_mid, top_mid, 0 if group == "near" else 1)]

    def build(unit, dst):
        name, p, tops, at = units[unit]
        for b in range(total // T):
            cols = slice(b * T, (b + 1) * T)
            scale = weight_ref[:, cols] * jnp.exp(tops[:, cols] - lse_ref[:, cols])
            coef = coef_ref[:, cols]
            pos = pos_ref[:, cols] - lax.broadcasted_iota(jnp.int32, (16, T), 0)
            for half in range(2):
                ahead = pos - first_row(name, 2 * at + half)
                for r in range(0, T, 16):
                    row = half * T + r
                    scaled = p[at * deep + row : at * deep + row + 16, cols].astype(F32) * scale
                    dst[row : row + 16, cols] = jnp.where(ahead == r, coef, scaled).astype(BF16)

    build(0, qs[0])
    for unit in range(len(units)):
        da = jnp.dot(qs[unit % 2][...], users_ref[...], preferred_element_type=F32)
        da_ref[unit * deep : (unit + 1) * deep, :] = da.astype(BF16)
        if unit + 1 < len(units):
            build(unit + 1, qs[(unit + 1) % 2])
    da_ref[len(units) * deep :, :] = loss_in[...]


def run_grads(group, users, p, p_mid, top, top_mid, lse, coefs, weights, positives, loss):
    total, width = users.shape
    count = p.shape[0] + p_mid.shape[0] // 2
    return call(
        lambda *refs: grads_kernel(group, *refs),
        "grads_" + group,
        [jax.ShapeDtypeStruct((count + EXTRA, width), BF16)],
        [pltpu.VMEM((2 * T, total), BF16)] * 2,
        (users, p, p_mid, top, top_mid, lse, coefs, weights, positives, loss),
        cost(count, total, width),
    )[0]


def simple_call(kernel, name, out_shape, *args):
    return call(kernel, name, out_shape, [], args)


def add_cores(near, back):
    width = near.shape[1]
    rows = NZ * T

    def kernel(near_ref, back_ref, first, second, keep, one, three):
        both = plus(near_ref[NY * rows :, :], back_ref[NY * rows :, :])

        def place(i):
            return plus(near_ref[i * rows : (i + 1) * rows, :], back_ref[i * rows : (i + 1) * rows, :])

        two = place(3)
        first[:T, :] = two[:T].astype(BF16)
        first[T:, :] = both.astype(BF16)
        second[...] = two[T:].astype(BF16)
        for i, out in enumerate((keep, one, three)):
            out[:rows, :] = place(i)
            out[rows:, :] = both

    shapes = [jax.ShapeDtypeStruct((T + EXTRA, width), BF16), jax.ShapeDtypeStruct((T, width), BF16)]
    shapes += [jax.ShapeDtypeStruct((rows + EXTRA, width), F32)] * 3
    return simple_call(kernel, "add_cores", shapes, near, back)


def add_place_2(one, three, first, second):
    rows = NZ * T

    def kernel(one_ref, three_ref, first_ref, second_ref, out1, out3):
        out1[:T, :] = plus(one_ref[:T, :], first_ref[:T, :]).astype(BF16)
        out1[T:rows, :] = one_ref[T:rows, :].astype(BF16)
        out1[rows:, :] = plus(one_ref[rows:, :], first_ref[T:, :]).astype(BF16)
        out3[:T, :] = three_ref[:T, :].astype(BF16)
        out3[T:rows, :] = plus(three_ref[T:rows, :], second_ref[...]).astype(BF16)
        out3[rows:, :] = three_ref[rows:, :].astype(BF16)

    shapes = [jax.ShapeDtypeStruct(one.shape, BF16)] * 2
    return simple_call(kernel, "add_place_2", shapes, one, three, first, second)


def add_rows(*parts):
    width = parts[0].shape[1]

    def kernel(*refs):
        ins, (keep, send) = refs[:3], refs[3:]
        loss = plus(*(r[NZ * T :, :] for r in ins))
        keep[:T, :] = plus(*(r[:T, :] for r in ins))
        keep[T:, :] = loss
        send[:T, :] = plus(*(r[T : NZ * T, :] for r in ins)).astype(BF16)
        send[T:, :] = loss.astype(BF16)

    shapes = [jax.ShapeDtypeStruct((T + EXTRA, width), F32), jax.ShapeDtypeStruct((T + EXTRA, width), BF16)]
    return simple_call(kernel, "add_rows", shapes, *parts)


def add_halves(one, three, first, second):
    half = one.shape[0] // NZ

    def kernel(one_ref, three_ref, first_ref, second_ref, out1, out3):
        out1[:half, :] = (one_ref[:half, :].astype(F32) + first_ref[...].astype(F32)).astype(BF16)
        out1[half:, :] = one_ref[half:, :]
        out3[:half, :] = three_ref[:half, :]
        out3[half:, :] = (three_ref[half:, :].astype(F32) + second_ref[...].astype(F32)).astype(BF16)

    shapes = [jax.ShapeDtypeStruct(one.shape, BF16)] * 2
    return simple_call(kernel, "add_halves", shapes, one, three, first, second)


def add_users(parts):
    width = parts[0].shape[0] // NZ

    def kernel(*refs):
        ins, (keep, send) = refs[:-2], refs[-2:]
        keep[...] = sum(r[:width, :].astype(F32) for r in ins)
        send[...] = sum(r[width:, :].astype(F32) for r in ins).astype(BF16)

    shapes = [jax.ShapeDtypeStruct((width, T), F32), jax.ShapeDtypeStruct((width, T), BF16)]
    return simple_call(kernel, "add_users", shapes, *parts)


def finish(keep_u, received_u, keep, received):
    def kernel(keep_u_ref, received_u_ref, keep_ref, received_ref, grad_u, grad, loss):
        grad_u[...] = plus(keep_u_ref[...], received_u_ref[...]).T
        grad[...] = plus(keep_ref[:T, :], received_ref[:T, :])
        loss[...] = jnp.sum(plus(keep_ref[T : T + 1, :], received_ref[T : T + 1, :]), axis=1, keepdims=True)

    shapes = [(T, keep_u.shape[0]), (T, keep.shape[1]), (1, 1)]
    shapes = [jax.ShapeDtypeStruct(x, F32) for x in shapes]
    return simple_call(kernel, "finish", shapes, keep_u, received_u, keep, received)


def join_stats(own, other):
    half = own.shape[0] // 2

    def kernel(own_ref, other_ref, out_ref):
        a, b = own_ref[:half, :], other_ref[:half, :]
        top = jnp.maximum(a, b)
        out_ref[:half, :] = top + jnp.log(jnp.exp(a - top) + jnp.exp(b - top))
        out_ref[half:, :] = own_ref[half:, :] + other_ref[half:, :]

    return simple_call(kernel, "join_stats", [jax.ShapeDtypeStruct(own.shape, F32)], own, other)[0]


def move(x, axis, target):
    return lax.ppermute(x, axis, [(i, target(i)) for i in range(lax.axis_size(axis))])


def shift_x(x, j):
    return move(x, "aa", lambda i: (i + j * NZ) % (NX * NZ))


def swap_z_hi(x):
    return move(x, "aa", lambda i: i ^ 1)


def shift_y(x, k):
    return move(x, "au", lambda i: i // 8 * 8 + (i % 8 + k * NC) % 8)


def swap_core(x):
    return move(x, "au", lambda i: i ^ 1)


def swap_z_lo(x):
    return move(x, "au", lambda i: i ^ 8)


def local(users, ads, counts, positives, weights):
    inv = users.shape[1] ** (-0.5)
    pos_row = (positives - lax.axis_index("aa") * counts.shape[0])[None, :]
    logc = jnp.log(counts.astype(F32))[None, :]
    weight_row = weights[None, :]
    users_z, ads_z, pos_row, logc = lax.optimization_barrier((swap_z_hi(users), swap_z_lo(ads), pos_row, logc))
    user_pair = jnp.concatenate([users, users_z], axis=0)
    ads_pair = jnp.concatenate([ads, ads_z], axis=0)
    user_1, user_3, ads_1, ads_3 = lax.optimization_barrier(
        (shift_x(user_pair, 1), shift_x(user_pair, -1), shift_y(ads_pair, 1), shift_y(ads_pair, -1))
    )
    user_2a, user_2b = shift_x(user_1[:T], 1), shift_x(user_3[T:], -1)
    ads_2a, ads_2b = shift_y(ads_1[:T], 1), shift_y(ads_3[T:], -1)
    near = jnp.concatenate([ads_pair, ads_1, ads_3], axis=0)
    far = swap_core(near)
    parts = (user_pair, user_1, user_3, user_2a, user_2b)

    rows_n, at_near = run_rows(("near",), (near,), pos_row, 0, positives.shape[0])
    p_near, top_near, acc, m, total, hits, staged, users_t = run_logits(
        "near", parts, (near,), logc, pos_row, inv, (at_near,)
    )
    ads_2a, ads_2b, hits = lax.optimization_barrier((ads_2a, ads_2b, hits))
    near_2 = jnp.concatenate([ads_2a, ads_2b], axis=0)
    far_2 = swap_core(near_2)
    p_far, top_far, acc, m, total, hits, at_far = run_logits(
        "far", (users_t,), (far,), logc, pos_row, inv, (acc, m, total, hits)
    )
    p_mid, top_mid, acc, m, total, hits, at_mid, stats = run_logits(
        "mid", (users_t,), (near_2, far_2), logc, pos_row, inv, (acc, m, total, hits)
    )
    half = positives.shape[0] // 2
    later = (("far", "mid"), (at_far, at_mid), pos_row)
    stats_z, (rows_a,) = lax.optimization_barrier((swap_z_hi(stats), run_rows(*later, 0, half)))
    stats = join_stats(stats, stats_z)
    moved = tuple(shift_x(stats, j) for j in range(1, NX))
    moved, (rows_b,) = lax.optimization_barrier((moved, run_rows(*later, half, half)))
    du_0, du_1, du_3, du_2a, du_2b, lse, coefs, loss = run_users(
        acc, m, rows_n, rows_a, rows_b, hits, weight_row, (stats, *moved), inv
    )
    tail = (lse, coefs, weight_row, pos_row, loss)
    du_2a, du_2b = shift_x(du_2a, 1), shift_x(du_2b, -1)
    da_far = run_grads("far", staged, p_far, p_mid, top_far, top_mid, *tail)
    da_far, du_2a, du_2b = lax.optimization_barrier((da_far, du_2a, du_2b))
    back = swap_core(da_far)
    du_1, du_3 = add_halves(du_1, du_3, du_2a, du_2b)
    du_1, du_3, staged = lax.optimization_barrier((du_1, du_3, staged))
    da_near = run_grads("near", staged, p_near, p_mid, top_near, top_mid, *tail)
    first, second, kept, one, three = add_cores(da_near, back)
    first, second, du_1, du_3 = lax.optimization_barrier((first, second, du_1, du_3))
    first, second = shift_y(first, -1), shift_y(second, 1)
    du_1, du_3 = shift_x(du_1, 1), shift_x(du_3, -1)
    first, second, du_1, du_3 = lax.optimization_barrier((first, second, du_1, du_3))
    one, three = add_place_2(one, three, first, second)
    one, three = shift_y(one, -1), shift_y(three, 1)
    keep_u, send_u = add_users((du_0, du_1, du_3))
    one, three, received_u = lax.optimization_barrier((one, three, swap_z_hi(send_u)))
    keep, send = add_rows(kept, one, three)
    grad_users, grad_ads, loss = finish(keep_u, received_u, keep, swap_z_lo(send))
    return grad_users, grad_ads, loss.reshape(())


def solution(mesh):
    return jax.shard_map(
        local,
        mesh=mesh,
        in_specs=(P(("au", "aa"), None), P(("aa", "au"), None), P("aa"), P("au"), P("au")),
        out_specs=(P(("au", "aa"), None), P(("aa", "au"), None), P()),
        check_vma=False,
    )
```

```python
import jax
import jax.numpy as jnp
from jax import lax
from jax.experimental import pallas as pl
from jax.experimental.pallas import tpu as pltpu
from jax.sharding import PartitionSpec as P

F32 = jnp.float32
BF16 = jnp.bfloat16
T = 256
LANES = 128
EXTRA = 16
LOG2E = 1.4426950408889634
LN2 = 0.6931471805599453
NX, NZ, NY, NC = 4, 2, 4, 2
VMEM_LIMIT = 24 * 2**20


def params():
    return pltpu.CompilerParams(vmem_limit_bytes=VMEM_LIMIT)


def call(kernel, name, out_shape, scratch, args, estimate=None):
    vmem = pl.BlockSpec(memory_space=pltpu.VMEM)
    return pl.pallas_call(
        kernel,
        in_specs=[vmem] * len(args),
        out_specs=[vmem] * len(out_shape),
        out_shape=out_shape,
        scratch_shapes=scratch,
        compiler_params=params(),
        cost_estimate=estimate,
        name=name,
    )(*args)


def user_block(j, zr):
    me = lax.axis_index("aa")
    x, z = me // NZ, me % NZ
    return lax.rem(x + NX - j, NX) * NZ + (z + zr - 2 * z * zr)


def ads_block(group, chunk):
    pair, zr = chunk // NZ, chunk % NZ
    k, cr = {"near": (pair ^ (pair >> 1), 0), "far": (pair ^ (pair >> 1), 1), "two": (2, 0)}[group]
    me = lax.axis_index("au")
    z, y, c = me // (NY * NC), (me // NC) % NY, me % NC
    return (z + zr - 2 * z * zr) * (NY * NC) + lax.rem(y + NY - k, NY) * NC + (c + cr - 2 * c * cr)


def stage_users(user_refs, staged, inv):
    for j in range(NX):
        for zr in range(NZ):
            spot = pl.multiple_of(user_block(j, zr) * T, T)
            block = user_refs[j][zr * T : (zr + 1) * T, :].astype(F32) * inv
            staged[pl.ds(spot, T), :] = block.astype(BF16)


def first_row(group, chunk):
    return pl.multiple_of(ads_block(group, chunk) * T, T)


def split(value):
    high = value.astype(BF16).astype(F32)
    mid = (value - high).astype(BF16).astype(F32)
    return high, mid, value - high - mid


def loss_rows(loss, width):
    high, mid, low = split(loss)
    lane = lax.broadcasted_iota(jnp.int32, (EXTRA, width), 1) - 3 * lax.axis_index("au")
    return jnp.where(lane == 0, high, jnp.where(lane == 1, mid, jnp.where(lane == 2, low, 0.0))).astype(BF16)


def plus(*values):
    return sum(v.astype(F32) for v in values)


def logits_kernel(group, n_ads, rows, inv, *refs):
    n = NX * NZ
    steps = n // 2
    chunks = rows // T
    first_call = group == "near"
    last_call = group == "far"
    if first_call:
        user_refs, refs = refs[:NX], refs[NX:]
    else:
        (users_t,), refs = refs[:1], refs[1:]
    ads_refs, refs = refs[:n_ads], refs[n_ads:]
    (logc_ref, pos_ref), refs = refs[:2], refs[2:]
    if not first_call:
        (acc_in, m_in, total_in, hit_in), refs = refs[:4], refs[4:]
    (p_ref, top_ref, ads_t, acc_ref, m_ref, total_ref, hit_ref), refs = refs[:7], refs[7:]
    if first_call:
        (staged, users_t), refs = refs[:2], refs[2:]
    if last_call:
        (stats_ref,), refs = refs[:1], refs[1:]
    ads_all, logc_all, s0, s1, *late = refs

    if first_call:
        stage_users(user_refs, staged, inv)
        for b in range(n):
            users_t[:, b * T : (b + 1) * T] = staged[b * T : (b + 1) * T, :].T
    spot = 0
    for r in ads_refs:
        ads_all[spot : spot + r.shape[0], :] = r[...]
        spot += r.shape[0]
    for c in range(chunks):
        part = slice(c * T, (c + 1) * T)
        ads_t[:, part] = ads_all[part, :].T
        logc = logc_ref[:, pl.ds(first_row(group, c), T)]
        logc_all[part, :] = jnp.broadcast_to(logc, (LANES, T)).T

    def columns(tile):
        return pl.ds(pl.multiple_of(tile * T, T), T)

    class Product:
        def __init__(self, tile, dst):
            self.cols, self.dst = columns(tile), dst
            self.side = users_t[:, self.cols]
            self.pos = pos_ref[:, self.cols] - lax.broadcasted_iota(jnp.int32, (8, T), 0)
            self.best = jnp.full((8, T), -jnp.inf, F32)
            self.found = jnp.zeros((8, T), F32)

        def chunk(self, c):
            ahead = self.pos - first_row(group, c)
            prod = jnp.dot(ads_all[c * T : (c + 1) * T, :], self.side, preferred_element_type=F32)
            for r in range(0, T, 8):
                row = c * T + r
                logc = logc_all[row : row + 8, :]
                x = prod[r : r + 8, :] * LOG2E - jnp.concatenate([logc] * (T // LANES), axis=1)
                self.dst[row : row + 8, :] = x
                self.best = jnp.maximum(self.best, x)
                self.found = jnp.where(ahead == r, x, self.found)

        def end(self):
            top_ref[:, self.cols] = jnp.max(self.best, axis=0, keepdims=True)
            hit = jnp.sum(self.found, axis=0, keepdims=True)
            hit_ref[:, self.cols] = hit if first_call else hit + hit_in[:, self.cols]

    class Exps:
        def __init__(self, tile, src, extra):
            self.cols, self.src, self.extra = columns(tile), src, extra
            self.top = top_ref[:, self.cols]
            self.total = jnp.zeros((8, T), F32)

        def chunk(self, c):
            for r in range(c * T, (c + 1) * T, 16):
                e = jnp.exp2(self.src[r : r + 16, :] - self.top)
                self.total += e[:8] + e[8:]
                e = e.astype(BF16)
                p_ref[r : r + 16, self.cols] = e
                self.extra[r : r + 16, :] = e

        def end(self):
            cols, top = self.cols, self.top
            total = jnp.sum(self.total, axis=0, keepdims=True)
            if first_call:
                m_ref[:, cols] = top
                total_ref[:, cols] = total
            else:
                m = jnp.maximum(m_in[:, cols], top)
                m_ref[:, cols] = m
                total_ref[:, cols] = total_in[:, cols] * jnp.exp2(m_in[:, cols] - m) + total * jnp.exp2(top - m)

    def gather(tile, e):
        cols = columns(tile)
        new = jnp.dot(ads_t[...], e[...], preferred_element_type=F32)
        if first_call:
            acc_ref[:, cols] = new
        else:
            m = m_ref[:, cols]
            acc_ref[:, cols] = acc_in[:, cols] * jnp.exp2(m_in[:, cols] - m) + new * jnp.exp2(top_ref[:, cols] - m)

    def turn(tile, src, dst, e_now, e_before):
        gather(jnp.maximum(tile - 1, 0), e_before)
        product, exps = Product(jnp.minimum(tile + 1, n - 1), dst), Exps(tile, src, e_now)
        for c in range(chunks):
            product.chunk(c)
            exps.chunk(c)
        product.end()
        exps.end()

    opening = Product(0, s0)
    for c in range(chunks):
        opening.chunk(c)
    opening.end()
    e0, e1 = late
    e1[...] = jnp.zeros_like(e1)
    m_ref[...] = jnp.zeros_like(m_ref) if first_call else m_in[...]

    @pl.loop(0, steps)
    def _(step):
        turn(2 * step, s0, s1, e0, e1)
        turn(2 * step + 1, s1, s0, e1, e0)

    gather(n - 1, e1)
    if last_call:
        lse = m_ref[...] + jnp.log2(total_ref[...])
        width = n * T // LANES
        for r in range(width):
            cols = slice(r * LANES, (r + 1) * LANES)
            stats_ref[r : r + 1, :] = lse[:, cols]
            stats_ref[width + r : width + r + 1, :] = hit_ref[:, cols]


def cost(rows, total, width):
    return pl.CostEstimate(flops=rows * total * width // 8, bytes_accessed=rows * total // 8, transcendentals=0)


def run_logits(group, users, ads, logc, positives, inv, before=()):
    width = ads[0].shape[1]
    count = sum(x.shape[0] for x in ads)
    total = NX * NZ * T
    stats_rows = 2 * total // LANES
    row = jax.ShapeDtypeStruct((1, total), F32)
    out_shape = [
        jax.ShapeDtypeStruct((count, total), BF16),
        row,
        jax.ShapeDtypeStruct((width, count), BF16),
        jax.ShapeDtypeStruct((width, total), F32),
        row,
        row,
        row,
    ]
    if group == "near":
        out_shape.append(jax.ShapeDtypeStruct((total, width), BF16))
        out_shape.append(jax.ShapeDtypeStruct((width, total), BF16))
    if group == "far":
        out_shape.append(jax.ShapeDtypeStruct((stats_rows, LANES), F32))
    scratch = [
        pltpu.VMEM((count, width), BF16),
        pltpu.VMEM((count, LANES), F32),
        pltpu.VMEM((count, T), F32),
        pltpu.VMEM((count, T), F32),
        pltpu.VMEM((count, T), BF16),
        pltpu.VMEM((count, T), BF16),
    ]
    return call(
        lambda *refs: logits_kernel(group, len(ads), count, inv, *refs),
        "logits_" + group,
        out_shape,
        scratch,
        (*users, *ads, logc, positives, *before),
        cost(count, total, width),
    )


GROUPS = ("near", "two", "far")


def rows_kernel(sizes, start, *refs):
    ads_refs, (pos_ref, out_ref, h0, h1) = refs[: len(sizes)], refs[len(sizes) :]
    tiles = out_ref.shape[1] // T

    def build(tile, dst):
        cols = pl.ds(pl.multiple_of(start + tile * T, T), T)
        pos = pos_ref[:, cols] - lax.broadcasted_iota(jnp.int32, (16, T), 0)
        spot = 0
        for group, size in zip(GROUPS, sizes):
            for c in range(size // T):
                ahead = pos - first_row(group, c)
                for r in range(0, T, 16):
                    dst[spot + r : spot + r + 16, :] = jnp.where(ahead == r, 1.0, 0.0).astype(BF16)
                spot += T

    def product(tile, src):
        cols = pl.ds(pl.multiple_of(tile * T, T), T)
        out = jnp.zeros((out_ref.shape[0], T), F32)
        spot = 0
        for ads, size in zip(ads_refs, sizes):
            out += jnp.dot(ads[...], src[spot : spot + size, :], preferred_element_type=F32)
            spot += size
        out_ref[:, cols] = out.astype(BF16)

    build(0, h0)

    @pl.loop(0, tiles // 2)
    def _(step):
        product(2 * step, h0)
        build(2 * step + 1, h1)
        product(2 * step + 1, h1)
        build(jnp.minimum(2 * step + 2, tiles - 1), h0)


def run_rows(ads_t, positives, start, total):
    width = ads_t[0].shape[0]
    sizes = [x.shape[1] for x in ads_t]
    return call(
        lambda *refs: rows_kernel(sizes, start, *refs),
        "positive_rows",
        [jax.ShapeDtypeStruct((width, total), BF16)],
        [pltpu.VMEM((sum(sizes), T), BF16)] * 2,
        (*ads_t, positives),
        cost(sum(sizes), total, width),
    )[0]


def users_kernel(inv, acc_ref, m_ref, rows_a, rows_b, hit_ref, weight_ref, *rest):
    stats_in, rest = rest[:NX], rest[NX:]
    du_refs, (lse_ref, coef_ref, loss_ref, stats_ref, rows_ref) = rest[:-5], rest[-5:]
    n = NX * NZ
    width = n * T // LANES
    for j in range(NX):
        stats_ref[pl.ds(lax.rem(lax.axis_index("aa") // NZ + NX - j, NX), 1)] = stats_in[j][...][None]
    rows_ref[:, : n * T // 2] = rows_a[...]
    rows_ref[:, n * T // 2 :] = rows_b[...]
    tops = stats_ref[:, :width, :]
    top = jnp.max(tops, axis=0)
    lse = top + jnp.log2(jnp.sum(jnp.exp2(tops - top[None]), axis=0))
    diff = (lse - jnp.sum(stats_ref[:, width:, :], axis=0)) * LN2
    loss = jnp.zeros((1, LANES), F32)
    for r in range(width):
        cols = slice(r * LANES, (r + 1) * LANES)
        lse_ref[:, cols] = lse[r : r + 1, :]
        loss += weight_ref[:, cols] * diff[r : r + 1, :]
    loss_ref[...] = loss_rows(jnp.sum(loss, axis=1, keepdims=True), loss_ref.shape[1])
    coef_ref[...] = weight_ref[...] * (jnp.exp2(hit_ref[...] - lse_ref[...]) - 1.0)

    def users_at(j, zr):
        cols = pl.ds(pl.multiple_of(user_block((NX - j) % NX, zr) * T, T), T)
        weight = weight_ref[:, cols] * inv
        scale = weight * jnp.exp2(m_ref[:, cols] - lse_ref[:, cols])
        return (acc_ref[:, cols] * scale - rows_ref[:, cols].astype(F32) * weight).astype(BF16)

    for part, j in enumerate((0, 1, 3)):
        for zr in range(NZ):
            du_refs[part][zr * T : (zr + 1) * T, :] = users_at(j, zr)
    du_refs[3][...] = users_at(2, 0)
    du_refs[4][...] = users_at(2, 1)


def run_users(acc, m, rows_a, rows_b, hits, weights, stats, inv):
    width, total = acc.shape
    row = jax.ShapeDtypeStruct((1, total), F32)
    shapes = [(NZ * width, T)] * 3 + [(width, T)] * 2
    out_shape = [jax.ShapeDtypeStruct(x, BF16) for x in shapes]
    out_shape += [row, row, jax.ShapeDtypeStruct((EXTRA, width), BF16)]
    return call(
        lambda *refs: users_kernel(inv, *refs),
        "grad_users",
        out_shape,
        [pltpu.VMEM((NX, *stats[0].shape), F32), pltpu.VMEM((width, total), BF16)],
        (acc, m, rows_a, rows_b, hits, weights, *stats),
    )


def grads_kernel(units, users_ref, lse_ref, coef_ref, weight_ref, pos_ref, loss_in, *refs):
    ps, tops, outs, qs = refs[: len(units)], refs[len(units) : 2 * len(units)], refs[2 * len(units) : -2], refs[-2:]
    deep = 2 * T
    total = users_ref.shape[0]

    def build(i, dst):
        group, at = units[i]
        for b in range(total // T):
            cols = slice(b * T, (b + 1) * T)
            scale = weight_ref[:, cols] * jnp.exp2(tops[i][:, cols] - lse_ref[:, cols])
            coef = coef_ref[:, cols]
            pos = pos_ref[:, cols] - lax.broadcasted_iota(jnp.int32, (16, T), 0)
            for half in range(2):
                ahead = pos - first_row(group, 2 * at + half)
                for r in range(0, T, 16):
                    row = half * T + r
                    scaled = ps[i][at * deep + row : at * deep + row + 16, cols].astype(F32) * scale
                    dst[row : row + 16, cols] = jnp.where(ahead == r, coef, scaled).astype(BF16)

    build(0, qs[0])
    for i in range(len(units)):
        da = jnp.dot(qs[i % 2][...], users_ref[...], preferred_element_type=F32)
        if i + 1 < len(units):
            build(i + 1, qs[(i + 1) % 2])
        da = da.astype(BF16)
        if len(outs) == 1:
            outs[0][i * deep : (i + 1) * deep, :] = da
        else:
            outs[i][:deep, :] = da
            outs[i][deep:, :] = loss_in[...]


def run_grads(name, units, users, lse, coefs, weights, positives, loss):
    total, width = users.shape
    deep = 2 * T
    places = [u[:2] for u in units]
    if name == "mid":
        shapes = [(deep + EXTRA, width)] * 2
    else:
        shapes = [(len(units) * deep, width)]
    return call(
        lambda *refs: grads_kernel(places, *refs),
        "grads_" + name,
        [jax.ShapeDtypeStruct(x, BF16) for x in shapes],
        [pltpu.VMEM((deep, total), BF16)] * 2,
        (users, lse, coefs, weights, positives, loss, *(u[2] for u in units), *(u[3] for u in units)),
        cost(len(units) * deep, total, width),
    )


def simple_call(kernel, name, out_shape, *args):
    return call(kernel, name, out_shape, [], args)


def add_mid(near, back):
    width = near.shape[1]

    def kernel(near_ref, back_ref, first, second, both):
        total = plus(near_ref[...], back_ref[...]).astype(BF16)
        first[:T, :] = total[:T, :]
        first[T:, :] = total[NZ * T :, :]
        second[...] = total[T : NZ * T, :]
        both[...] = total[NZ * T :, :]

    shapes = [(T + EXTRA, width), (T, width), (EXTRA, width)]
    return simple_call(kernel, "add_mid", [jax.ShapeDtypeStruct(x, BF16) for x in shapes], near, back)


def add_near(near, back, both, first, second):
    width = near.shape[1]
    rows = NZ * T

    def kernel(near_ref, back_ref, both_ref, first_ref, second_ref, keep, one, three):
        def term(i):
            return plus(near_ref[i * T : (i + 1) * T, :], back_ref[i * T : (i + 1) * T, :])

        keep[:T, :] = term(0)
        keep[T:rows, :] = term(1)
        keep[rows:, :] = both_ref[...].astype(F32)
        one[:T, :] = plus(term(2), first_ref[:T, :]).astype(BF16)
        one[T:rows, :] = term(3).astype(BF16)
        one[rows:, :] = plus(both_ref[...], first_ref[T:, :]).astype(BF16)
        three[:T, :] = term(4).astype(BF16)
        three[T:rows, :] = plus(term(5), second_ref[...]).astype(BF16)
        three[rows:, :] = both_ref[...]

    shapes = [jax.ShapeDtypeStruct((rows + EXTRA, width), t) for t in (F32, BF16, BF16)]
    return simple_call(kernel, "add_near", shapes, near, back, both, first, second)


def add_rows(*parts):
    width = parts[0].shape[1]

    def kernel(*refs):
        ins, (keep, send) = refs[:-2], refs[-2:]
        loss = plus(*(r[NZ * T :, :] for r in ins))
        keep[:T, :] = plus(*(r[:T, :] for r in ins))
        keep[T:, :] = loss
        send[:T, :] = plus(*(r[T : NZ * T, :] for r in ins)).astype(BF16)
        send[T:, :] = loss.astype(BF16)

    shapes = [jax.ShapeDtypeStruct((T + EXTRA, width), F32), jax.ShapeDtypeStruct((T + EXTRA, width), BF16)]
    return simple_call(kernel, "add_rows", shapes, *parts)


def add_halves(one, three, first, second):
    half = one.shape[0] // NZ

    def kernel(one_ref, three_ref, first_ref, second_ref, out1, out3):
        out1[:half, :] = (one_ref[:half, :].astype(F32) + first_ref[...].astype(F32)).astype(BF16)
        out1[half:, :] = one_ref[half:, :]
        out3[:half, :] = three_ref[:half, :]
        out3[half:, :] = (three_ref[half:, :].astype(F32) + second_ref[...].astype(F32)).astype(BF16)

    shapes = [jax.ShapeDtypeStruct(one.shape, BF16)] * 2
    return simple_call(kernel, "add_halves", shapes, one, three, first, second)


def add_users(parts):
    width = parts[0].shape[0] // NZ

    def kernel(*refs):
        ins, (keep, send) = refs[:-2], refs[-2:]
        keep[...] = sum(r[:width, :].astype(F32) for r in ins)
        send[...] = sum(r[width:, :].astype(F32) for r in ins).astype(BF16)

    shapes = [jax.ShapeDtypeStruct((width, T), F32), jax.ShapeDtypeStruct((width, T), BF16)]
    return simple_call(kernel, "add_users", shapes, *parts)


def finish(keep_u, received_u, keep, received):
    def kernel(keep_u_ref, received_u_ref, keep_ref, received_ref, grad_u, grad, loss):
        grad_u[...] = plus(keep_u_ref[...], received_u_ref[...]).T
        grad[...] = plus(keep_ref[:T, :], received_ref[:T, :])
        loss[...] = jnp.sum(plus(keep_ref[T : T + 1, :], received_ref[T : T + 1, :]), axis=1, keepdims=True)

    shapes = [(T, keep_u.shape[0]), (T, keep.shape[1]), (1, 1)]
    shapes = [jax.ShapeDtypeStruct(x, F32) for x in shapes]
    return simple_call(kernel, "finish", shapes, keep_u, received_u, keep, received)


def join_stats(own, other):
    half = own.shape[0] // 2

    def kernel(own_ref, other_ref, out_ref):
        a, b = own_ref[:half, :], other_ref[:half, :]
        top = jnp.maximum(a, b)
        out_ref[:half, :] = top + jnp.log2(jnp.exp2(a - top) + jnp.exp2(b - top))
        out_ref[half:, :] = own_ref[half:, :] + other_ref[half:, :]

    return simple_call(kernel, "join_stats", [jax.ShapeDtypeStruct(own.shape, F32)], own, other)[0]


def move(x, axis, target):
    return lax.ppermute(x, axis, [(i, target(i)) for i in range(lax.axis_size(axis))])


def shift_x(x, j):
    return move(x, "aa", lambda i: (i + j * NZ) % (NX * NZ))


def swap_z_hi(x):
    return move(x, "aa", lambda i: i ^ 1)


def shift_y(x, k):
    return move(x, "au", lambda i: i // 8 * 8 + (i % 8 + k * NC) % 8)


def swap_core(x):
    return move(x, "au", lambda i: i ^ 1)


def swap_z_lo(x):
    return move(x, "au", lambda i: i ^ 8)


def local(users, ads, counts, positives, weights):
    inv = users.shape[1] ** (-0.5)
    pos_row = (positives - lax.axis_index("aa") * counts.shape[0])[None, :]
    logc = (jnp.log(counts.astype(F32)) * LOG2E)[None, :]
    weight_row = weights[None, :]
    users_z, ads_z, pos_row, logc = lax.optimization_barrier((swap_z_hi(users), swap_z_lo(ads), pos_row, logc))
    user_pair = jnp.concatenate([users, users_z], axis=0)
    ads_pair = jnp.concatenate([ads, ads_z], axis=0)
    user_pair, ads_pair = lax.optimization_barrier((user_pair, ads_pair))
    user_2 = shift_x(user_pair, 2)
    user_1, user_3 = shift_x(user_pair, 1), shift_x(user_pair, -1)
    ads_1, ads_3 = shift_y(ads_pair, 1), shift_y(ads_pair, -1)
    ads_2 = shift_y(ads_pair, 2)
    parts = lax.optimization_barrier((user_pair, user_1, user_2, user_3))

    p_near, top_near, at_near, acc, m, total, hits, staged, users_t = run_logits(
        "near", parts, (ads_pair, ads_1, ads_3), logc, pos_row, inv
    )
    ads_2, ads_1, ads_3, hits = lax.optimization_barrier((ads_2, ads_1, ads_3, hits))
    far = swap_core(jnp.concatenate([ads_pair, ads_1, ads_3, ads_2], axis=0))
    p_two, top_two, at_two, acc, m, total, hits = run_logits(
        "two", (users_t,), (ads_2,), logc, pos_row, inv, (acc, m, total, hits)
    )
    p_far, top_far, at_far, acc, m, total, hits, stats = run_logits(
        "far", (users_t,), (far,), logc, pos_row, inv, (acc, m, total, hits)
    )
    half = stats.shape[0] * LANES // 4
    ads_t = (at_near, at_two, at_far)
    stats_z, rows_a = lax.optimization_barrier((swap_z_hi(stats), run_rows(ads_t, pos_row, 0, half)))
    stats = join_stats(stats, stats_z)
    moved = tuple(shift_x(stats, j) for j in range(1, NX))
    moved, rows_b = lax.optimization_barrier((moved, run_rows(ads_t, pos_row, half, half)))
    du_0, du_1, du_3, du_2a, du_2b, lse, coefs, loss = run_users(
        acc, m, rows_a, rows_b, hits, weight_row, (stats, *moved), inv
    )
    tail = (lse, coefs, weight_row, pos_row, loss)
    pay_2, da_2 = run_grads("mid", [("far", 3, p_far, top_far), ("two", 0, p_two, top_two)], staged, *tail)
    back_2 = swap_core(pay_2)
    da_2, staged = lax.optimization_barrier((da_2, staged))
    (da_near,) = run_grads("near", [("near", i, p_near, top_near) for i in range(3)], staged, *tail)
    da_near, back_2 = lax.optimization_barrier((da_near, back_2))
    first, second, both = add_mid(da_2, back_2)
    first, second, staged = lax.optimization_barrier((first, second, staged))
    first, second = shift_y(first, -1), shift_y(second, 1)
    du_2a, du_2b = shift_x(du_2a, 1), shift_x(du_2b, -1)
    (da_far,) = run_grads("far", [("far", i, p_far, top_far) for i in range(3)], staged, *tail)
    back = swap_core(da_far)
    first, second, du_2a, du_2b = lax.optimization_barrier((first, second, du_2a, du_2b))
    du_1, du_3 = add_halves(du_1, du_3, du_2a, du_2b)
    du_1, du_3 = shift_x(du_1, 1), shift_x(du_3, -1)
    kept, one, three = add_near(da_near, back, both, first, second)
    one, three = shift_y(one, -1), shift_y(three, 1)
    keep_u, send_u = add_users((du_0, du_1, du_3))
    one, three, received_u = lax.optimization_barrier((one, three, swap_z_hi(send_u)))
    keep, send = add_rows(kept, one, three)
    grad_users, grad_ads, loss = finish(keep_u, received_u, keep, swap_z_lo(send))
    return grad_users, grad_ads, loss.reshape(())


def solution(mesh):
    return jax.shard_map(
        local,
        mesh=mesh,
        in_specs=(P(("au", "aa"), None), P(("aa", "au"), None), P("aa"), P("au"), P("au")),
        out_specs=(P(("au", "aa"), None), P(("aa", "au"), None), P()),
        check_vma=False,
    )
```

```python
import jax
import jax.numpy as jnp
from jax import lax
from jax.experimental import pallas as pl
from jax.experimental.pallas import tpu as pltpu
from jax.sharding import PartitionSpec as P

F32 = jnp.float32
BF16 = jnp.bfloat16
T = 256
LANES = 128
EXTRA = 16
LOG2E = 1.4426950408889634
LN2 = 0.6931471805599453
NX, NZ, NY, NC = 4, 2, 4, 2
VMEM_LIMIT = 24 * 2**20


def params():
    return pltpu.CompilerParams(vmem_limit_bytes=VMEM_LIMIT)


def call(kernel, name, out_shape, scratch, args, estimate=None):
    vmem = pl.BlockSpec(memory_space=pltpu.VMEM)
    return pl.pallas_call(
        kernel,
        in_specs=[vmem] * len(args),
        out_specs=[vmem] * len(out_shape),
        out_shape=out_shape,
        scratch_shapes=scratch,
        compiler_params=params(),
        cost_estimate=estimate,
        name=name,
    )(*args)


def user_block(j, zr):
    me = lax.axis_index("aa")
    x, z = me // NZ, me % NZ
    return lax.rem(x + NX - j, NX) * NZ + (z + zr - 2 * z * zr)


def ads_block(group, chunk):
    pair, zr = chunk // NZ, chunk % NZ
    k, cr = {"near": (pair ^ (pair >> 1), 0), "far": (pair ^ (pair >> 1), 1), "two": (2, 0)}[group]
    me = lax.axis_index("au")
    z, y, c = me // (NY * NC), (me // NC) % NY, me % NC
    return (z + zr - 2 * z * zr) * (NY * NC) + lax.rem(y + NY - k, NY) * NC + (c + cr - 2 * c * cr)


def stage_users(user_refs, staged, inv):
    for j in range(NX):
        for zr in range(NZ):
            spot = pl.multiple_of(user_block(j, zr) * T, T)
            block = user_refs[j][zr * T : (zr + 1) * T, :].astype(F32) * inv
            staged[pl.ds(spot, T), :] = block.astype(BF16)


def first_row(group, chunk):
    return pl.multiple_of(ads_block(group, chunk) * T, T)


def split(value):
    high = value.astype(BF16).astype(F32)
    mid = (value - high).astype(BF16).astype(F32)
    return high, mid, value - high - mid


def loss_rows(loss, width):
    high, mid, low = split(loss)
    lane = lax.broadcasted_iota(jnp.int32, (EXTRA, width), 1) - 3 * lax.axis_index("au")
    return jnp.where(lane == 0, high, jnp.where(lane == 1, mid, jnp.where(lane == 2, low, 0.0))).astype(BF16)


def plus(*values):
    return sum(v.astype(F32) for v in values)


def logits_kernel(group, n_ads, rows, inv, *refs):
    n = NX * NZ
    steps = n // 2
    chunks = rows // T
    deep = 2 * T
    first_call = group == "near"
    last_call = group == "far"
    if first_call:
        user_refs, refs = refs[:NX], refs[NX:]
    else:
        (users_t,), refs = refs[:1], refs[1:]
    ads_refs, refs = refs[:n_ads], refs[n_ads:]
    (logc_ref, pos_ref), refs = refs[:2], refs[2:]
    if not first_call:
        (acc_in, m_in, total_in, hit_in), refs = refs[:4], refs[4:]
    (p_ref, top_ref, ads_t, acc_ref, m_ref, total_ref, hit_ref), refs = refs[:7], refs[7:]
    if first_call:
        (staged, users_t), refs = refs[:2], refs[2:]
    if last_call:
        (stats_ref,), refs = refs[:1], refs[1:]
    ads_all, logc_all, s0, s1, *late = refs

    if first_call:
        stage_users(user_refs, staged, inv)
        for b in range(n):
            users_t[:, b * T : (b + 1) * T] = staged[b * T : (b + 1) * T, :].T
    spot = 0
    for r in ads_refs:
        ads_all[spot : spot + r.shape[0], :] = r[...]
        spot += r.shape[0]
    for c in range(chunks):
        part = slice(c * T, (c + 1) * T)
        ads_t[:, part] = ads_all[part, :].T
        logc = logc_ref[:, pl.ds(first_row(group, c), T)]
        logc_all[part, :] = jnp.broadcast_to(logc, (LANES, T)).T

    def columns(tile):
        return pl.ds(pl.multiple_of(tile * T, T), T)

    def product(tile, dst):
        side = users_t[:, columns(tile)]
        for c in range(0, rows, deep):
            dst[c : c + deep, :] = jnp.dot(ads_all[c : c + deep, :], side, preferred_element_type=F32)

    def exps(tile, src, extra):
        cols = columns(tile)
        pos = pos_ref[:, cols] - lax.broadcasted_iota(jnp.int32, (8, T), 0)
        best = jnp.full((8, T), -jnp.inf, F32)
        found = jnp.zeros((8, T), F32)
        for c in range(chunks):
            ahead = pos - first_row(group, c)
            for r in range(0, T, 8):
                at = slice(c * T + r, c * T + r + 8)
                x = src[at, :] * LOG2E - jnp.concatenate([logc_all[at, :]] * (T // LANES), axis=1)
                src[at, :] = x
                best = jnp.maximum(best, x)
                found = jnp.where(ahead == r, x, found)
        top = jnp.max(best, axis=0, keepdims=True)
        top_ref[:, cols] = top
        hit = jnp.sum(found, axis=0, keepdims=True)
        hit_ref[:, cols] = hit if first_call else hit + hit_in[:, cols]
        total = jnp.zeros((8, T), F32)
        for r in range(0, rows, 16):
            e = jnp.exp2(src[r : r + 16, :] - top)
            total += e[:8] + e[8:]
            e = e.astype(BF16)
            p_ref[r : r + 16, cols] = e
            extra[r : r + 16, :] = e
        total = jnp.sum(total, axis=0, keepdims=True)
        if first_call:
            m_ref[:, cols] = top
            total_ref[:, cols] = total
        else:
            m = jnp.maximum(m_in[:, cols], top)
            m_ref[:, cols] = m
            total_ref[:, cols] = total_in[:, cols] * jnp.exp2(m_in[:, cols] - m) + total * jnp.exp2(top - m)

    def gather(tile, e):
        cols = columns(tile)
        new = jnp.dot(ads_t[...], e[...], preferred_element_type=F32)
        if first_call:
            acc_ref[:, cols] = new
        else:
            m = m_ref[:, cols]
            acc_ref[:, cols] = acc_in[:, cols] * jnp.exp2(m_in[:, cols] - m) + new * jnp.exp2(top_ref[:, cols] - m)

    def turn(tile, src, dst, e_now, e_before):
        gather(jnp.maximum(tile - 1, 0), e_before)
        product(jnp.minimum(tile + 1, n - 1), dst)
        exps(tile, src, e_now)

    product(0, s0)
    e0, e1 = late
    e1[...] = jnp.zeros_like(e1)
    m_ref[...] = jnp.zeros_like(m_ref) if first_call else m_in[...]

    @pl.loop(0, steps)
    def _(step):
        turn(2 * step, s0, s1, e0, e1)
        turn(2 * step + 1, s1, s0, e1, e0)

    gather(n - 1, e1)
    if last_call:
        lse = m_ref[...] + jnp.log2(total_ref[...])
        width = n * T // LANES
        for r in range(width):
            cols = slice(r * LANES, (r + 1) * LANES)
            stats_ref[r : r + 1, :] = lse[:, cols]
            stats_ref[width + r : width + r + 1, :] = hit_ref[:, cols]


def cost(rows, total, width):
    return pl.CostEstimate(flops=rows * total * width // 8, bytes_accessed=rows * total // 8, transcendentals=0)


def run_logits(group, users, ads, logc, positives, inv, before=()):
    width = ads[0].shape[1]
    count = sum(x.shape[0] for x in ads)
    total = NX * NZ * T
    stats_rows = 2 * total // LANES
    row = jax.ShapeDtypeStruct((1, total), F32)
    out_shape = [
        jax.ShapeDtypeStruct((count, total), BF16),
        row,
        jax.ShapeDtypeStruct((width, count), BF16),
        jax.ShapeDtypeStruct((width, total), F32),
        row,
        row,
        row,
    ]
    if group == "near":
        out_shape.append(jax.ShapeDtypeStruct((total, width), BF16))
        out_shape.append(jax.ShapeDtypeStruct((width, total), BF16))
    if group == "far":
        out_shape.append(jax.ShapeDtypeStruct((stats_rows, LANES), F32))
    scratch = [
        pltpu.VMEM((count, width), BF16),
        pltpu.VMEM((count, LANES), F32),
        pltpu.VMEM((count, T), F32),
        pltpu.VMEM((count, T), F32),
        pltpu.VMEM((count, T), BF16),
        pltpu.VMEM((count, T), BF16),
    ]
    return call(
        lambda *refs: logits_kernel(group, len(ads), count, inv, *refs),
        "logits_" + group,
        out_shape,
        scratch,
        (*users, *ads, logc, positives, *before),
        cost(count, total, width),
    )


GROUPS = ("near", "two", "far")


def rows_kernel(sizes, start, *refs):
    ads_refs, (pos_ref, out_ref, h0, h1) = refs[: len(sizes)], refs[len(sizes) :]
    tiles = out_ref.shape[1] // T

    def build(tile, dst):
        cols = pl.ds(pl.multiple_of(start + tile * T, T), T)
        pos = pos_ref[:, cols] - lax.broadcasted_iota(jnp.int32, (16, T), 0)
        spot = 0
        for group, size in zip(GROUPS, sizes):
            for c in range(size // T):
                ahead = pos - first_row(group, c)
                for r in range(0, T, 16):
                    dst[spot + r : spot + r + 16, :] = jnp.where(ahead == r, 1.0, 0.0).astype(BF16)
                spot += T

    def product(tile, src):
        cols = pl.ds(pl.multiple_of(tile * T, T), T)
        out = jnp.zeros((out_ref.shape[0], T), F32)
        spot = 0
        for ads, size in zip(ads_refs, sizes):
            out += jnp.dot(ads[...], src[spot : spot + size, :], preferred_element_type=F32)
            spot += size
        out_ref[:, cols] = out.astype(BF16)

    build(0, h0)

    @pl.loop(0, tiles // 2)
    def _(step):
        product(2 * step, h0)
        build(2 * step + 1, h1)
        product(2 * step + 1, h1)
        build(jnp.minimum(2 * step + 2, tiles - 1), h0)


def run_rows(ads_t, positives, start, total):
    width = ads_t[0].shape[0]
    sizes = [x.shape[1] for x in ads_t]
    return call(
        lambda *refs: rows_kernel(sizes, start, *refs),
        "positive_rows",
        [jax.ShapeDtypeStruct((width, total), BF16)],
        [pltpu.VMEM((sum(sizes), T), BF16)] * 2,
        (*ads_t, positives),
        cost(sum(sizes), total, width),
    )[0]


def users_kernel(inv, acc_ref, m_ref, rows_a, rows_b, hit_ref, weight_ref, *rest):
    stats_in, rest = rest[:NX], rest[NX:]
    du_refs, (lse_ref, coef_ref, loss_ref, stats_ref, rows_ref) = rest[:-5], rest[-5:]
    n = NX * NZ
    width = n * T // LANES
    for j in range(NX):
        stats_ref[pl.ds(lax.rem(lax.axis_index("aa") // NZ + NX - j, NX), 1)] = stats_in[j][...][None]
    rows_ref[:, : n * T // 2] = rows_a[...]
    rows_ref[:, n * T // 2 :] = rows_b[...]
    tops = stats_ref[:, :width, :]
    top = jnp.max(tops, axis=0)
    lse = top + jnp.log2(jnp.sum(jnp.exp2(tops - top[None]), axis=0))
    diff = (lse - jnp.sum(stats_ref[:, width:, :], axis=0)) * LN2
    loss = jnp.zeros((1, LANES), F32)
    for r in range(width):
        cols = slice(r * LANES, (r + 1) * LANES)
        lse_ref[:, cols] = lse[r : r + 1, :]
        loss += weight_ref[:, cols] * diff[r : r + 1, :]
    loss_ref[...] = loss_rows(jnp.sum(loss, axis=1, keepdims=True), loss_ref.shape[1])
    coef_ref[...] = weight_ref[...] * (jnp.exp2(hit_ref[...] - lse_ref[...]) - 1.0)

    def users_at(j, zr):
        cols = pl.ds(pl.multiple_of(user_block((NX - j) % NX, zr) * T, T), T)
        weight = weight_ref[:, cols] * inv
        scale = weight * jnp.exp2(m_ref[:, cols] - lse_ref[:, cols])
        return (acc_ref[:, cols] * scale - rows_ref[:, cols].astype(F32) * weight).astype(BF16)

    for part, j in enumerate((0, 1, 3)):
        for zr in range(NZ):
            du_refs[part][zr * T : (zr + 1) * T, :] = users_at(j, zr)
    du_refs[3][...] = users_at(2, 0)
    du_refs[4][...] = users_at(2, 1)


def run_users(acc, m, rows_a, rows_b, hits, weights, stats, inv):
    width, total = acc.shape
    row = jax.ShapeDtypeStruct((1, total), F32)
    shapes = [(NZ * width, T)] * 3 + [(width, T)] * 2
    out_shape = [jax.ShapeDtypeStruct(x, BF16) for x in shapes]
    out_shape += [row, row, jax.ShapeDtypeStruct((EXTRA, width), BF16)]
    return call(
        lambda *refs: users_kernel(inv, *refs),
        "grad_users",
        out_shape,
        [pltpu.VMEM((NX, *stats[0].shape), F32), pltpu.VMEM((width, total), BF16)],
        (acc, m, rows_a, rows_b, hits, weights, *stats),
    )


def grads_kernel(units, users_ref, lse_ref, coef_ref, weight_ref, pos_ref, loss_in, *refs):
    ps, tops, outs, qs = refs[: len(units)], refs[len(units) : 2 * len(units)], refs[2 * len(units) : -2], refs[-2:]
    deep = 2 * T
    total = users_ref.shape[0]

    def build(i, dst):
        group, at = units[i]
        for b in range(total // T):
            cols = slice(b * T, (b + 1) * T)
            scale = weight_ref[:, cols] * jnp.exp2(tops[i][:, cols] - lse_ref[:, cols])
            coef = coef_ref[:, cols]
            pos = pos_ref[:, cols] - lax.broadcasted_iota(jnp.int32, (16, T), 0)
            for half in range(2):
                ahead = pos - first_row(group, 2 * at + half)
                for r in range(0, T, 16):
                    row = half * T + r
                    scaled = ps[i][at * deep + row : at * deep + row + 16, cols].astype(F32) * scale
                    dst[row : row + 16, cols] = jnp.where(ahead == r, coef, scaled).astype(BF16)

    build(0, qs[0])
    for i in range(len(units)):
        da = jnp.dot(qs[i % 2][...], users_ref[...], preferred_element_type=F32)
        if i + 1 < len(units):
            build(i + 1, qs[(i + 1) % 2])
        da = da.astype(BF16)
        if len(outs) == 1:
            outs[0][i * deep : (i + 1) * deep, :] = da
        else:
            outs[i][:deep, :] = da
            outs[i][deep:, :] = loss_in[...]


def run_grads(name, units, users, lse, coefs, weights, positives, loss):
    total, width = users.shape
    deep = 2 * T
    places = [u[:2] for u in units]
    if name == "mid":
        shapes = [(deep + EXTRA, width)] * 2
    else:
        shapes = [(len(units) * deep, width)]
    return call(
        lambda *refs: grads_kernel(places, *refs),
        "grads_" + name,
        [jax.ShapeDtypeStruct(x, BF16) for x in shapes],
        [pltpu.VMEM((deep, total), BF16)] * 2,
        (users, lse, coefs, weights, positives, loss, *(u[2] for u in units), *(u[3] for u in units)),
        cost(len(units) * deep, total, width),
    )


def simple_call(kernel, name, out_shape, *args):
    return call(kernel, name, out_shape, [], args)


def add_mid(near, back):
    width = near.shape[1]

    def kernel(near_ref, back_ref, first, second, both):
        total = plus(near_ref[...], back_ref[...]).astype(BF16)
        first[:T, :] = total[:T, :]
        first[T:, :] = total[NZ * T :, :]
        second[...] = total[T : NZ * T, :]
        both[...] = total[NZ * T :, :]

    shapes = [(T + EXTRA, width), (T, width), (EXTRA, width)]
    return simple_call(kernel, "add_mid", [jax.ShapeDtypeStruct(x, BF16) for x in shapes], near, back)


def add_near(near, back, both, first, second):
    width = near.shape[1]
    rows = NZ * T

    def kernel(near_ref, back_ref, both_ref, first_ref, second_ref, keep, one, three):
        def term(i):
            return plus(near_ref[i * T : (i + 1) * T, :], back_ref[i * T : (i + 1) * T, :])

        keep[:T, :] = term(0)
        keep[T:rows, :] = term(1)
        keep[rows:, :] = both_ref[...].astype(F32)
        one[:T, :] = plus(term(2), first_ref[:T, :]).astype(BF16)
        one[T:rows, :] = term(3).astype(BF16)
        one[rows:, :] = plus(both_ref[...], first_ref[T:, :]).astype(BF16)
        three[:T, :] = term(4).astype(BF16)
        three[T:rows, :] = plus(term(5), second_ref[...]).astype(BF16)
        three[rows:, :] = both_ref[...]

    shapes = [jax.ShapeDtypeStruct((rows + EXTRA, width), t) for t in (F32, BF16, BF16)]
    return simple_call(kernel, "add_near", shapes, near, back, both, first, second)


def add_rows(*parts):
    width = parts[0].shape[1]

    def kernel(*refs):
        ins, (keep, send) = refs[:-2], refs[-2:]
        loss = plus(*(r[NZ * T :, :] for r in ins))
        keep[:T, :] = plus(*(r[:T, :] for r in ins))
        keep[T:, :] = loss
        send[:T, :] = plus(*(r[T : NZ * T, :] for r in ins)).astype(BF16)
        send[T:, :] = loss.astype(BF16)

    shapes = [jax.ShapeDtypeStruct((T + EXTRA, width), F32), jax.ShapeDtypeStruct((T + EXTRA, width), BF16)]
    return simple_call(kernel, "add_rows", shapes, *parts)


def add_halves(one, three, first, second):
    half = one.shape[0] // NZ

    def kernel(one_ref, three_ref, first_ref, second_ref, out1, out3):
        out1[:half, :] = (one_ref[:half, :].astype(F32) + first_ref[...].astype(F32)).astype(BF16)
        out1[half:, :] = one_ref[half:, :]
        out3[:half, :] = three_ref[:half, :]
        out3[half:, :] = (three_ref[half:, :].astype(F32) + second_ref[...].astype(F32)).astype(BF16)

    shapes = [jax.ShapeDtypeStruct(one.shape, BF16)] * 2
    return simple_call(kernel, "add_halves", shapes, one, three, first, second)


def add_users(parts):
    width = parts[0].shape[0] // NZ

    def kernel(*refs):
        ins, (keep, send) = refs[:-2], refs[-2:]
        keep[...] = sum(r[:width, :].astype(F32) for r in ins)
        send[...] = sum(r[width:, :].astype(F32) for r in ins).astype(BF16)

    shapes = [jax.ShapeDtypeStruct((width, T), F32), jax.ShapeDtypeStruct((width, T), BF16)]
    return simple_call(kernel, "add_users", shapes, *parts)


def finish(keep_u, received_u, keep, received):
    def kernel(keep_u_ref, received_u_ref, keep_ref, received_ref, grad_u, grad, loss):
        grad_u[...] = plus(keep_u_ref[...], received_u_ref[...]).T
        grad[...] = plus(keep_ref[:T, :], received_ref[:T, :])
        loss[...] = jnp.sum(plus(keep_ref[T : T + 1, :], received_ref[T : T + 1, :]), axis=1, keepdims=True)

    shapes = [(T, keep_u.shape[0]), (T, keep.shape[1]), (1, 1)]
    shapes = [jax.ShapeDtypeStruct(x, F32) for x in shapes]
    return simple_call(kernel, "finish", shapes, keep_u, received_u, keep, received)


def join_stats(own, other):
    half = own.shape[0] // 2

    def kernel(own_ref, other_ref, out_ref):
        a, b = own_ref[:half, :], other_ref[:half, :]
        top = jnp.maximum(a, b)
        out_ref[:half, :] = top + jnp.log2(jnp.exp2(a - top) + jnp.exp2(b - top))
        out_ref[half:, :] = own_ref[half:, :] + other_ref[half:, :]

    return simple_call(kernel, "join_stats", [jax.ShapeDtypeStruct(own.shape, F32)], own, other)[0]


def move(x, axis, target):
    return lax.ppermute(x, axis, [(i, target(i)) for i in range(lax.axis_size(axis))])


def shift_x(x, j):
    return move(x, "aa", lambda i: (i + j * NZ) % (NX * NZ))


def swap_z_hi(x):
    return move(x, "aa", lambda i: i ^ 1)


def shift_y(x, k):
    return move(x, "au", lambda i: i // 8 * 8 + (i % 8 + k * NC) % 8)


def swap_core(x):
    return move(x, "au", lambda i: i ^ 1)


def swap_z_lo(x):
    return move(x, "au", lambda i: i ^ 8)


def local(users, ads, counts, positives, weights):
    inv = users.shape[1] ** (-0.5)
    pos_row = (positives - lax.axis_index("aa") * counts.shape[0])[None, :]
    logc = (jnp.log(counts.astype(F32)) * LOG2E)[None, :]
    weight_row = weights[None, :]
    users_z, ads_z, pos_row, logc = lax.optimization_barrier((swap_z_hi(users), swap_z_lo(ads), pos_row, logc))
    user_pair = jnp.concatenate([users, users_z], axis=0)
    ads_pair = jnp.concatenate([ads, ads_z], axis=0)
    user_pair, ads_pair = lax.optimization_barrier((user_pair, ads_pair))
    user_2 = shift_x(user_pair, 2)
    user_1, user_3 = shift_x(user_pair, 1), shift_x(user_pair, -1)
    ads_1, ads_3 = shift_y(ads_pair, 1), shift_y(ads_pair, -1)
    ads_2 = shift_y(ads_pair, 2)
    parts = lax.optimization_barrier((user_pair, user_1, user_2, user_3))

    p_near, top_near, at_near, acc, m, total, hits, staged, users_t = run_logits(
        "near", parts, (ads_pair, ads_1, ads_3), logc, pos_row, inv
    )
    ads_2, ads_1, ads_3, hits = lax.optimization_barrier((ads_2, ads_1, ads_3, hits))
    far = swap_core(jnp.concatenate([ads_pair, ads_1, ads_3, ads_2], axis=0))
    p_two, top_two, at_two, acc, m, total, hits = run_logits(
        "two", (users_t,), (ads_2,), logc, pos_row, inv, (acc, m, total, hits)
    )
    p_far, top_far, at_far, acc, m, total, hits, stats = run_logits(
        "far", (users_t,), (far,), logc, pos_row, inv, (acc, m, total, hits)
    )
    half = stats.shape[0] * LANES // 4
    ads_t = (at_near, at_two, at_far)
    stats_z, rows_a = lax.optimization_barrier((swap_z_hi(stats), run_rows(ads_t, pos_row, 0, half)))
    stats = join_stats(stats, stats_z)
    moved = tuple(shift_x(stats, j) for j in range(1, NX))
    moved, rows_b = lax.optimization_barrier((moved, run_rows(ads_t, pos_row, half, half)))
    du_0, du_1, du_3, du_2a, du_2b, lse, coefs, loss = run_users(
        acc, m, rows_a, rows_b, hits, weight_row, (stats, *moved), inv
    )
    tail = (lse, coefs, weight_row, pos_row, loss)
    du_2a, du_2b = shift_x(du_2a, 1), shift_x(du_2b, -1)
    pay_2, da_2 = run_grads("mid", [("far", 3, p_far, top_far), ("two", 0, p_two, top_two)], staged, *tail)
    back_2 = swap_core(pay_2)
    da_2, staged = lax.optimization_barrier((da_2, staged))
    (da_far,) = run_grads("far", [("far", i, p_far, top_far) for i in range(3)], staged, *tail)
    da_far, back_2, du_2a, du_2b = lax.optimization_barrier((da_far, back_2, du_2a, du_2b))
    du_1, du_3 = add_halves(du_1, du_3, du_2a, du_2b)
    back = swap_core(da_far)
    first, second, both = add_mid(da_2, back_2)
    first, second, du_1, du_3, staged = lax.optimization_barrier((first, second, du_1, du_3, staged))
    first, second = shift_y(first, -1), shift_y(second, 1)
    du_1, du_3 = shift_x(du_1, 1), shift_x(du_3, -1)
    (da_near,) = run_grads("near", [("near", i, p_near, top_near) for i in range(3)], staged, *tail)
    da_near, first, second, du_1, du_3 = lax.optimization_barrier((da_near, first, second, du_1, du_3))
    kept, one, three = add_near(da_near, back, both, first, second)
    one, three = shift_y(one, -1), shift_y(three, 1)
    keep_u, send_u = add_users((du_0, du_1, du_3))
    one, three, received_u = lax.optimization_barrier((one, three, swap_z_hi(send_u)))
    keep, send = add_rows(kept, one, three)
    grad_users, grad_ads, loss = finish(keep_u, received_u, keep, swap_z_lo(send))
    return grad_users, grad_ads, loss.reshape(())


def solution(mesh):
    return jax.shard_map(
        local,
        mesh=mesh,
        in_specs=(P(("au", "aa"), None), P(("aa", "au"), None), P("aa"), P("au"), P("au")),
        out_specs=(P(("au", "aa"), None), P(("aa", "au"), None), P()),
        check_vma=False,
    )
```

```python
import jax
import jax.numpy as jnp
from jax import lax
from jax.experimental import pallas as pl
from jax.experimental.pallas import tpu as pltpu
from jax.sharding import PartitionSpec as P

F32 = jnp.float32
BF16 = jnp.bfloat16
T = 256
LANES = 128
EXTRA = 16
LOG2E = 1.4426950408889634
LN2 = 0.6931471805599453
NX, NZ, NY, NC = 4, 2, 4, 2
VMEM_LIMIT = 24 * 2**20


def params():
    return pltpu.CompilerParams(vmem_limit_bytes=VMEM_LIMIT)


def call(kernel, name, out_shape, scratch, args, estimate=None):
    vmem = pl.BlockSpec(memory_space=pltpu.VMEM)
    return pl.pallas_call(
        kernel,
        in_specs=[vmem] * len(args),
        out_specs=[vmem] * len(out_shape),
        out_shape=out_shape,
        scratch_shapes=scratch,
        compiler_params=params(),
        cost_estimate=estimate,
        name=name,
    )(*args)


def user_block(j, zr):
    me = lax.axis_index("aa")
    x, z = me // NZ, me % NZ
    return lax.rem(x + NX - j, NX) * NZ + (z + zr - 2 * z * zr)


def ads_block(group, chunk):
    pair, zr = chunk // NZ, chunk % NZ
    k, cr = {"near": (pair ^ (pair >> 1), 0), "far": (pair ^ (pair >> 1), 1), "two": (2, 0)}[group]
    me = lax.axis_index("au")
    z, y, c = me // (NY * NC), (me // NC) % NY, me % NC
    return (z + zr - 2 * z * zr) * (NY * NC) + lax.rem(y + NY - k, NY) * NC + (c + cr - 2 * c * cr)


def stage_users(user_refs, staged, inv):
    for j in range(NX):
        for zr in range(NZ):
            spot = pl.multiple_of(user_block(j, zr) * T, T)
            block = user_refs[j][zr * T : (zr + 1) * T, :].astype(F32) * inv
            staged[pl.ds(spot, T), :] = block.astype(BF16)


def first_row(group, chunk):
    return pl.multiple_of(ads_block(group, chunk) * T, T)


def split(value):
    high = value.astype(BF16).astype(F32)
    mid = (value - high).astype(BF16).astype(F32)
    return high, mid, value - high - mid


def loss_rows(loss, width):
    high, mid, low = split(loss)
    lane = lax.broadcasted_iota(jnp.int32, (EXTRA, width), 1) - 3 * lax.axis_index("au")
    return jnp.where(lane == 0, high, jnp.where(lane == 1, mid, jnp.where(lane == 2, low, 0.0))).astype(BF16)


def plus(*values):
    return sum(v.astype(F32) for v in values)


def logits_kernel(group, n_ads, rows, inv, *refs):
    n = NX * NZ
    chunks = rows // T
    first_call = group == "near"
    last_call = group == "far"
    if first_call:
        user_refs, refs = refs[:NX], refs[NX:]
    else:
        (users_t,), refs = refs[:1], refs[1:]
    ads_refs, refs = refs[:n_ads], refs[n_ads:]
    (logc_ref, pos_ref), refs = refs[:2], refs[2:]
    if not first_call:
        (acc_in, m_in, total_in, hit_in), refs = refs[:4], refs[4:]
    (p_ref, top_ref, ads_t, acc_ref, m_ref, total_ref, hit_ref), refs = refs[:7], refs[7:]
    if first_call:
        (staged, users_t), refs = refs[:2], refs[2:]
    if last_call:
        (stats_ref,), refs = refs[:1], refs[1:]
    ads_all, logc_all, s0, s1, *late = refs

    if first_call:
        stage_users(user_refs, staged, inv)
        for b in range(n):
            users_t[:, b * T : (b + 1) * T] = staged[b * T : (b + 1) * T, :].T
    spot = 0
    for r in ads_refs:
        ads_all[spot : spot + r.shape[0], :] = r[...]
        spot += r.shape[0]
    for c in range(chunks):
        part = slice(c * T, (c + 1) * T)
        ads_t[:, part] = ads_all[part, :].T
        logc = logc_ref[:, pl.ds(first_row(group, c), T)]
        logc_all[part, :] = jnp.broadcast_to(logc, (LANES, T)).T

    def columns(tile):
        return slice(tile * T, (tile + 1) * T)

    class Product:
        def __init__(self, tile, dst):
            self.cols, self.dst = columns(tile), dst
            self.side = users_t[:, self.cols]
            self.pos = pos_ref[:, self.cols] - lax.broadcasted_iota(jnp.int32, (8, T), 0)
            self.best = jnp.full((8, T), -jnp.inf, F32)
            self.found = jnp.zeros((8, T), F32)

        def chunk(self, c):
            ahead = self.pos - first_row(group, c)
            prod = jnp.dot(ads_all[c * T : (c + 1) * T, :], self.side, preferred_element_type=F32)
            for r in range(0, T, 8):
                row = c * T + r
                logc = logc_all[row : row + 8, :]
                x = prod[r : r + 8, :] * LOG2E - jnp.concatenate([logc] * (T // LANES), axis=1)
                self.dst[row : row + 8, :] = x
                self.best = jnp.maximum(self.best, x)
                self.found = jnp.where(ahead == r, x, self.found)

        def end(self):
            top_ref[:, self.cols] = jnp.max(self.best, axis=0, keepdims=True)
            hit = jnp.sum(self.found, axis=0, keepdims=True)
            hit_ref[:, self.cols] = hit if first_call else hit + hit_in[:, self.cols]

    class Exps:
        def __init__(self, tile, src, extra):
            self.cols, self.src, self.extra = columns(tile), src, extra
            self.top = top_ref[:, self.cols]
            self.total = jnp.zeros((8, T), F32)

        def chunk(self, c):
            for r in range(c * T, (c + 1) * T, 16):
                e = jnp.exp2(self.src[r : r + 16, :] - self.top)
                self.total += e[:8] + e[8:]
                e = e.astype(BF16)
                p_ref[r : r + 16, self.cols] = e
                self.extra[r : r + 16, :] = e

        def end(self):
            cols, top = self.cols, self.top
            total = jnp.sum(self.total, axis=0, keepdims=True)
            if first_call:
                m_ref[:, cols] = top
                total_ref[:, cols] = total
            else:
                m = jnp.maximum(m_in[:, cols], top)
                m_ref[:, cols] = m
                total_ref[:, cols] = total_in[:, cols] * jnp.exp2(m_in[:, cols] - m) + total * jnp.exp2(top - m)

    def gather(tile, e):
        cols = columns(tile)
        new = jnp.dot(ads_t[...], e[...], preferred_element_type=F32)
        if first_call:
            acc_ref[:, cols] = new
        else:
            m = m_ref[:, cols]
            acc_ref[:, cols] = acc_in[:, cols] * jnp.exp2(m_in[:, cols] - m) + new * jnp.exp2(top_ref[:, cols] - m)

    def turn(tile, src, dst, e_now, e_before):
        if tile:
            gather(tile - 1, e_before)
        product = Product(tile + 1, dst) if tile + 1 < n else None
        exps = Exps(tile, src, e_now)
        for c in range(chunks):
            if product:
                product.chunk(c)
            exps.chunk(c)
        if product:
            product.end()
        exps.end()

    opening = Product(0, s0)
    for c in range(chunks):
        opening.chunk(c)
    opening.end()
    for tile in range(n):
        if tile % 2:
            turn(tile, s1, s0, late[1], late[0])
        else:
            turn(tile, s0, s1, late[0], late[1])
    gather(n - 1, late[(n - 1) % 2])
    if last_call:
        lse = m_ref[...] + jnp.log2(total_ref[...])
        width = n * T // LANES
        for r in range(width):
            cols = slice(r * LANES, (r + 1) * LANES)
            stats_ref[r : r + 1, :] = lse[:, cols]
            stats_ref[width + r : width + r + 1, :] = hit_ref[:, cols]


def cost(rows, total, width):
    return pl.CostEstimate(flops=rows * total * width // 8, bytes_accessed=rows * total // 8, transcendentals=0)


def run_logits(group, users, ads, logc, positives, inv, before=()):
    width = ads[0].shape[1]
    count = sum(x.shape[0] for x in ads)
    total = NX * NZ * T
    stats_rows = 2 * total // LANES
    row = jax.ShapeDtypeStruct((1, total), F32)
    out_shape = [
        jax.ShapeDtypeStruct((count, total), BF16),
        row,
        jax.ShapeDtypeStruct((width, count), BF16),
        jax.ShapeDtypeStruct((width, total), F32),
        row,
        row,
        row,
    ]
    if group == "near":
        out_shape.append(jax.ShapeDtypeStruct((total, width), BF16))
        out_shape.append(jax.ShapeDtypeStruct((width, total), BF16))
    if group == "far":
        out_shape.append(jax.ShapeDtypeStruct((stats_rows, LANES), F32))
    scratch = [
        pltpu.VMEM((count, width), BF16),
        pltpu.VMEM((count, LANES), F32),
        pltpu.VMEM((count, T), F32),
        pltpu.VMEM((count, T), F32),
        pltpu.VMEM((count, T), BF16),
        pltpu.VMEM((count, T), BF16),
    ]
    return call(
        lambda *refs: logits_kernel(group, len(ads), count, inv, *refs),
        "logits_" + group,
        out_shape,
        scratch,
        (*users, *ads, logc, positives, *before),
        cost(count, total, width),
    )


GROUPS = ("near", "two", "far")


def rows_kernel(sizes, start, *refs):
    ads_refs, (pos_ref, out_ref, h0, h1) = refs[: len(sizes)], refs[len(sizes) :]
    tiles = out_ref.shape[1] // T

    def build(tile, dst):
        cols = slice(start + tile * T, start + (tile + 1) * T)
        pos = pos_ref[:, cols] - lax.broadcasted_iota(jnp.int32, (16, T), 0)
        spot = 0
        for group, size in zip(GROUPS, sizes):
            for c in range(size // T):
                ahead = pos - first_row(group, c)
                for r in range(0, T, 16):
                    dst[spot + r : spot + r + 16, :] = jnp.where(ahead == r, 1.0, 0.0).astype(BF16)
                spot += T

    def product(tile, src):
        cols = slice(tile * T, (tile + 1) * T)
        out = jnp.zeros((out_ref.shape[0], T), F32)
        spot = 0
        for ads, size in zip(ads_refs, sizes):
            out += jnp.dot(ads[...], src[spot : spot + size, :], preferred_element_type=F32)
            spot += size
        out_ref[:, cols] = out.astype(BF16)

    build(0, h0)
    for tile in range(tiles):
        now, then = (h1, h0) if tile % 2 else (h0, h1)
        product(tile, now)
        if tile + 1 < tiles:
            build(tile + 1, then)


def run_rows(ads_t, positives, start, total):
    width = ads_t[0].shape[0]
    sizes = [x.shape[1] for x in ads_t]
    return call(
        lambda *refs: rows_kernel(sizes, start, *refs),
        "positive_rows",
        [jax.ShapeDtypeStruct((width, total), BF16)],
        [pltpu.VMEM((sum(sizes), T), BF16)] * 2,
        (*ads_t, positives),
        cost(sum(sizes), total, width),
    )[0]


def users_kernel(inv, acc_ref, m_ref, rows_a, rows_b, hit_ref, weight_ref, *rest):
    stats_in, rest = rest[:NX], rest[NX:]
    du_refs, (lse_ref, coef_ref, loss_ref, stats_ref, rows_ref) = rest[:-5], rest[-5:]
    n = NX * NZ
    width = n * T // LANES
    for j in range(NX):
        stats_ref[pl.ds(lax.rem(lax.axis_index("aa") // NZ + NX - j, NX), 1)] = stats_in[j][...][None]
    rows_ref[:, : n * T // 2] = rows_a[...]
    rows_ref[:, n * T // 2 :] = rows_b[...]
    tops = stats_ref[:, :width, :]
    top = jnp.max(tops, axis=0)
    lse = top + jnp.log2(jnp.sum(jnp.exp2(tops - top[None]), axis=0))
    diff = (lse - jnp.sum(stats_ref[:, width:, :], axis=0)) * LN2
    loss = jnp.zeros((1, LANES), F32)
    for r in range(width):
        cols = slice(r * LANES, (r + 1) * LANES)
        lse_ref[:, cols] = lse[r : r + 1, :]
        loss += weight_ref[:, cols] * diff[r : r + 1, :]
    loss_ref[...] = loss_rows(jnp.sum(loss, axis=1, keepdims=True), loss_ref.shape[1])
    coef_ref[...] = weight_ref[...] * (jnp.exp2(hit_ref[...] - lse_ref[...]) - 1.0)

    def users_at(j, zr):
        cols = pl.ds(pl.multiple_of(user_block((NX - j) % NX, zr) * T, T), T)
        weight = weight_ref[:, cols] * inv
        scale = weight * jnp.exp2(m_ref[:, cols] - lse_ref[:, cols])
        return (acc_ref[:, cols] * scale - rows_ref[:, cols].astype(F32) * weight).astype(BF16)

    for part, j in enumerate((0, 1, 3)):
        for zr in range(NZ):
            du_refs[part][zr * T : (zr + 1) * T, :] = users_at(j, zr)
    du_refs[3][...] = users_at(2, 0)
    du_refs[4][...] = users_at(2, 1)


def run_users(acc, m, rows_a, rows_b, hits, weights, stats, inv):
    width, total = acc.shape
    row = jax.ShapeDtypeStruct((1, total), F32)
    shapes = [(NZ * width, T)] * 3 + [(width, T)] * 2
    out_shape = [jax.ShapeDtypeStruct(x, BF16) for x in shapes]
    out_shape += [row, row, jax.ShapeDtypeStruct((EXTRA, width), BF16)]
    return call(
        lambda *refs: users_kernel(inv, *refs),
        "grad_users",
        out_shape,
        [pltpu.VMEM((NX, *stats[0].shape), F32), pltpu.VMEM((width, total), BF16)],
        (acc, m, rows_a, rows_b, hits, weights, *stats),
    )


def grads_kernel(units, users_ref, lse_ref, coef_ref, weight_ref, pos_ref, loss_in, *refs):
    ps, tops, outs, qs = refs[: len(units)], refs[len(units) : 2 * len(units)], refs[2 * len(units) : -2], refs[-2:]
    deep = 2 * T
    total = users_ref.shape[0]

    def build(i, dst):
        group, at = units[i]
        for b in range(total // T):
            cols = slice(b * T, (b + 1) * T)
            scale = weight_ref[:, cols] * jnp.exp2(tops[i][:, cols] - lse_ref[:, cols])
            coef = coef_ref[:, cols]
            pos = pos_ref[:, cols] - lax.broadcasted_iota(jnp.int32, (16, T), 0)
            for half in range(2):
                ahead = pos - first_row(group, 2 * at + half)
                for r in range(0, T, 16):
                    row = half * T + r
                    scaled = ps[i][at * deep + row : at * deep + row + 16, cols].astype(F32) * scale
                    dst[row : row + 16, cols] = jnp.where(ahead == r, coef, scaled).astype(BF16)

    build(0, qs[0])
    for i in range(len(units)):
        da = jnp.dot(qs[i % 2][...], users_ref[...], preferred_element_type=F32)
        if i + 1 < len(units):
            build(i + 1, qs[(i + 1) % 2])
        da = da.astype(BF16)
        if len(outs) == 1:
            outs[0][i * deep : (i + 1) * deep, :] = da
        else:
            outs[i][:deep, :] = da
            outs[i][deep:, :] = loss_in[...]


def run_grads(name, units, users, lse, coefs, weights, positives, loss):
    total, width = users.shape
    deep = 2 * T
    places = [u[:2] for u in units]
    if name == "mid":
        shapes = [(deep + EXTRA, width)] * 2
    else:
        shapes = [(len(units) * deep, width)]
    return call(
        lambda *refs: grads_kernel(places, *refs),
        "grads_" + name,
        [jax.ShapeDtypeStruct(x, BF16) for x in shapes],
        [pltpu.VMEM((deep, total), BF16)] * 2,
        (users, lse, coefs, weights, positives, loss, *(u[2] for u in units), *(u[3] for u in units)),
        cost(len(units) * deep, total, width),
    )


def simple_call(kernel, name, out_shape, *args):
    return call(kernel, name, out_shape, [], args)


def add_mid(near, back):
    width = near.shape[1]

    def kernel(near_ref, back_ref, first, second, both):
        total = plus(near_ref[...], back_ref[...]).astype(BF16)
        first[:T, :] = total[:T, :]
        first[T:, :] = total[NZ * T :, :]
        second[...] = total[T : NZ * T, :]
        both[...] = total[NZ * T :, :]

    shapes = [(T + EXTRA, width), (T, width), (EXTRA, width)]
    return simple_call(kernel, "add_mid", [jax.ShapeDtypeStruct(x, BF16) for x in shapes], near, back)


def add_near(near, back, both, first, second):
    width = near.shape[1]
    rows = NZ * T

    def kernel(near_ref, back_ref, both_ref, first_ref, second_ref, keep, one, three):
        def term(i):
            return plus(near_ref[i * T : (i + 1) * T, :], back_ref[i * T : (i + 1) * T, :])

        keep[:T, :] = term(0)
        keep[T:rows, :] = term(1)
        keep[rows:, :] = both_ref[...].astype(F32)
        one[:T, :] = plus(term(2), first_ref[:T, :]).astype(BF16)
        one[T:rows, :] = term(3).astype(BF16)
        one[rows:, :] = plus(both_ref[...], first_ref[T:, :]).astype(BF16)
        three[:T, :] = term(4).astype(BF16)
        three[T:rows, :] = plus(term(5), second_ref[...]).astype(BF16)
        three[rows:, :] = both_ref[...]

    shapes = [jax.ShapeDtypeStruct((rows + EXTRA, width), t) for t in (F32, BF16, BF16)]
    return simple_call(kernel, "add_near", shapes, near, back, both, first, second)


def add_rows(*parts):
    width = parts[0].shape[1]

    def kernel(*refs):
        ins, (keep, send) = refs[:-2], refs[-2:]
        loss = plus(*(r[NZ * T :, :] for r in ins))
        keep[:T, :] = plus(*(r[:T, :] for r in ins))
        keep[T:, :] = loss
        send[:T, :] = plus(*(r[T : NZ * T, :] for r in ins)).astype(BF16)
        send[T:, :] = loss.astype(BF16)

    shapes = [jax.ShapeDtypeStruct((T + EXTRA, width), F32), jax.ShapeDtypeStruct((T + EXTRA, width), BF16)]
    return simple_call(kernel, "add_rows", shapes, *parts)


def add_halves(one, three, first, second):
    half = one.shape[0] // NZ

    def kernel(one_ref, three_ref, first_ref, second_ref, out1, out3):
        out1[:half, :] = (one_ref[:half, :].astype(F32) + first_ref[...].astype(F32)).astype(BF16)
        out1[half:, :] = one_ref[half:, :]
        out3[:half, :] = three_ref[:half, :]
        out3[half:, :] = (three_ref[half:, :].astype(F32) + second_ref[...].astype(F32)).astype(BF16)

    shapes = [jax.ShapeDtypeStruct(one.shape, BF16)] * 2
    return simple_call(kernel, "add_halves", shapes, one, three, first, second)


def add_users(parts):
    width = parts[0].shape[0] // NZ

    def kernel(*refs):
        ins, (keep, send) = refs[:-2], refs[-2:]
        keep[...] = sum(r[:width, :].astype(F32) for r in ins)
        send[...] = sum(r[width:, :].astype(F32) for r in ins).astype(BF16)

    shapes = [jax.ShapeDtypeStruct((width, T), F32), jax.ShapeDtypeStruct((width, T), BF16)]
    return simple_call(kernel, "add_users", shapes, *parts)


def finish(keep_u, received_u, keep, received):
    def kernel(keep_u_ref, received_u_ref, keep_ref, received_ref, grad_u, grad, loss):
        grad_u[...] = plus(keep_u_ref[...], received_u_ref[...]).T
        grad[...] = plus(keep_ref[:T, :], received_ref[:T, :])
        loss[...] = jnp.sum(plus(keep_ref[T : T + 1, :], received_ref[T : T + 1, :]), axis=1, keepdims=True)

    shapes = [(T, keep_u.shape[0]), (T, keep.shape[1]), (1, 1)]
    shapes = [jax.ShapeDtypeStruct(x, F32) for x in shapes]
    return simple_call(kernel, "finish", shapes, keep_u, received_u, keep, received)


def join_stats(own, other):
    half = own.shape[0] // 2

    def kernel(own_ref, other_ref, out_ref):
        a, b = own_ref[:half, :], other_ref[:half, :]
        top = jnp.maximum(a, b)
        out_ref[:half, :] = top + jnp.log2(jnp.exp2(a - top) + jnp.exp2(b - top))
        out_ref[half:, :] = own_ref[half:, :] + other_ref[half:, :]

    return simple_call(kernel, "join_stats", [jax.ShapeDtypeStruct(own.shape, F32)], own, other)[0]


def move(x, axis, target):
    return lax.ppermute(x, axis, [(i, target(i)) for i in range(lax.axis_size(axis))])


def shift_x(x, j):
    return move(x, "aa", lambda i: (i + j * NZ) % (NX * NZ))


def swap_z_hi(x):
    return move(x, "aa", lambda i: i ^ 1)


def shift_y(x, k):
    return move(x, "au", lambda i: i // 8 * 8 + (i % 8 + k * NC) % 8)


def swap_core(x):
    return move(x, "au", lambda i: i ^ 1)


def swap_z_lo(x):
    return move(x, "au", lambda i: i ^ 8)


def local(users, ads, counts, positives, weights):
    inv = users.shape[1] ** (-0.5)
    pos_row = (positives - lax.axis_index("aa") * counts.shape[0])[None, :]
    logc = (jnp.log(counts.astype(F32)) * LOG2E)[None, :]
    weight_row = weights[None, :]
    users_z, ads_z, pos_row, logc = lax.optimization_barrier((swap_z_hi(users), swap_z_lo(ads), pos_row, logc))
    user_pair = jnp.concatenate([users, users_z], axis=0)
    ads_pair = jnp.concatenate([ads, ads_z], axis=0)
    user_pair, ads_pair = lax.optimization_barrier((user_pair, ads_pair))
    user_2 = shift_x(user_pair, 2)
    user_1, user_3 = shift_x(user_pair, 1), shift_x(user_pair, -1)
    ads_1, ads_3 = shift_y(ads_pair, 1), shift_y(ads_pair, -1)
    ads_2 = shift_y(ads_pair, 2)
    parts = lax.optimization_barrier((user_pair, user_1, user_2, user_3))

    p_near, top_near, at_near, acc, m, total, hits, staged, users_t = run_logits(
        "near", parts, (ads_pair, ads_1, ads_3), logc, pos_row, inv
    )
    ads_2, ads_1, ads_3, hits = lax.optimization_barrier((ads_2, ads_1, ads_3, hits))
    far = swap_core(jnp.concatenate([ads_pair, ads_1, ads_3, ads_2], axis=0))
    p_two, top_two, at_two, acc, m, total, hits = run_logits(
        "two", (users_t,), (ads_2,), logc, pos_row, inv, (acc, m, total, hits)
    )
    p_far, top_far, at_far, acc, m, total, hits, stats = run_logits(
        "far", (users_t,), (far,), logc, pos_row, inv, (acc, m, total, hits)
    )
    half = stats.shape[0] * LANES // 4
    ads_t = (at_near, at_two, at_far)
    stats_z, rows_a = lax.optimization_barrier((swap_z_hi(stats), run_rows(ads_t, pos_row, 0, half)))
    stats = join_stats(stats, stats_z)
    moved = tuple(shift_x(stats, j) for j in range(1, NX))
    moved, rows_b = lax.optimization_barrier((moved, run_rows(ads_t, pos_row, half, half)))
    du_0, du_1, du_3, du_2a, du_2b, lse, coefs, loss = run_users(
        acc, m, rows_a, rows_b, hits, weight_row, (stats, *moved), inv
    )
    tail = (lse, coefs, weight_row, pos_row, loss)
    du_2a, du_2b = shift_x(du_2a, 1), shift_x(du_2b, -1)
    pay_2, da_2 = run_grads("mid", [("far", 3, p_far, top_far), ("two", 0, p_two, top_two)], staged, *tail)
    back_2 = swap_core(pay_2)
    da_2, staged = lax.optimization_barrier((da_2, staged))
    (da_far,) = run_grads("far", [("far", i, p_far, top_far) for i in range(3)], staged, *tail)
    da_far, back_2, du_2a, du_2b = lax.optimization_barrier((da_far, back_2, du_2a, du_2b))
    du_1, du_3 = add_halves(du_1, du_3, du_2a, du_2b)
    back = swap_core(da_far)
    first, second, both = add_mid(da_2, back_2)
    first, second, du_1, du_3, staged = lax.optimization_barrier((first, second, du_1, du_3, staged))
    first, second = shift_y(first, -1), shift_y(second, 1)
    du_1, du_3 = shift_x(du_1, 1), shift_x(du_3, -1)
    (da_near,) = run_grads("near", [("near", i, p_near, top_near) for i in range(3)], staged, *tail)
    da_near, first, second, du_1, du_3 = lax.optimization_barrier((da_near, first, second, du_1, du_3))
    kept, one, three = add_near(da_near, back, both, first, second)
    one, three = shift_y(one, -1), shift_y(three, 1)
    keep_u, send_u = add_users((du_0, du_1, du_3))
    one, three, received_u = lax.optimization_barrier((one, three, swap_z_hi(send_u)))
    keep, send = add_rows(kept, one, three)
    grad_users, grad_ads, loss = finish(keep_u, received_u, keep, swap_z_lo(send))
    return grad_users, grad_ads, loss.reshape(())


def solution(mesh):
    return jax.shard_map(
        local,
        mesh=mesh,
        in_specs=(P(("au", "aa"), None), P(("aa", "au"), None), P("aa"), P("au"), P("au")),
        out_specs=(P(("au", "aa"), None), P(("aa", "au"), None), P()),
        check_vma=False,
    )
```

```python
import jax
import jax.numpy as jnp
from jax import lax
from jax.experimental import pallas as pl
from jax.experimental.pallas import tpu as pltpu
from jax.sharding import PartitionSpec as P

F32 = jnp.float32
BF16 = jnp.bfloat16
T = 256
LANES = 128
EXTRA = 16
LOG2E = 1.4426950408889634
LN2 = 0.6931471805599453
NX, NZ, NY, NC = 4, 2, 4, 2
VMEM_LIMIT = 24 * 2**20


def params():
    return pltpu.CompilerParams(vmem_limit_bytes=VMEM_LIMIT)


def call(kernel, name, out_shape, scratch, args, estimate=None):
    vmem = pl.BlockSpec(memory_space=pltpu.VMEM)
    return pl.pallas_call(
        kernel,
        in_specs=[vmem] * len(args),
        out_specs=[vmem] * len(out_shape),
        out_shape=out_shape,
        scratch_shapes=scratch,
        compiler_params=params(),
        cost_estimate=estimate,
        name=name,
    )(*args)


def user_block(j, zr):
    me = lax.axis_index("aa")
    x, z = me // NZ, me % NZ
    return lax.rem(x + NX - j, NX) * NZ + (z + zr - 2 * z * zr)


def ads_block(group, chunk):
    pair, zr = chunk // NZ, chunk % NZ
    k, cr = {"near": (pair ^ (pair >> 1), 0), "far": (pair ^ (pair >> 1), 1), "two": (2, 0)}[group]
    me = lax.axis_index("au")
    z, y, c = me // (NY * NC), (me // NC) % NY, me % NC
    return (z + zr - 2 * z * zr) * (NY * NC) + lax.rem(y + NY - k, NY) * NC + (c + cr - 2 * c * cr)


def stage_users(user_refs, staged, inv):
    for j in range(NX):
        for zr in range(NZ):
            spot = pl.multiple_of(user_block(j, zr) * T, T)
            block = user_refs[j][zr * T : (zr + 1) * T, :].astype(F32) * inv
            staged[pl.ds(spot, T), :] = block.astype(BF16)


def first_row(group, chunk):
    return pl.multiple_of(ads_block(group, chunk) * T, T)


def split(value):
    high = value.astype(BF16).astype(F32)
    mid = (value - high).astype(BF16).astype(F32)
    return high, mid, value - high - mid


def loss_rows(loss, width):
    high, mid, low = split(loss)
    lane = lax.broadcasted_iota(jnp.int32, (EXTRA, width), 1) - 3 * lax.axis_index("au")
    return jnp.where(lane == 0, high, jnp.where(lane == 1, mid, jnp.where(lane == 2, low, 0.0))).astype(BF16)


def plus(*values):
    return sum(v.astype(F32) for v in values)


def logits_kernel(group, n_ads, rows, inv, *refs):
    n = NX * NZ
    chunks = rows // T
    first_call = group == "near"
    last_call = group == "far"
    if first_call:
        user_refs, refs = refs[:NX], refs[NX:]
    else:
        (users_t,), refs = refs[:1], refs[1:]
    ads_refs, refs = refs[:n_ads], refs[n_ads:]
    (logc_ref, pos_ref), refs = refs[:2], refs[2:]
    if not first_call:
        (acc_in, m_in, total_in, hit_in), refs = refs[:4], refs[4:]
    (p_ref, top_ref, ads_t, acc_ref, m_ref, total_ref, hit_ref), refs = refs[:7], refs[7:]
    if first_call:
        (staged, users_t), refs = refs[:2], refs[2:]
    if last_call:
        (stats_ref,), refs = refs[:1], refs[1:]
    ads_all, logc_all, s0, s1, *late = refs

    if first_call:
        stage_users(user_refs, staged, inv)
        for b in range(n):
            users_t[:, b * T : (b + 1) * T] = staged[b * T : (b + 1) * T, :].T
    spot = 0
    for r in ads_refs:
        ads_all[spot : spot + r.shape[0], :] = r[...]
        spot += r.shape[0]
    for c in range(chunks):
        part = slice(c * T, (c + 1) * T)
        ads_t[:, part] = ads_all[part, :].T
        logc = logc_ref[:, pl.ds(first_row(group, c), T)]
        logc_all[part, :] = jnp.broadcast_to(logc, (LANES, T)).T

    def columns(tile):
        return slice(tile * T, (tile + 1) * T)

    class Product:
        def __init__(self, tile, dst):
            self.cols, self.dst = columns(tile), dst
            self.side = users_t[:, self.cols]
            self.pos = pos_ref[:, self.cols] - lax.broadcasted_iota(jnp.int32, (8, T), 0)
            self.best = jnp.full((8, T), -jnp.inf, F32)
            self.found = jnp.zeros((8, T), F32)

        def chunk(self, c):
            ahead = self.pos - first_row(group, c)
            prod = jnp.dot(ads_all[c * T : (c + 1) * T, :], self.side, preferred_element_type=F32)
            for r in range(0, T, 8):
                row = c * T + r
                logc = logc_all[row : row + 8, :]
                x = prod[r : r + 8, :] * LOG2E - jnp.concatenate([logc] * (T // LANES), axis=1)
                self.dst[row : row + 8, :] = x
                self.best = jnp.maximum(self.best, x)
                self.found = jnp.where(ahead == r, x, self.found)

        def end(self):
            top_ref[:, self.cols] = jnp.max(self.best, axis=0, keepdims=True)
            hit = jnp.sum(self.found, axis=0, keepdims=True)
            hit_ref[:, self.cols] = hit if first_call else hit + hit_in[:, self.cols]

    class Exps:
        def __init__(self, tile, src, extra):
            self.cols, self.src, self.extra = columns(tile), src, extra
            self.top = top_ref[:, self.cols]
            self.total = jnp.zeros((8, T), F32)

        def chunk(self, c):
            for r in range(c * T, (c + 1) * T, 16):
                e = jnp.exp2(self.src[r : r + 16, :] - self.top)
                self.total += e[:8] + e[8:]
                e = e.astype(BF16)
                p_ref[r : r + 16, self.cols] = e
                self.extra[r : r + 16, :] = e

        def end(self):
            cols, top = self.cols, self.top
            total = jnp.sum(self.total, axis=0, keepdims=True)
            if first_call:
                m_ref[:, cols] = top
                total_ref[:, cols] = total
            else:
                m = jnp.maximum(m_in[:, cols], top)
                m_ref[:, cols] = m
                total_ref[:, cols] = total_in[:, cols] * jnp.exp2(m_in[:, cols] - m) + total * jnp.exp2(top - m)

    def gather(tile, e):
        cols = columns(tile)
        new = jnp.dot(ads_t[...], e[...], preferred_element_type=F32)
        if first_call:
            acc_ref[:, cols] = new
        else:
            m = m_ref[:, cols]
            acc_ref[:, cols] = acc_in[:, cols] * jnp.exp2(m_in[:, cols] - m) + new * jnp.exp2(top_ref[:, cols] - m)

    def turn(tile, src, dst, e_now, e_before):
        if tile:
            gather(tile - 1, e_before)
        product = Product(tile + 1, dst) if tile + 1 < n else None
        exps = Exps(tile, src, e_now)
        for c in range(chunks):
            if product:
                product.chunk(c)
            exps.chunk(c)
        if product:
            product.end()
        exps.end()

    opening = Product(0, s0)
    for c in range(chunks):
        opening.chunk(c)
    opening.end()
    for tile in range(n):
        if tile % 2:
            turn(tile, s1, s0, late[1], late[0])
        else:
            turn(tile, s0, s1, late[0], late[1])
    gather(n - 1, late[(n - 1) % 2])
    if last_call:
        lse = m_ref[...] + jnp.log2(total_ref[...])
        width = n * T // LANES
        for r in range(width):
            cols = slice(r * LANES, (r + 1) * LANES)
            stats_ref[r : r + 1, :] = lse[:, cols]
            stats_ref[width + r : width + r + 1, :] = hit_ref[:, cols]


def cost(rows, total, width):
    return pl.CostEstimate(flops=rows * total * width // 8, bytes_accessed=rows * total // 8, transcendentals=0)


def run_logits(group, users, ads, logc, positives, inv, before=()):
    width = ads[0].shape[1]
    count = sum(x.shape[0] for x in ads)
    total = NX * NZ * T
    stats_rows = 2 * total // LANES
    row = jax.ShapeDtypeStruct((1, total), F32)
    out_shape = [
        jax.ShapeDtypeStruct((count, total), BF16),
        row,
        jax.ShapeDtypeStruct((width, count), BF16),
        jax.ShapeDtypeStruct((width, total), F32),
        row,
        row,
        row,
    ]
    if group == "near":
        out_shape.append(jax.ShapeDtypeStruct((total, width), BF16))
        out_shape.append(jax.ShapeDtypeStruct((width, total), BF16))
    if group == "far":
        out_shape.append(jax.ShapeDtypeStruct((stats_rows, LANES), F32))
    scratch = [
        pltpu.VMEM((count, width), BF16),
        pltpu.VMEM((count, LANES), F32),
        pltpu.VMEM((count, T), F32),
        pltpu.VMEM((count, T), F32),
        pltpu.VMEM((count, T), BF16),
        pltpu.VMEM((count, T), BF16),
    ]
    return call(
        lambda *refs: logits_kernel(group, len(ads), count, inv, *refs),
        "logits_" + group,
        out_shape,
        scratch,
        (*users, *ads, logc, positives, *before),
        cost(count, total, width),
    )


GROUPS = ("near", "two", "far")


def rows_kernel(sizes, start, *refs):
    ads_refs, (pos_ref, out_ref, h0, h1) = refs[: len(sizes)], refs[len(sizes) :]
    tiles = out_ref.shape[1] // T

    def build(tile, dst):
        cols = slice(start + tile * T, start + (tile + 1) * T)
        pos = pos_ref[:, cols] - lax.broadcasted_iota(jnp.int32, (16, T), 0)
        spot = 0
        for group, size in zip(GROUPS, sizes):
            for c in range(size // T):
                ahead = pos - first_row(group, c)
                for r in range(0, T, 16):
                    dst[spot + r : spot + r + 16, :] = jnp.where(ahead == r, 1.0, 0.0).astype(BF16)
                spot += T

    def product(tile, src):
        cols = slice(tile * T, (tile + 1) * T)
        out = jnp.zeros((out_ref.shape[0], T), F32)
        spot = 0
        for ads, size in zip(ads_refs, sizes):
            out += jnp.dot(ads[...], src[spot : spot + size, :], preferred_element_type=F32)
            spot += size
        out_ref[:, cols] = out.astype(BF16)

    build(0, h0)
    for tile in range(tiles):
        now, then = (h1, h0) if tile % 2 else (h0, h1)
        product(tile, now)
        if tile + 1 < tiles:
            build(tile + 1, then)


def run_rows(ads_t, positives, start, total):
    width = ads_t[0].shape[0]
    sizes = [x.shape[1] for x in ads_t]
    return call(
        lambda *refs: rows_kernel(sizes, start, *refs),
        "positive_rows",
        [jax.ShapeDtypeStruct((width, total), BF16)],
        [pltpu.VMEM((sum(sizes), T), BF16)] * 2,
        (*ads_t, positives),
        cost(sum(sizes), total, width),
    )[0]


def users_kernel(inv, acc_ref, m_ref, rows_a, rows_b, hit_ref, weight_ref, *rest):
    stats_in, rest = rest[:NX], rest[NX:]
    du_ref, lse_ref, coef_ref, loss_ref, stats_ref, rows_ref = rest
    n = NX * NZ
    width = n * T // LANES
    for j in range(NX):
        stats_ref[pl.ds(lax.rem(lax.axis_index("aa") // NZ + NX - j, NX), 1)] = stats_in[j][...][None]
    rows_ref[:, : n * T // 2] = rows_a[...]
    rows_ref[:, n * T // 2 :] = rows_b[...]
    tops = stats_ref[:, :width, :]
    top = jnp.max(tops, axis=0)
    lse = top + jnp.log2(jnp.sum(jnp.exp2(tops - top[None]), axis=0))
    diff = (lse - jnp.sum(stats_ref[:, width:, :], axis=0)) * LN2
    loss = jnp.zeros((1, LANES), F32)
    for r in range(width):
        cols = slice(r * LANES, (r + 1) * LANES)
        lse_ref[:, cols] = lse[r : r + 1, :]
        loss += weight_ref[:, cols] * diff[r : r + 1, :]
    loss_ref[...] = loss_rows(jnp.sum(loss, axis=1, keepdims=True), loss_ref.shape[1])
    coef_ref[...] = weight_ref[...] * (jnp.exp2(hit_ref[...] - lse_ref[...]) - 1.0)

    for b in range(n):
        cols = slice(b * T, (b + 1) * T)
        weight = weight_ref[:, cols] * inv
        scale = weight * jnp.exp2(m_ref[:, cols] - lse_ref[:, cols])
        du = acc_ref[:, cols] * scale - rows_ref[:, cols].astype(F32) * weight
        du_ref[cols, :] = du.astype(BF16)


def run_users(acc, m, rows_a, rows_b, hits, weights, stats, inv):
    width, total = acc.shape
    row = jax.ShapeDtypeStruct((1, total), F32)
    out_shape = [jax.ShapeDtypeStruct((total // T * width, T), BF16)]
    out_shape += [row, row, jax.ShapeDtypeStruct((EXTRA, width), BF16)]
    return call(
        lambda *refs: users_kernel(inv, *refs),
        "grad_users",
        out_shape,
        [pltpu.VMEM((NX, *stats[0].shape), F32), pltpu.VMEM((width, total), BF16)],
        (acc, m, rows_a, rows_b, hits, weights, *stats),
    )


def grads_kernel(units, users_ref, lse_ref, coef_ref, weight_ref, pos_ref, loss_in, *refs):
    ps, tops, outs, qs = refs[: len(units)], refs[len(units) : 2 * len(units)], refs[2 * len(units) : -2], refs[-2:]
    deep = 2 * T
    total = users_ref.shape[0]

    def build(i, dst):
        group, at = units[i]
        for b in range(total // T):
            cols = slice(b * T, (b + 1) * T)
            scale = weight_ref[:, cols] * jnp.exp2(tops[i][:, cols] - lse_ref[:, cols])
            coef = coef_ref[:, cols]
            pos = pos_ref[:, cols] - lax.broadcasted_iota(jnp.int32, (16, T), 0)
            for half in range(2):
                ahead = pos - first_row(group, 2 * at + half)
                for r in range(0, T, 16):
                    row = half * T + r
                    scaled = ps[i][at * deep + row : at * deep + row + 16, cols].astype(F32) * scale
                    dst[row : row + 16, cols] = jnp.where(ahead == r, coef, scaled).astype(BF16)

    build(0, qs[0])
    for i in range(len(units)):
        da = jnp.dot(qs[i % 2][...], users_ref[...], preferred_element_type=F32)
        if i + 1 < len(units):
            build(i + 1, qs[(i + 1) % 2])
        da = da.astype(BF16)
        if len(outs) == 1:
            outs[0][i * deep : (i + 1) * deep, :] = da
        else:
            outs[i][:deep, :] = da
            outs[i][deep:, :] = loss_in[...]


def run_grads(name, units, users, lse, coefs, weights, positives, loss):
    total, width = users.shape
    deep = 2 * T
    places = [u[:2] for u in units]
    if name == "mid":
        shapes = [(deep + EXTRA, width)] * 2
    else:
        shapes = [(len(units) * deep, width)]
    return call(
        lambda *refs: grads_kernel(places, *refs),
        "grads_" + name,
        [jax.ShapeDtypeStruct(x, BF16) for x in shapes],
        [pltpu.VMEM((deep, total), BF16)] * 2,
        (users, lse, coefs, weights, positives, loss, *(u[2] for u in units), *(u[3] for u in units)),
        cost(len(units) * deep, total, width),
    )


def simple_call(kernel, name, out_shape, *args):
    return call(kernel, name, out_shape, [], args)


def add_mid(near, back):
    width = near.shape[1]

    def kernel(near_ref, back_ref, first, second, both):
        total = plus(near_ref[...], back_ref[...]).astype(BF16)
        first[:T, :] = total[:T, :]
        first[T:, :] = total[NZ * T :, :]
        second[...] = total[T : NZ * T, :]
        both[...] = total[NZ * T :, :]

    shapes = [(T + EXTRA, width), (T, width), (EXTRA, width)]
    return simple_call(kernel, "add_mid", [jax.ShapeDtypeStruct(x, BF16) for x in shapes], near, back)


def add_near(near, back, both, first, second):
    width = near.shape[1]
    rows = NZ * T

    def kernel(near_ref, back_ref, both_ref, first_ref, second_ref, keep, one, three):
        def term(i):
            return plus(near_ref[i * T : (i + 1) * T, :], back_ref[i * T : (i + 1) * T, :])

        keep[:T, :] = term(0)
        keep[T:rows, :] = term(1)
        keep[rows:, :] = both_ref[...].astype(F32)
        one[:T, :] = plus(term(2), first_ref[:T, :]).astype(BF16)
        one[T:rows, :] = term(3).astype(BF16)
        one[rows:, :] = plus(both_ref[...], first_ref[T:, :]).astype(BF16)
        three[:T, :] = term(4).astype(BF16)
        three[T:rows, :] = plus(term(5), second_ref[...]).astype(BF16)
        three[rows:, :] = both_ref[...]

    shapes = [jax.ShapeDtypeStruct((rows + EXTRA, width), t) for t in (F32, BF16, BF16)]
    return simple_call(kernel, "add_near", shapes, near, back, both, first, second)


def add_rows(*parts):
    width = parts[0].shape[1]

    def kernel(*refs):
        ins, (keep, send) = refs[:-2], refs[-2:]
        loss = plus(*(r[NZ * T :, :] for r in ins))
        keep[:T, :] = plus(*(r[:T, :] for r in ins))
        keep[T:, :] = loss
        send[:T, :] = plus(*(r[T : NZ * T, :] for r in ins)).astype(BF16)
        send[T:, :] = loss.astype(BF16)

    shapes = [jax.ShapeDtypeStruct((T + EXTRA, width), F32), jax.ShapeDtypeStruct((T + EXTRA, width), BF16)]
    return simple_call(kernel, "add_rows", shapes, *parts)


def finish(parts_u, keep, received):
    def kernel(parts_ref, keep_ref, received_ref, grad_u, grad, loss):
        width = parts_ref.shape[0] // (NX * NZ)
        grad_u[...] = plus(*(parts_ref[b * width : (b + 1) * width, :] for b in range(NX * NZ))).T
        grad[...] = plus(keep_ref[:T, :], received_ref[:T, :])
        loss[...] = jnp.sum(plus(keep_ref[T : T + 1, :], received_ref[T : T + 1, :]), axis=1, keepdims=True)

    shapes = [(T, parts_u.shape[0] // (NX * NZ)), (T, keep.shape[1]), (1, 1)]
    shapes = [jax.ShapeDtypeStruct(x, F32) for x in shapes]
    return simple_call(kernel, "finish", shapes, parts_u, keep, received)


def join_stats(own, other):
    half = own.shape[0] // 2

    def kernel(own_ref, other_ref, out_ref):
        a, b = own_ref[:half, :], other_ref[:half, :]
        top = jnp.maximum(a, b)
        out_ref[:half, :] = top + jnp.log2(jnp.exp2(a - top) + jnp.exp2(b - top))
        out_ref[half:, :] = own_ref[half:, :] + other_ref[half:, :]

    return simple_call(kernel, "join_stats", [jax.ShapeDtypeStruct(own.shape, F32)], own, other)[0]


def move(x, axis, target):
    return lax.ppermute(x, axis, [(i, target(i)) for i in range(lax.axis_size(axis))])


def shift_x(x, j):
    return move(x, "aa", lambda i: (i + j * NZ) % (NX * NZ))


def swap_z_hi(x):
    return move(x, "aa", lambda i: i ^ 1)


def shift_y(x, k):
    return move(x, "au", lambda i: i // 8 * 8 + (i % 8 + k * NC) % 8)


def swap_core(x):
    return move(x, "au", lambda i: i ^ 1)


def swap_z_lo(x):
    return move(x, "au", lambda i: i ^ 8)


def local(users, ads, counts, positives, weights):
    inv = users.shape[1] ** (-0.5)
    pos_row = (positives - lax.axis_index("aa") * counts.shape[0])[None, :]
    logc = (jnp.log(counts.astype(F32)) * LOG2E)[None, :]
    weight_row = weights[None, :]
    users_z, ads_z, pos_row, logc = lax.optimization_barrier((swap_z_hi(users), swap_z_lo(ads), pos_row, logc))
    user_pair = jnp.concatenate([users, users_z], axis=0)
    ads_pair = jnp.concatenate([ads, ads_z], axis=0)
    user_pair, ads_pair = lax.optimization_barrier((user_pair, ads_pair))
    user_2 = shift_x(user_pair, 2)
    user_1, user_3 = shift_x(user_pair, 1), shift_x(user_pair, -1)
    ads_1, ads_3 = shift_y(ads_pair, 1), shift_y(ads_pair, -1)
    ads_2 = shift_y(ads_pair, 2)
    parts = lax.optimization_barrier((user_pair, user_1, user_2, user_3))

    p_near, top_near, at_near, acc, m, total, hits, staged, users_t = run_logits(
        "near", parts, (ads_pair, ads_1, ads_3), logc, pos_row, inv
    )
    ads_2, ads_1, ads_3, hits = lax.optimization_barrier((ads_2, ads_1, ads_3, hits))
    far = swap_core(jnp.concatenate([ads_pair, ads_1, ads_3, ads_2], axis=0))
    p_two, top_two, at_two, acc, m, total, hits = run_logits(
        "two", (users_t,), (ads_2,), logc, pos_row, inv, (acc, m, total, hits)
    )
    p_far, top_far, at_far, acc, m, total, hits, stats = run_logits(
        "far", (users_t,), (far,), logc, pos_row, inv, (acc, m, total, hits)
    )
    half = stats.shape[0] * LANES // 4
    ads_t = (at_near, at_two, at_far)
    stats_z, rows_a = lax.optimization_barrier((swap_z_hi(stats), run_rows(ads_t, pos_row, 0, half)))
    stats = join_stats(stats, stats_z)
    moved = tuple(shift_x(stats, j) for j in range(1, NX))
    moved, rows_b = lax.optimization_barrier((moved, run_rows(ads_t, pos_row, half, half)))
    du, lse, coefs, loss = run_users(acc, m, rows_a, rows_b, hits, weight_row, (stats, *moved), inv)
    tail = (lse, coefs, weight_row, pos_row, loss)
    du = lax.all_to_all(du, "aa", split_axis=0, concat_axis=0, tiled=True)
    pay_2, da_2 = run_grads("mid", [("far", 3, p_far, top_far), ("two", 0, p_two, top_two)], staged, *tail)
    back_2 = swap_core(pay_2)
    da_2, staged = lax.optimization_barrier((da_2, staged))
    (da_far,) = run_grads("far", [("far", i, p_far, top_far) for i in range(3)], staged, *tail)
    da_far, back_2 = lax.optimization_barrier((da_far, back_2))
    back = swap_core(da_far)
    first, second, both = add_mid(da_2, back_2)
    first, second, staged = lax.optimization_barrier((first, second, staged))
    first, second = shift_y(first, -1), shift_y(second, 1)
    (da_near,) = run_grads("near", [("near", i, p_near, top_near) for i in range(3)], staged, *tail)
    da_near, first, second = lax.optimization_barrier((da_near, first, second))
    kept, one, three = add_near(da_near, back, both, first, second)
    one, three = shift_y(one, -1), shift_y(three, 1)
    one, three, du = lax.optimization_barrier((one, three, du))
    keep, send = add_rows(kept, one, three)
    grad_users, grad_ads, loss = finish(du, keep, swap_z_lo(send))
    return grad_users, grad_ads, loss.reshape(())


def solution(mesh):
    return jax.shard_map(
        local,
        mesh=mesh,
        in_specs=(P(("au", "aa"), None), P(("aa", "au"), None), P("aa"), P("au"), P("au")),
        out_specs=(P(("au", "aa"), None), P(("aa", "au"), None), P()),
        check_vma=False,
    )
```

```python
import jax
import jax.numpy as jnp
from jax import lax
from jax.experimental import pallas as pl
from jax.experimental.pallas import tpu as pltpu
from jax.sharding import PartitionSpec as P

F32 = jnp.float32
BF16 = jnp.bfloat16
T = 256
LANES = 128
EXTRA = 16
LOG2E = 1.4426950408889634
LN2 = 0.6931471805599453
NX, NZ, NY, NC = 4, 2, 4, 2
VMEM_LIMIT = 15 * 2**20


def params():
    return pltpu.CompilerParams(vmem_limit_bytes=VMEM_LIMIT)


def call(kernel, name, out_shape, scratch, args, estimate=None):
    vmem = pl.BlockSpec(memory_space=pltpu.VMEM)
    return pl.pallas_call(
        kernel,
        in_specs=[vmem] * len(args),
        out_specs=[vmem] * len(out_shape),
        out_shape=out_shape,
        scratch_shapes=scratch,
        compiler_params=params(),
        cost_estimate=estimate,
        name=name,
    )(*args)


def user_block(j, zr):
    me = lax.axis_index("aa")
    x, z = me // NZ, me % NZ
    return lax.rem(x + NX - j, NX) * NZ + (z + zr - 2 * z * zr)


def ads_block(group, chunk):
    pair, zr = chunk // NZ, chunk % NZ
    k, cr = {"near": (pair ^ (pair >> 1), 0), "far": (pair ^ (pair >> 1), 1), "two": (2, 0)}[group]
    me = lax.axis_index("au")
    z, y, c = me // (NY * NC), (me // NC) % NY, me % NC
    return (z + zr - 2 * z * zr) * (NY * NC) + lax.rem(y + NY - k, NY) * NC + (c + cr - 2 * c * cr)


def stage_users(user_refs, staged, inv):
    for j in range(NX):
        for zr in range(NZ):
            spot = pl.multiple_of(user_block(j, zr) * T, T)
            block = user_refs[j][zr * T : (zr + 1) * T, :].astype(F32) * inv
            staged[pl.ds(spot, T), :] = block.astype(BF16)


def first_row(group, chunk):
    return pl.multiple_of(ads_block(group, chunk) * T, T)


def split(value):
    high = value.astype(BF16).astype(F32)
    mid = (value - high).astype(BF16).astype(F32)
    return high, mid, value - high - mid


def loss_rows(loss, width):
    high, mid, low = split(loss)
    lane = lax.broadcasted_iota(jnp.int32, (EXTRA, width), 1) - 3 * lax.axis_index("au")
    return jnp.where(lane == 0, high, jnp.where(lane == 1, mid, jnp.where(lane == 2, low, 0.0))).astype(BF16)


def plus(*values):
    return sum(v.astype(F32) for v in values)


def logits_kernel(group, n_ads, rows, inv, *refs):
    n = NX * NZ
    chunks = rows // T
    first_call = group == "near"
    last_call = group == "far"
    if first_call:
        user_refs, refs = refs[:NX], refs[NX:]
    else:
        (users_t,), refs = refs[:1], refs[1:]
    ads_refs, refs = refs[:n_ads], refs[n_ads:]
    (logc_ref, pos_ref), refs = refs[:2], refs[2:]
    if not first_call:
        (acc_in, m_in, total_in, hit_in), refs = refs[:4], refs[4:]
    (p_ref, top_ref, ads_t, acc_ref, m_ref, total_ref, hit_ref), refs = refs[:7], refs[7:]
    if first_call:
        (staged, users_t), refs = refs[:2], refs[2:]
    if last_call:
        (stats_ref,), refs = refs[:1], refs[1:]
    ads_all, logc_all, s0, s1 = refs

    if first_call:
        stage_users(user_refs, staged, inv)
        for b in range(n):
            users_t[:, b * T : (b + 1) * T] = staged[b * T : (b + 1) * T, :].T
    spot = 0
    for r in ads_refs:
        ads_all[spot : spot + r.shape[0], :] = r[...]
        spot += r.shape[0]
    for c in range(chunks):
        part = slice(c * T, (c + 1) * T)
        ads_t[:, part] = ads_all[part, :].T
        logc = logc_ref[:, pl.ds(first_row(group, c), T)]
        logc_all[part, :] = jnp.broadcast_to(logc, (LANES, T)).T

    def columns(tile):
        return slice(tile * T, (tile + 1) * T)

    class Product:
        def __init__(self, tile, dst):
            self.cols, self.dst = columns(tile), dst
            self.side = users_t[:, self.cols]
            self.pos = pos_ref[:, self.cols] - lax.broadcasted_iota(jnp.int32, (8, T), 0)
            self.best = jnp.full((8, T), -jnp.inf, F32)
            self.found = jnp.zeros((8, T), F32)

        def chunk(self, c):
            ahead = self.pos - first_row(group, c)
            prod = jnp.dot(ads_all[c * T : (c + 1) * T, :], self.side, preferred_element_type=F32)
            for r in range(0, T, 8):
                row = c * T + r
                logc = logc_all[row : row + 8, :]
                x = prod[r : r + 8, :] * LOG2E - jnp.concatenate([logc] * (T // LANES), axis=1)
                self.dst[row : row + 8, :] = x
                self.best = jnp.maximum(self.best, x)
                self.found = jnp.where(ahead == r, x, self.found)

        def end(self):
            top_ref[:, self.cols] = jnp.max(self.best, axis=0, keepdims=True)
            hit = jnp.sum(self.found, axis=0, keepdims=True)
            hit_ref[:, self.cols] = hit if first_call else hit + hit_in[:, self.cols]

    class Exps:
        def __init__(self, tile, src):
            self.cols, self.src = columns(tile), src
            self.top = top_ref[:, self.cols]
            self.total = jnp.zeros((8, T), F32)

        def chunk(self, c):
            for r in range(c * T, (c + 1) * T, 16):
                e = jnp.exp2(self.src[r : r + 16, :] - self.top)
                self.total += e[:8] + e[8:]
                p_ref[r : r + 16, self.cols] = e.astype(BF16)

        def end(self):
            cols, top = self.cols, self.top
            total = jnp.sum(self.total, axis=0, keepdims=True)
            if first_call:
                m_ref[:, cols] = top
                total_ref[:, cols] = total
            else:
                m = jnp.maximum(m_in[:, cols], top)
                m_ref[:, cols] = m
                total_ref[:, cols] = total_in[:, cols] * jnp.exp2(m_in[:, cols] - m) + total * jnp.exp2(top - m)

    def gather(tile):
        cols = columns(tile)
        new = jnp.dot(ads_t[...], p_ref[:, cols], preferred_element_type=F32)
        if first_call:
            acc_ref[:, cols] = new
        else:
            m = m_ref[:, cols]
            acc_ref[:, cols] = acc_in[:, cols] * jnp.exp2(m_in[:, cols] - m) + new * jnp.exp2(top_ref[:, cols] - m)

    def turn(tile, src, dst):
        if tile:
            gather(tile - 1)
        product = Product(tile + 1, dst) if tile + 1 < n else None
        exps = Exps(tile, src)
        for c in range(chunks):
            if product:
                product.chunk(c)
            exps.chunk(c)
        if product:
            product.end()
        exps.end()

    opening = Product(0, s0)
    for c in range(chunks):
        opening.chunk(c)
    opening.end()
    for tile in range(n):
        if tile % 2:
            turn(tile, s1, s0)
        else:
            turn(tile, s0, s1)
    gather(n - 1)
    if last_call:
        lse = m_ref[...] + jnp.log2(total_ref[...])
        width = n * T // LANES
        for r in range(width):
            cols = slice(r * LANES, (r + 1) * LANES)
            stats_ref[r : r + 1, :] = lse[:, cols]
            stats_ref[width + r : width + r + 1, :] = hit_ref[:, cols]


def cost(rows, total, width):
    return pl.CostEstimate(flops=rows * total * width // 8, bytes_accessed=rows * total // 8, transcendentals=0)


def run_logits(group, users, ads, logc, positives, inv, before=()):
    width = ads[0].shape[1]
    count = sum(x.shape[0] for x in ads)
    total = NX * NZ * T
    stats_rows = 2 * total // LANES
    row = jax.ShapeDtypeStruct((1, total), F32)
    out_shape = [
        jax.ShapeDtypeStruct((count, total), BF16),
        row,
        jax.ShapeDtypeStruct((width, count), BF16),
        jax.ShapeDtypeStruct((width, total), F32),
        row,
        row,
        row,
    ]
    if group == "near":
        out_shape.append(jax.ShapeDtypeStruct((total, width), BF16))
        out_shape.append(jax.ShapeDtypeStruct((width, total), BF16))
    if group == "far":
        out_shape.append(jax.ShapeDtypeStruct((stats_rows, LANES), F32))
    scratch = [
        pltpu.VMEM((count, width), BF16),
        pltpu.VMEM((count, LANES), F32),
        pltpu.VMEM((count, T), F32),
        pltpu.VMEM((count, T), F32),
    ]
    return call(
        lambda *refs: logits_kernel(group, len(ads), count, inv, *refs),
        "logits_" + group,
        out_shape,
        scratch,
        (*users, *ads, logc, positives, *before),
        cost(count, total, width),
    )


GROUPS = ("near", "two", "far")


def rows_kernel(sizes, start, *refs):
    ads_refs, (pos_ref, out_ref, h0, h1) = refs[: len(sizes)], refs[len(sizes) :]
    tiles = out_ref.shape[1] // T

    def build(tile, dst):
        cols = slice(start + tile * T, start + (tile + 1) * T)
        pos = pos_ref[:, cols] - lax.broadcasted_iota(jnp.int32, (16, T), 0)
        spot = 0
        for group, size in zip(GROUPS, sizes):
            for c in range(size // T):
                ahead = pos - first_row(group, c)
                for r in range(0, T, 16):
                    dst[spot + r : spot + r + 16, :] = jnp.where(ahead == r, 1.0, 0.0).astype(BF16)
                spot += T

    def product(tile, src):
        cols = slice(tile * T, (tile + 1) * T)
        out = jnp.zeros((out_ref.shape[0], T), F32)
        spot = 0
        for ads, size in zip(ads_refs, sizes):
            out += jnp.dot(ads[...], src[spot : spot + size, :], preferred_element_type=F32)
            spot += size
        out_ref[:, cols] = out.astype(BF16)

    build(0, h0)
    for tile in range(tiles):
        now, then = (h1, h0) if tile % 2 else (h0, h1)
        product(tile, now)
        if tile + 1 < tiles:
            build(tile + 1, then)


def run_rows(ads_t, positives, start, total):
    width = ads_t[0].shape[0]
    sizes = [x.shape[1] for x in ads_t]
    return call(
        lambda *refs: rows_kernel(sizes, start, *refs),
        "positive_rows",
        [jax.ShapeDtypeStruct((width, total), BF16)],
        [pltpu.VMEM((sum(sizes), T), BF16)] * 2,
        (*ads_t, positives),
        cost(sum(sizes), total, width),
    )[0]


def users_kernel(inv, acc_ref, m_ref, rows_a, rows_b, hit_ref, weight_ref, *rest):
    stats_in, rest = rest[:NX], rest[NX:]
    du_ref, lse_ref, coef_ref, loss_ref, stats_ref, rows_ref = rest
    n = NX * NZ
    width = n * T // LANES
    for j in range(NX):
        stats_ref[pl.ds(lax.rem(lax.axis_index("aa") // NZ + NX - j, NX), 1)] = stats_in[j][...][None]
    rows_ref[:, : n * T // 2] = rows_a[...]
    rows_ref[:, n * T // 2 :] = rows_b[...]
    tops = stats_ref[:, :width, :]
    top = jnp.max(tops, axis=0)
    lse = top + jnp.log2(jnp.sum(jnp.exp2(tops - top[None]), axis=0))
    diff = (lse - jnp.sum(stats_ref[:, width:, :], axis=0)) * LN2
    loss = jnp.zeros((1, LANES), F32)
    for r in range(width):
        cols = slice(r * LANES, (r + 1) * LANES)
        lse_ref[:, cols] = lse[r : r + 1, :]
        loss += weight_ref[:, cols] * diff[r : r + 1, :]
    loss_ref[...] = loss_rows(jnp.sum(loss, axis=1, keepdims=True), loss_ref.shape[1])
    coef_ref[...] = weight_ref[...] * (jnp.exp2(hit_ref[...] - lse_ref[...]) - 1.0)

    for b in range(n):
        cols = slice(b * T, (b + 1) * T)
        weight = weight_ref[:, cols] * inv
        scale = weight * jnp.exp2(m_ref[:, cols] - lse_ref[:, cols])
        du = acc_ref[:, cols] * scale - rows_ref[:, cols].astype(F32) * weight
        du_ref[cols, :] = du.astype(BF16)


def run_users(acc, m, rows_a, rows_b, hits, weights, stats, inv):
    width, total = acc.shape
    row = jax.ShapeDtypeStruct((1, total), F32)
    out_shape = [jax.ShapeDtypeStruct((total // T * width, T), BF16)]
    out_shape += [row, row, jax.ShapeDtypeStruct((EXTRA, width), BF16)]
    return call(
        lambda *refs: users_kernel(inv, *refs),
        "grad_users",
        out_shape,
        [pltpu.VMEM((NX, *stats[0].shape), F32), pltpu.VMEM((width, total), BF16)],
        (acc, m, rows_a, rows_b, hits, weights, *stats),
    )


def grads_kernel(units, users_ref, lse_ref, coef_ref, weight_ref, pos_ref, loss_in, *refs):
    ps, tops, outs, qs = refs[: len(units)], refs[len(units) : 2 * len(units)], refs[2 * len(units) : -2], refs[-2:]
    deep = 2 * T
    total = users_ref.shape[0]

    def build(i, dst):
        group, at = units[i]
        for b in range(total // T):
            cols = slice(b * T, (b + 1) * T)
            scale = weight_ref[:, cols] * jnp.exp2(tops[i][:, cols] - lse_ref[:, cols])
            coef = coef_ref[:, cols]
            pos = pos_ref[:, cols] - lax.broadcasted_iota(jnp.int32, (16, T), 0)
            for half in range(2):
                ahead = pos - first_row(group, 2 * at + half)
                for r in range(0, T, 16):
                    row = half * T + r
                    scaled = ps[i][at * deep + row : at * deep + row + 16, cols].astype(F32) * scale
                    dst[row : row + 16, cols] = jnp.where(ahead == r, coef, scaled).astype(BF16)

    build(0, qs[0])
    for i in range(len(units)):
        da = jnp.dot(qs[i % 2][...], users_ref[...], preferred_element_type=F32)
        if i + 1 < len(units):
            build(i + 1, qs[(i + 1) % 2])
        da = da.astype(BF16)
        if len(outs) == 1:
            outs[0][i * deep : (i + 1) * deep, :] = da
        else:
            outs[i][:deep, :] = da
            outs[i][deep:, :] = loss_in[...]


def run_grads(name, units, users, lse, coefs, weights, positives, loss):
    total, width = users.shape
    deep = 2 * T
    places = [u[:2] for u in units]
    if name == "mid":
        shapes = [(deep + EXTRA, width)] * 2
    else:
        shapes = [(len(units) * deep, width)]
    return call(
        lambda *refs: grads_kernel(places, *refs),
        "grads_" + name,
        [jax.ShapeDtypeStruct(x, BF16) for x in shapes],
        [pltpu.VMEM((deep, total), BF16)] * 2,
        (users, lse, coefs, weights, positives, loss, *(u[2] for u in units), *(u[3] for u in units)),
        cost(len(units) * deep, total, width),
    )


def simple_call(kernel, name, out_shape, *args):
    return call(kernel, name, out_shape, [], args)


def add_mid(near, back):
    width = near.shape[1]

    def kernel(near_ref, back_ref, first, second, both):
        total = plus(near_ref[...], back_ref[...]).astype(BF16)
        first[:T, :] = total[:T, :]
        first[T:, :] = total[NZ * T :, :]
        second[...] = total[T : NZ * T, :]
        both[...] = total[NZ * T :, :]

    shapes = [(T + EXTRA, width), (T, width), (EXTRA, width)]
    return simple_call(kernel, "add_mid", [jax.ShapeDtypeStruct(x, BF16) for x in shapes], near, back)


def add_near(near, back, both, first, second):
    width = near.shape[1]
    rows = NZ * T

    def kernel(near_ref, back_ref, both_ref, first_ref, second_ref, keep, one, three):
        def term(i):
            return plus(near_ref[i * T : (i + 1) * T, :], back_ref[i * T : (i + 1) * T, :])

        keep[:T, :] = term(0)
        keep[T:rows, :] = term(1)
        keep[rows:, :] = both_ref[...].astype(F32)
        one[:T, :] = plus(term(2), first_ref[:T, :]).astype(BF16)
        one[T:rows, :] = term(3).astype(BF16)
        one[rows:, :] = plus(both_ref[...], first_ref[T:, :]).astype(BF16)
        three[:T, :] = term(4).astype(BF16)
        three[T:rows, :] = plus(term(5), second_ref[...]).astype(BF16)
        three[rows:, :] = both_ref[...]

    shapes = [jax.ShapeDtypeStruct((rows + EXTRA, width), t) for t in (F32, BF16, BF16)]
    return simple_call(kernel, "add_near", shapes, near, back, both, first, second)


def add_rows(*parts):
    width = parts[0].shape[1]

    def kernel(*refs):
        ins, (keep, send) = refs[:-2], refs[-2:]
        loss = plus(*(r[NZ * T :, :] for r in ins))
        keep[:T, :] = plus(*(r[:T, :] for r in ins))
        keep[T:, :] = loss
        send[:T, :] = plus(*(r[T : NZ * T, :] for r in ins)).astype(BF16)
        send[T:, :] = loss.astype(BF16)

    shapes = [jax.ShapeDtypeStruct((T + EXTRA, width), F32), jax.ShapeDtypeStruct((T + EXTRA, width), BF16)]
    return simple_call(kernel, "add_rows", shapes, *parts)


def finish(parts_u, keep, received):
    def kernel(parts_ref, keep_ref, received_ref, grad_u, grad, loss):
        width = parts_ref.shape[0] // (NX * NZ)
        grad_u[...] = plus(*(parts_ref[b * width : (b + 1) * width, :] for b in range(NX * NZ))).T
        grad[...] = plus(keep_ref[:T, :], received_ref[:T, :])
        loss[...] = jnp.sum(plus(keep_ref[T : T + 1, :], received_ref[T : T + 1, :]), axis=1, keepdims=True)

    shapes = [(T, parts_u.shape[0] // (NX * NZ)), (T, keep.shape[1]), (1, 1)]
    shapes = [jax.ShapeDtypeStruct(x, F32) for x in shapes]
    return simple_call(kernel, "finish", shapes, parts_u, keep, received)


def join_stats(own, other):
    half = own.shape[0] // 2

    def kernel(own_ref, other_ref, out_ref):
        a, b = own_ref[:half, :], other_ref[:half, :]
        top = jnp.maximum(a, b)
        out_ref[:half, :] = top + jnp.log2(jnp.exp2(a - top) + jnp.exp2(b - top))
        out_ref[half:, :] = own_ref[half:, :] + other_ref[half:, :]

    return simple_call(kernel, "join_stats", [jax.ShapeDtypeStruct(own.shape, F32)], own, other)[0]


def move(x, axis, target):
    return lax.ppermute(x, axis, [(i, target(i)) for i in range(lax.axis_size(axis))])


def shift_x(x, j):
    return move(x, "aa", lambda i: (i + j * NZ) % (NX * NZ))


def swap_z_hi(x):
    return move(x, "aa", lambda i: i ^ 1)


def shift_y(x, k):
    return move(x, "au", lambda i: i // 8 * 8 + (i % 8 + k * NC) % 8)


def swap_core(x):
    return move(x, "au", lambda i: i ^ 1)


def swap_z_lo(x):
    return move(x, "au", lambda i: i ^ 8)


def local(users, ads, counts, positives, weights):
    inv = users.shape[1] ** (-0.5)
    pos_row = (positives - lax.axis_index("aa") * counts.shape[0])[None, :]
    logc = (jnp.log(counts.astype(F32)) * LOG2E)[None, :]
    weight_row = weights[None, :]
    users_z, ads_z, pos_row, logc = lax.optimization_barrier((swap_z_hi(users), swap_z_lo(ads), pos_row, logc))
    user_pair = jnp.concatenate([users, users_z], axis=0)
    ads_pair = jnp.concatenate([ads, ads_z], axis=0)
    user_pair, ads_pair = lax.optimization_barrier((user_pair, ads_pair))
    user_2 = shift_x(user_pair, 2)
    user_1, user_3 = shift_x(user_pair, 1), shift_x(user_pair, -1)
    ads_1, ads_3 = shift_y(ads_pair, 1), shift_y(ads_pair, -1)
    ads_2 = shift_y(ads_pair, 2)
    parts = lax.optimization_barrier((user_pair, user_1, user_2, user_3))

    p_near, top_near, at_near, acc, m, total, hits, staged, users_t = run_logits(
        "near", parts, (ads_pair, ads_1, ads_3), logc, pos_row, inv
    )
    ads_2, ads_1, ads_3, hits = lax.optimization_barrier((ads_2, ads_1, ads_3, hits))
    far = swap_core(jnp.concatenate([ads_pair, ads_1, ads_3, ads_2], axis=0))
    p_two, top_two, at_two, acc, m, total, hits = run_logits(
        "two", (users_t,), (ads_2,), logc, pos_row, inv, (acc, m, total, hits)
    )
    p_far, top_far, at_far, acc, m, total, hits, stats = run_logits(
        "far", (users_t,), (far,), logc, pos_row, inv, (acc, m, total, hits)
    )
    half = stats.shape[0] * LANES // 4
    ads_t = (at_near, at_two, at_far)
    stats_z, rows_a = lax.optimization_barrier((swap_z_hi(stats), run_rows(ads_t, pos_row, 0, half)))
    stats = join_stats(stats, stats_z)
    moved = tuple(shift_x(stats, j) for j in range(1, NX))
    moved, rows_b = lax.optimization_barrier((moved, run_rows(ads_t, pos_row, half, half)))
    du, lse, coefs, loss = run_users(acc, m, rows_a, rows_b, hits, weight_row, (stats, *moved), inv)
    tail = (lse, coefs, weight_row, pos_row, loss)
    du = lax.all_to_all(du, "aa", split_axis=0, concat_axis=0, tiled=True)
    pay_2, da_2 = run_grads("mid", [("far", 3, p_far, top_far), ("two", 0, p_two, top_two)], staged, *tail)
    back_2 = swap_core(pay_2)
    da_2, staged = lax.optimization_barrier((da_2, staged))
    (da_far,) = run_grads("far", [("far", i, p_far, top_far) for i in range(3)], staged, *tail)
    da_far, back_2 = lax.optimization_barrier((da_far, back_2))
    back = swap_core(da_far)
    first, second, both = add_mid(da_2, back_2)
    first, second, staged = lax.optimization_barrier((first, second, staged))
    first, second = shift_y(first, -1), shift_y(second, 1)
    (da_near,) = run_grads("near", [("near", i, p_near, top_near) for i in range(3)], staged, *tail)
    da_near, first, second = lax.optimization_barrier((da_near, first, second))
    kept, one, three = add_near(da_near, back, both, first, second)
    one, three = shift_y(one, -1), shift_y(three, 1)
    one, three, du = lax.optimization_barrier((one, three, du))
    keep, send = add_rows(kept, one, three)
    grad_users, grad_ads, loss = finish(du, keep, swap_z_lo(send))
    return grad_users, grad_ads, loss.reshape(())


def solution(mesh):
    return jax.shard_map(
        local,
        mesh=mesh,
        in_specs=(P(("au", "aa"), None), P(("aa", "au"), None), P("aa"), P("au"), P("au")),
        out_specs=(P(("au", "aa"), None), P(("aa", "au"), None), P()),
        check_vma=False,
    )
```

```python
import jax
import jax.numpy as jnp
from jax import lax
from jax.experimental import pallas as pl
from jax.experimental.pallas import tpu as pltpu
from jax.sharding import PartitionSpec as P

F32 = jnp.float32
BF16 = jnp.bfloat16
T = 256
LANES = 128
EXTRA = 16
LOG2E = 1.4426950408889634
LN2 = 0.6931471805599453
NX, NZ, NY, NC = 4, 2, 4, 2
VMEM_LIMIT = 24 * 2**20


def params():
    return pltpu.CompilerParams(vmem_limit_bytes=VMEM_LIMIT)


def call(kernel, name, out_shape, scratch, args, estimate=None):
    vmem = pl.BlockSpec(memory_space=pltpu.VMEM)
    return pl.pallas_call(
        kernel,
        in_specs=[vmem] * len(args),
        out_specs=[vmem] * len(out_shape),
        out_shape=out_shape,
        scratch_shapes=scratch,
        compiler_params=params(),
        cost_estimate=estimate,
        name=name,
    )(*args)


def user_block(j, zr):
    me = lax.axis_index("aa")
    x, z = me // NZ, me % NZ
    return lax.rem(x + NX - j, NX) * NZ + (z + zr - 2 * z * zr)


def ads_block(group, chunk):
    pair, zr = chunk // NZ, chunk % NZ
    k, cr = {"near": (pair ^ (pair >> 1), 0), "far": (pair ^ (pair >> 1), 1), "two": (2, 0)}[group]
    me = lax.axis_index("au")
    z, y, c = me // (NY * NC), (me // NC) % NY, me % NC
    return (z + zr - 2 * z * zr) * (NY * NC) + lax.rem(y + NY - k, NY) * NC + (c + cr - 2 * c * cr)


def stage_users(user_refs, staged, inv):
    for j in range(NX):
        for zr in range(NZ):
            spot = pl.multiple_of(user_block(j, zr) * T, T)
            block = user_refs[j][zr * T : (zr + 1) * T, :].astype(F32) * inv
            staged[pl.ds(spot, T), :] = block.astype(BF16)


def first_row(group, chunk):
    return pl.multiple_of(ads_block(group, chunk) * T, T)


def split(value):
    high = value.astype(BF16).astype(F32)
    mid = (value - high).astype(BF16).astype(F32)
    return high, mid, value - high - mid


def loss_rows(loss, width):
    high, mid, low = split(loss)
    lane = lax.broadcasted_iota(jnp.int32, (EXTRA, width), 1) - 3 * lax.axis_index("au")
    return jnp.where(lane == 0, high, jnp.where(lane == 1, mid, jnp.where(lane == 2, low, 0.0))).astype(BF16)


def plus(*values):
    return sum(v.astype(F32) for v in values)


def logits_kernel(group, n_ads, rows, inv, *refs):
    n = NX * NZ
    chunks = rows // T
    first_call = group == "near"
    last_call = group == "far"
    if first_call:
        user_refs, refs = refs[:NX], refs[NX:]
    else:
        (users_t,), refs = refs[:1], refs[1:]
    ads_refs, refs = refs[:n_ads], refs[n_ads:]
    (logc_ref, pos_ref), refs = refs[:2], refs[2:]
    if not first_call:
        (acc_in, m_in, total_in, hit_in), refs = refs[:4], refs[4:]
    (p_ref, top_ref, ads_t, acc_ref, m_ref, total_ref, hit_ref), refs = refs[:7], refs[7:]
    if first_call:
        (staged, users_t), refs = refs[:2], refs[2:]
    if last_call:
        (stats_ref,), refs = refs[:1], refs[1:]
    ads_all, logc_all, s0, s1 = refs

    if first_call:
        stage_users(user_refs, staged, inv)
        for b in range(n):
            users_t[:, b * T : (b + 1) * T] = staged[b * T : (b + 1) * T, :].T
    spot = 0
    for r in ads_refs:
        ads_all[spot : spot + r.shape[0], :] = r[...]
        spot += r.shape[0]
    for c in range(chunks):
        part = slice(c * T, (c + 1) * T)
        ads_t[:, part] = ads_all[part, :].T
        logc = logc_ref[:, pl.ds(first_row(group, c), T)]
        logc_all[part, :] = jnp.broadcast_to(logc, (LANES, T)).T

    def columns(tile):
        return slice(tile * T, (tile + 1) * T)

    class Product:
        def __init__(self, tile, dst):
            self.cols, self.dst = columns(tile), dst
            self.side = users_t[:, self.cols]
            self.pos = pos_ref[:, self.cols] - lax.broadcasted_iota(jnp.int32, (8, T), 0)
            self.best = jnp.full((8, T), -jnp.inf, F32)
            self.found = jnp.zeros((8, T), F32)

        def chunk(self, c):
            ahead = self.pos - first_row(group, c)
            prod = jnp.dot(ads_all[c * T : (c + 1) * T, :], self.side, preferred_element_type=F32)
            for r in range(0, T, 8):
                row = c * T + r
                logc = logc_all[row : row + 8, :]
                x = prod[r : r + 8, :] * LOG2E - jnp.concatenate([logc] * (T // LANES), axis=1)
                self.dst[row : row + 8, :] = x
                self.best = jnp.maximum(self.best, x)
                self.found = jnp.where(ahead == r, x, self.found)

        def end(self):
            top_ref[:, self.cols] = jnp.max(self.best, axis=0, keepdims=True)
            hit = jnp.sum(self.found, axis=0, keepdims=True)
            hit_ref[:, self.cols] = hit if first_call else hit + hit_in[:, self.cols]

    class Exps:
        def __init__(self, tile, src):
            self.cols, self.src = columns(tile), src
            self.top = top_ref[:, self.cols]
            self.total = jnp.zeros((8, T), F32)

        def chunk(self, c):
            for r in range(c * T, (c + 1) * T, 16):
                e = jnp.exp2(self.src[r : r + 16, :] - self.top)
                self.total += e[:8] + e[8:]
                p_ref[r : r + 16, self.cols] = e.astype(BF16)

        def end(self):
            cols, top = self.cols, self.top
            total = jnp.sum(self.total, axis=0, keepdims=True)
            if first_call:
                m_ref[:, cols] = top
                total_ref[:, cols] = total
            else:
                m = jnp.maximum(m_in[:, cols], top)
                m_ref[:, cols] = m
                total_ref[:, cols] = total_in[:, cols] * jnp.exp2(m_in[:, cols] - m) + total * jnp.exp2(top - m)

    def gather(tile):
        cols = columns(tile)
        new = jnp.dot(ads_t[...], p_ref[:, cols], preferred_element_type=F32)
        if first_call:
            acc_ref[:, cols] = new
        else:
            m = m_ref[:, cols]
            acc_ref[:, cols] = acc_in[:, cols] * jnp.exp2(m_in[:, cols] - m) + new * jnp.exp2(top_ref[:, cols] - m)

    def turn(tile, src, dst):
        if tile:
            gather(tile - 1)
        product = Product(tile + 1, dst) if tile + 1 < n else None
        exps = Exps(tile, src)
        for c in range(chunks):
            if product:
                product.chunk(c)
            exps.chunk(c)
        if product:
            product.end()
        exps.end()

    opening = Product(0, s0)
    for c in range(chunks):
        opening.chunk(c)
    opening.end()
    for tile in range(n):
        if tile % 2:
            turn(tile, s1, s0)
        else:
            turn(tile, s0, s1)
    gather(n - 1)
    if last_call:
        lse = m_ref[...] + jnp.log2(total_ref[...])
        width = n * T // LANES
        for r in range(width):
            cols = slice(r * LANES, (r + 1) * LANES)
            stats_ref[r : r + 1, :] = lse[:, cols]
            stats_ref[width + r : width + r + 1, :] = hit_ref[:, cols]


def cost(rows, total, width):
    return pl.CostEstimate(flops=rows * total * width // 8, bytes_accessed=rows * total // 8, transcendentals=0)


def run_logits(group, users, ads, logc, positives, inv, before=()):
    width = ads[0].shape[1]
    count = sum(x.shape[0] for x in ads)
    total = NX * NZ * T
    stats_rows = 2 * total // LANES
    row = jax.ShapeDtypeStruct((1, total), F32)
    out_shape = [
        jax.ShapeDtypeStruct((count, total), BF16),
        row,
        jax.ShapeDtypeStruct((width, count), BF16),
        jax.ShapeDtypeStruct((width, total), F32),
        row,
        row,
        row,
    ]
    if group == "near":
        out_shape.append(jax.ShapeDtypeStruct((total, width), BF16))
        out_shape.append(jax.ShapeDtypeStruct((width, total), BF16))
    if group == "far":
        out_shape.append(jax.ShapeDtypeStruct((stats_rows, LANES), F32))
    scratch = [
        pltpu.VMEM((count, width), BF16),
        pltpu.VMEM((count, LANES), F32),
        pltpu.VMEM((count, T), F32),
        pltpu.VMEM((count, T), F32),
    ]
    return call(
        lambda *refs: logits_kernel(group, len(ads), count, inv, *refs),
        "logits_" + group,
        out_shape,
        scratch,
        (*users, *ads, logc, positives, *before),
        cost(count, total, width),
    )


GROUPS = ("near", "two", "far")


def rows_kernel(sizes, start, *refs):
    ads_refs, (pos_ref, out_ref, h0, h1) = refs[: len(sizes)], refs[len(sizes) :]
    tiles = out_ref.shape[1] // T

    def build(tile, dst):
        cols = slice(start + tile * T, start + (tile + 1) * T)
        pos = pos_ref[:, cols] - lax.broadcasted_iota(jnp.int32, (16, T), 0)
        spot = 0
        for group, size in zip(GROUPS, sizes):
            for c in range(size // T):
                ahead = pos - first_row(group, c)
                for r in range(0, T, 16):
                    dst[spot + r : spot + r + 16, :] = jnp.where(ahead == r, 1.0, 0.0).astype(BF16)
                spot += T

    def product(tile, src):
        cols = slice(tile * T, (tile + 1) * T)
        out = jnp.zeros((out_ref.shape[0], T), F32)
        spot = 0
        for ads, size in zip(ads_refs, sizes):
            out += jnp.dot(ads[...], src[spot : spot + size, :], preferred_element_type=F32)
            spot += size
        out_ref[:, cols] = out.astype(BF16)

    build(0, h0)
    for tile in range(tiles):
        now, then = (h1, h0) if tile % 2 else (h0, h1)
        product(tile, now)
        if tile + 1 < tiles:
            build(tile + 1, then)


def run_rows(ads_t, positives, start, total):
    width = ads_t[0].shape[0]
    sizes = [x.shape[1] for x in ads_t]
    return call(
        lambda *refs: rows_kernel(sizes, start, *refs),
        "positive_rows",
        [jax.ShapeDtypeStruct((width, total), BF16)],
        [pltpu.VMEM((sum(sizes), T), BF16)] * 2,
        (*ads_t, positives),
        cost(sum(sizes), total, width),
    )[0]


def users_kernel(inv, acc_ref, m_ref, rows_a, rows_b, hit_ref, weight_ref, *rest):
    stats_in, rest = rest[:NX], rest[NX:]
    du_refs, (lse_ref, coef_ref, loss_ref, stats_ref, rows_ref) = rest[:-5], rest[-5:]
    n = NX * NZ
    width = n * T // LANES
    for j in range(NX):
        stats_ref[pl.ds(lax.rem(lax.axis_index("aa") // NZ + NX - j, NX), 1)] = stats_in[j][...][None]
    rows_ref[:, : n * T // 2] = rows_a[...]
    rows_ref[:, n * T // 2 :] = rows_b[...]
    tops = stats_ref[:, :width, :]
    top = jnp.max(tops, axis=0)
    lse = top + jnp.log2(jnp.sum(jnp.exp2(tops - top[None]), axis=0))
    diff = (lse - jnp.sum(stats_ref[:, width:, :], axis=0)) * LN2
    loss = jnp.zeros((1, LANES), F32)
    for r in range(width):
        cols = slice(r * LANES, (r + 1) * LANES)
        lse_ref[:, cols] = lse[r : r + 1, :]
        loss += weight_ref[:, cols] * diff[r : r + 1, :]
    loss_ref[...] = loss_rows(jnp.sum(loss, axis=1, keepdims=True), loss_ref.shape[1])
    coef_ref[...] = weight_ref[...] * (jnp.exp2(hit_ref[...] - lse_ref[...]) - 1.0)

    def users_at(j, zr):
        cols = pl.ds(pl.multiple_of(user_block((NX - j) % NX, zr) * T, T), T)
        weight = weight_ref[:, cols] * inv
        scale = weight * jnp.exp2(m_ref[:, cols] - lse_ref[:, cols])
        return (acc_ref[:, cols] * scale - rows_ref[:, cols].astype(F32) * weight).astype(BF16)

    for part, j in enumerate((0, 1, 3)):
        for zr in range(NZ):
            du_refs[part][zr * T : (zr + 1) * T, :] = users_at(j, zr)
    du_refs[3][...] = users_at(2, 0)
    du_refs[4][...] = users_at(2, 1)


def run_users(acc, m, rows_a, rows_b, hits, weights, stats, inv):
    width, total = acc.shape
    row = jax.ShapeDtypeStruct((1, total), F32)
    shapes = [(NZ * width, T)] * 3 + [(width, T)] * 2
    out_shape = [jax.ShapeDtypeStruct(x, BF16) for x in shapes]
    out_shape += [row, row, jax.ShapeDtypeStruct((EXTRA, width), BF16)]
    return call(
        lambda *refs: users_kernel(inv, *refs),
        "grad_users",
        out_shape,
        [pltpu.VMEM((NX, *stats[0].shape), F32), pltpu.VMEM((width, total), BF16)],
        (acc, m, rows_a, rows_b, hits, weights, *stats),
    )


def grads_kernel(units, users_ref, lse_ref, coef_ref, weight_ref, pos_ref, loss_in, *refs):
    ps, tops, outs, qs = refs[: len(units)], refs[len(units) : 2 * len(units)], refs[2 * len(units) : -2], refs[-2:]
    deep = 2 * T
    total = users_ref.shape[0]

    def build(i, dst):
        group, at = units[i]
        for b in range(total // T):
            cols = slice(b * T, (b + 1) * T)
            scale = weight_ref[:, cols] * jnp.exp2(tops[i][:, cols] - lse_ref[:, cols])
            coef = coef_ref[:, cols]
            pos = pos_ref[:, cols] - lax.broadcasted_iota(jnp.int32, (16, T), 0)
            for half in range(2):
                ahead = pos - first_row(group, 2 * at + half)
                for r in range(0, T, 16):
                    row = half * T + r
                    scaled = ps[i][at * deep + row : at * deep + row + 16, cols].astype(F32) * scale
                    dst[row : row + 16, cols] = jnp.where(ahead == r, coef, scaled).astype(BF16)

    build(0, qs[0])
    for i in range(len(units)):
        da = jnp.dot(qs[i % 2][...], users_ref[...], preferred_element_type=F32)
        if i + 1 < len(units):
            build(i + 1, qs[(i + 1) % 2])
        da = da.astype(BF16)
        if len(outs) == 1:
            outs[0][i * deep : (i + 1) * deep, :] = da
        else:
            outs[i][:deep, :] = da
            outs[i][deep:, :] = loss_in[...]


def run_grads(name, units, users, lse, coefs, weights, positives, loss):
    total, width = users.shape
    deep = 2 * T
    places = [u[:2] for u in units]
    if name == "mid":
        shapes = [(deep + EXTRA, width)] * 2
    else:
        shapes = [(len(units) * deep, width)]
    return call(
        lambda *refs: grads_kernel(places, *refs),
        "grads_" + name,
        [jax.ShapeDtypeStruct(x, BF16) for x in shapes],
        [pltpu.VMEM((deep, total), BF16)] * 2,
        (users, lse, coefs, weights, positives, loss, *(u[2] for u in units), *(u[3] for u in units)),
        cost(len(units) * deep, total, width),
    )


def simple_call(kernel, name, out_shape, *args):
    return call(kernel, name, out_shape, [], args)


def add_mid(near, back):
    width = near.shape[1]

    def kernel(near_ref, back_ref, first, second, both):
        total = plus(near_ref[...], back_ref[...]).astype(BF16)
        first[:T, :] = total[:T, :]
        first[T:, :] = total[NZ * T :, :]
        second[...] = total[T : NZ * T, :]
        both[...] = total[NZ * T :, :]

    shapes = [(T + EXTRA, width), (T, width), (EXTRA, width)]
    return simple_call(kernel, "add_mid", [jax.ShapeDtypeStruct(x, BF16) for x in shapes], near, back)


def add_near(near, back, both, first, second):
    width = near.shape[1]
    rows = NZ * T

    def kernel(near_ref, back_ref, both_ref, first_ref, second_ref, keep, one, three):
        def term(i):
            return plus(near_ref[i * T : (i + 1) * T, :], back_ref[i * T : (i + 1) * T, :])

        keep[:T, :] = term(0)
        keep[T:rows, :] = term(1)
        keep[rows:, :] = both_ref[...].astype(F32)
        one[:T, :] = plus(term(2), first_ref[:T, :]).astype(BF16)
        one[T:rows, :] = term(3).astype(BF16)
        one[rows:, :] = plus(both_ref[...], first_ref[T:, :]).astype(BF16)
        three[:T, :] = term(4).astype(BF16)
        three[T:rows, :] = plus(term(5), second_ref[...]).astype(BF16)
        three[rows:, :] = both_ref[...]

    shapes = [jax.ShapeDtypeStruct((rows + EXTRA, width), t) for t in (F32, BF16, BF16)]
    return simple_call(kernel, "add_near", shapes, near, back, both, first, second)


def add_rows(*parts):
    width = parts[0].shape[1]

    def kernel(*refs):
        ins, (keep, send) = refs[:-2], refs[-2:]
        loss = plus(*(r[NZ * T :, :] for r in ins))
        keep[:T, :] = plus(*(r[:T, :] for r in ins))
        keep[T:, :] = loss
        send[:T, :] = plus(*(r[T : NZ * T, :] for r in ins)).astype(BF16)
        send[T:, :] = loss.astype(BF16)

    shapes = [jax.ShapeDtypeStruct((T + EXTRA, width), F32), jax.ShapeDtypeStruct((T + EXTRA, width), BF16)]
    return simple_call(kernel, "add_rows", shapes, *parts)


def add_halves(one, three, first, second):
    half = one.shape[0] // NZ

    def kernel(one_ref, three_ref, first_ref, second_ref, out1, out3):
        out1[:half, :] = (one_ref[:half, :].astype(F32) + first_ref[...].astype(F32)).astype(BF16)
        out1[half:, :] = one_ref[half:, :]
        out3[:half, :] = three_ref[:half, :]
        out3[half:, :] = (three_ref[half:, :].astype(F32) + second_ref[...].astype(F32)).astype(BF16)

    shapes = [jax.ShapeDtypeStruct(one.shape, BF16)] * 2
    return simple_call(kernel, "add_halves", shapes, one, three, first, second)


def add_users(parts):
    width = parts[0].shape[0] // NZ

    def kernel(*refs):
        ins, (keep, send) = refs[:-2], refs[-2:]
        keep[...] = sum(r[:width, :].astype(F32) for r in ins)
        send[...] = sum(r[width:, :].astype(F32) for r in ins).astype(BF16)

    shapes = [jax.ShapeDtypeStruct((width, T), F32), jax.ShapeDtypeStruct((width, T), BF16)]
    return simple_call(kernel, "add_users", shapes, *parts)


def finish(keep_u, received_u, keep, received):
    def kernel(keep_u_ref, received_u_ref, keep_ref, received_ref, grad_u, grad, loss):
        grad_u[...] = plus(keep_u_ref[...], received_u_ref[...]).T
        grad[...] = plus(keep_ref[:T, :], received_ref[:T, :])
        loss[...] = jnp.sum(plus(keep_ref[T : T + 1, :], received_ref[T : T + 1, :]), axis=1, keepdims=True)

    shapes = [(T, keep_u.shape[0]), (T, keep.shape[1]), (1, 1)]
    shapes = [jax.ShapeDtypeStruct(x, F32) for x in shapes]
    return simple_call(kernel, "finish", shapes, keep_u, received_u, keep, received)


def join_stats(own, other):
    half = own.shape[0] // 2

    def kernel(own_ref, other_ref, out_ref):
        a, b = own_ref[:half, :], other_ref[:half, :]
        top = jnp.maximum(a, b)
        out_ref[:half, :] = top + jnp.log2(jnp.exp2(a - top) + jnp.exp2(b - top))
        out_ref[half:, :] = own_ref[half:, :] + other_ref[half:, :]

    return simple_call(kernel, "join_stats", [jax.ShapeDtypeStruct(own.shape, F32)], own, other)[0]


def move(x, axis, target):
    return lax.ppermute(x, axis, [(i, target(i)) for i in range(lax.axis_size(axis))])


def shift_x(x, j):
    return move(x, "aa", lambda i: (i + j * NZ) % (NX * NZ))


def swap_z_hi(x):
    return move(x, "aa", lambda i: i ^ 1)


def shift_y(x, k):
    return move(x, "au", lambda i: i // 8 * 8 + (i % 8 + k * NC) % 8)


def swap_core(x):
    return move(x, "au", lambda i: i ^ 1)


def swap_z_lo(x):
    return move(x, "au", lambda i: i ^ 8)


def local(users, ads, counts, positives, weights):
    inv = users.shape[1] ** (-0.5)
    pos_row = (positives - lax.axis_index("aa") * counts.shape[0])[None, :]
    logc = (jnp.log(counts.astype(F32)) * LOG2E)[None, :]
    weight_row = weights[None, :]
    users_z, ads_z, pos_row, logc = lax.optimization_barrier((swap_z_hi(users), swap_z_lo(ads), pos_row, logc))
    user_pair = jnp.concatenate([users, users_z], axis=0)
    ads_pair = jnp.concatenate([ads, ads_z], axis=0)
    user_pair, ads_pair = lax.optimization_barrier((user_pair, ads_pair))
    user_2 = shift_x(user_pair, 2)
    user_1, user_3 = shift_x(user_pair, 1), shift_x(user_pair, -1)
    ads_1, ads_3 = shift_y(ads_pair, 1), shift_y(ads_pair, -1)
    ads_2 = shift_y(ads_pair, 2)
    parts = lax.optimization_barrier((user_pair, user_1, user_2, user_3))

    p_near, top_near, at_near, acc, m, total, hits, staged, users_t = run_logits(
        "near", parts, (ads_pair, ads_1, ads_3), logc, pos_row, inv
    )
    ads_2, ads_1, ads_3, hits = lax.optimization_barrier((ads_2, ads_1, ads_3, hits))
    far = swap_core(jnp.concatenate([ads_pair, ads_1, ads_3, ads_2], axis=0))
    p_two, top_two, at_two, acc, m, total, hits = run_logits(
        "two", (users_t,), (ads_2,), logc, pos_row, inv, (acc, m, total, hits)
    )
    p_far, top_far, at_far, acc, m, total, hits, stats = run_logits(
        "far", (users_t,), (far,), logc, pos_row, inv, (acc, m, total, hits)
    )
    half = stats.shape[0] * LANES // 4
    ads_t = (at_near, at_two, at_far)
    stats_z, rows_a = lax.optimization_barrier((swap_z_hi(stats), run_rows(ads_t, pos_row, 0, half)))
    stats = join_stats(stats, stats_z)
    moved = tuple(shift_x(stats, j) for j in range(1, NX))
    moved, rows_b = lax.optimization_barrier((moved, run_rows(ads_t, pos_row, half, half)))
    du_0, du_1, du_3, du_2a, du_2b, lse, coefs, loss = run_users(
        acc, m, rows_a, rows_b, hits, weight_row, (stats, *moved), inv
    )
    tail = (lse, coefs, weight_row, pos_row, loss)
    du_2a, du_2b = shift_x(du_2a, 1), shift_x(du_2b, -1)
    pay_2, da_2 = run_grads("mid", [("far", 3, p_far, top_far), ("two", 0, p_two, top_two)], staged, *tail)
    back_2 = swap_core(pay_2)
    da_2, staged = lax.optimization_barrier((da_2, staged))
    (da_far,) = run_grads("far", [("far", i, p_far, top_far) for i in range(3)], staged, *tail)
    da_far, back_2 = lax.optimization_barrier((da_far, back_2))
    back = swap_core(da_far)
    first, second, both = add_mid(da_2, back_2)
    first, second, staged = lax.optimization_barrier((first, second, staged))
    first, second = shift_y(first, -1), shift_y(second, 1)
    (da_near,) = run_grads("near", [("near", i, p_near, top_near) for i in range(3)], staged, *tail)
    da_near, du_2a, du_2b = lax.optimization_barrier((da_near, du_2a, du_2b))
    du_1, du_3 = add_halves(du_1, du_3, du_2a, du_2b)
    da_near, du_1, du_3 = lax.optimization_barrier((da_near, du_1, du_3))
    du_1, du_3 = shift_x(du_1, 1), shift_x(du_3, -1)
    kept, one, three = add_near(da_near, back, both, first, second)
    one, three = shift_y(one, -1), shift_y(three, 1)
    keep_u, send_u = add_users((du_0, du_1, du_3))
    one, three, received_u = lax.optimization_barrier((one, three, swap_z_hi(send_u)))
    keep, send = add_rows(kept, one, three)
    grad_users, grad_ads, loss = finish(keep_u, received_u, keep, swap_z_lo(send))
    return grad_users, grad_ads, loss.reshape(())


def solution(mesh):
    return jax.shard_map(
        local,
        mesh=mesh,
        in_specs=(P(("au", "aa"), None), P(("aa", "au"), None), P("aa"), P("au"), P("au")),
        out_specs=(P(("au", "aa"), None), P(("aa", "au"), None), P()),
        check_vma=False,
    )
```
